32 devices in a mesh: dp: 8 (over y, x, core), tensor: 4 (over z).
Axes of the slice: x: 2, y: 2, z: 4, core: 2. Of those that a mesh axis runs over, the one named last changes fastest.
Arguments:
- tokens: bfloat16 [16384, 1536], P(('dp', 'tensor')), may hold values from -6 to 6
- positions: int32 [16384], P('dp'), may hold values from 0 to 2047, as said below
- norm1_gain: bfloat16 [1536], P('dp'), may hold values from 0.5 to 1.5
- w_query: bfloat16 [1536, 1536], P('dp', 'tensor'), may hold values from -0.3125 to 0.3125
- key_weight: bfloat16 [1536, 768], P('dp', 'tensor'), may hold values from -0.3125 to 0.3125
- value_weight: bfloat16 [1536, 768], P('dp', 'tensor'), may hold values from -0.15625 to 0.15625
- w_out: bfloat16 [1536, 1536], P('dp', 'tensor'), may hold values from -0.625 to 0.625
- norm2_gain: bfloat16 [1536], P('dp'), may hold values from 0.5 to 1.5
- w_gate: bfloat16 [1536, 4096], P('dp', 'tensor'), may hold values from -0.15625 to 0.15625
- w_up: bfloat16 [1536, 4096], P('dp', 'tensor'), may hold values from -0.15625 to 0.15625
- w_down: bfloat16 [1536, 4096], P('dp', 'tensor'), may hold values from -0.09375 to 0.09375
- cotangent: bfloat16 [16384, 1536], P(('dp', 'tensor')), may hold values from -6 to 6
Outputs:
- mixed: bfloat16 [16384, 1536], P(('dp', 'tensor'))
- grad_tokens: float32 [16384, 1536], P(('dp', 'tensor'))
- grad_norm1: float32 [1536], P('dp')
- grad_query: float32 [1536, 1536], P('dp', 'tensor')
- grad_key: float32 [1536, 768], P('dp', 'tensor')
- grad_value: float32 [1536, 768], P('dp', 'tensor')
- grad_output: float32 [1536, 1536], P('dp', 'tensor')
- grad_norm2: float32 [1536], P('dp')
- grad_gate: float32 [1536, 4096], P('dp', 'tensor')
- grad_up: float32 [1536, 4096], P('dp', 'tensor')
- grad_down: float32 [1536, 4096], P('dp', 'tensor')
The draws below stay inside these ranges and needn't reach their ends.
Inputs may be any that keep to these rules, and one draw needn't show every extreme that they name: Each aligned block of 2048 tokens is one sequence holding one or three packed documents; positions count 0, 1, 2, ... from each document's first token, and every sequence starts a document at its first token.
All inputs are finite; a program needn't handle non-finite values.
Results may differ from the reference program's by a relative error of at most 0.02.
Values may be sent and summed in bfloat16 or wider, within the bound.
No kernel may reach another device: no remote copies, remote signals or barrier semaphores. Data moves between devices by JAX's collectives and lax.ppermute only.
A program may use at most 192 MiB of HBM per device.

```python
import jax
import jax.numpy as jnp
from jax import lax

MODEL_WIDTH = 1536
QUERY_HEADS = 16
KEY_VALUE_HEADS = 8
HEAD_SIZE = 96
FF = 4096
SEQUENCE_LENGTH = 2048
TOKENS = 16384


def draw_positions(key, part):
    key = jax.random.fold_in(key, 11)
    first_key, last_key, pick_key = jax.random.split(key, 3)
    seq_count = TOKENS // SEQUENCE_LENGTH
    eighth = SEQUENCE_LENGTH // 8
    first_cut = jax.random.randint(first_key, (seq_count, 1), 1, eighth)
    last_cut = jax.random.randint(last_key, (seq_count, 1), SEQUENCE_LENGTH - eighth + 1, SEQUENCE_LENGTH)
    single = jax.random.randint(pick_key, (1, 1), 0, seq_count)
    seq_index = jnp.arange(seq_count, dtype=jnp.int32)[:, None]
    first_cut = jnp.where(seq_index == single, 0, first_cut)
    last_cut = jnp.where(seq_index == single, SEQUENCE_LENGTH, last_cut)
    token_index = jnp.arange(SEQUENCE_LENGTH, dtype=jnp.int32)[None, :]
    doc_start = jnp.where(token_index >= last_cut, last_cut, jnp.where(token_index >= first_cut, first_cut, 0))
    return (token_index - doc_start).reshape(TOKENS).astype(jnp.int32)


def block_levels(own_key, extent, pieces, smallest, high):
    def one(position, shards_of):
        draws = jax.random.uniform(jax.random.fold_in(jax.random.fold_in(own_key, 6), position), (shards_of,), jnp.float32, smallest / len(pieces), high / len(pieces))
        return jnp.repeat(jnp.exp(draws), extent[position] // shards_of).reshape((-1,) + (1,) * (len(extent) - position - 1))

    level = one(*pieces[0])
    for cut in pieces[1:]:
        level = level * one(*cut)
    return level


def centred(rng, shape, spread, limit, pieces=(), held_as=jnp.bfloat16):
    drawn = spread * jax.random.normal(rng, shape, jnp.float32)
    if pieces:
        drawn = drawn * block_levels(rng, shape, pieces, -0.22, 0.18)
    return jnp.clip(drawn, -limit, limit).astype(held_as)


def setup_inputs(seed: int = 0) -> dict:
    keys = jax.random.split(jax.random.key(seed), 13)
    return {
        "tokens": centred(keys[0], (TOKENS, MODEL_WIDTH), 1.0, 6.0, ((0, 32),)),
        "positions": draw_positions(jax.random.fold_in(keys[12], 71), 0),
        "norm1_gain": jnp.clip(1.0 + 0.1 * jax.random.normal(keys[2], (MODEL_WIDTH,), jnp.float32), 0.5, 1.5).astype(jnp.bfloat16),
        "w_query": centred(keys[3], (MODEL_WIDTH, QUERY_HEADS * HEAD_SIZE), (MODEL_WIDTH // 4) ** -0.5, 0.3125, ((0, 8), (1, 4))),
        "key_weight": centred(keys[4], (MODEL_WIDTH, KEY_VALUE_HEADS * HEAD_SIZE), (MODEL_WIDTH // 4) ** -0.5, 0.3125, ((0, 8), (1, 4))),
        "value_weight": centred(keys[5], (MODEL_WIDTH, KEY_VALUE_HEADS * HEAD_SIZE), MODEL_WIDTH ** -0.5, 0.15625, ((0, 8), (1, 4))),
        "w_out": centred(keys[6], (MODEL_WIDTH, QUERY_HEADS * HEAD_SIZE), (QUERY_HEADS * HEAD_SIZE // 16) ** -0.5, 0.625, ((0, 8), (1, 4))),
        "norm2_gain": jnp.clip(1.0 + 0.1 * jax.random.normal(keys[7], (MODEL_WIDTH,), jnp.float32), 0.5, 1.5).astype(jnp.bfloat16),
        "w_gate": centred(keys[8], (MODEL_WIDTH, FF), MODEL_WIDTH ** -0.5, 0.15625, ((0, 8), (1, 4))),
        "w_up": centred(keys[9], (MODEL_WIDTH, FF), MODEL_WIDTH ** -0.5, 0.15625, ((0, 8), (1, 4))),
        "w_down": centred(keys[10], (MODEL_WIDTH, FF), FF ** -0.5, 0.09375, ((0, 8), (1, 4))),
        "cotangent": centred(keys[11], (TOKENS, MODEL_WIDTH), 1.0, 6.0, ((0, 32),)),
    }


epsilon = 1e-05
rope_base = 100000.0
masked_score = -1e+30
highest = lax.Precision.HIGHEST

@jax.custom_vjp
def reduced_output(v):
    return lax.optimization_barrier(v.astype(jnp.bfloat16)).astype(jnp.float32)

@jax.custom_vjp
def reduced_backward(v):
    return v

def low_keep(v):
    return (reduced_output(v), None)

def low_pass(kept, grad):
    return (grad,)

def back_keep(v):
    return (v, None)

def back_low(kept, grad):
    return (reduced_output(grad),)
reduced_output.defvjp(low_keep, low_pass)
reduced_backward.defvjp(back_keep, back_low)

def matrix_product(left, right):
    return jnp.dot(left, right, precision=highest)

def normalize(values, gain):
    return values * lax.rsqrt(lax.optimization_barrier(jnp.mean(values * values, -1, keepdims=True)) + epsilon) * gain

def spin_tables(places):
    inverse = rope_base ** (-(2.0 / HEAD_SIZE) * jnp.arange(HEAD_SIZE // 2, dtype=jnp.float32))
    angles = places.astype(jnp.float32)[:, None] * inverse[None, :]
    return (jnp.cos(angles), jnp.sin(angles))

def apply_rotation(values, cosine_table, sine_table):
    middle = values.shape[-1] // 2
    leading = values[..., :middle]
    trailing = values[..., middle:]
    cos_part = cosine_table[:, None, :]
    sin_part = sine_table[:, None, :]
    return jnp.concatenate([leading * cos_part - trailing * sin_part, trailing * cos_part + leading * sin_part], -1)

def visible(query_index, places, length):
    key_index = jnp.arange(length, dtype=jnp.int32)[None, :]
    return (key_index <= query_index[:, None]) & (key_index >= (query_index - places)[:, None])

def attend(query_rows, every_key, every_value, places):
    block_rows = min(512, SEQUENCE_LENGTH)
    starts = jnp.arange(SEQUENCE_LENGTH // block_rows, dtype=jnp.int32) * block_rows

    def one_block(row_start):
        query_block = lax.dynamic_slice_in_dim(query_rows, row_start, block_rows, 0)
        place_block = lax.dynamic_slice_in_dim(places, row_start, block_rows, 0)
        query_index = row_start + jnp.arange(block_rows, dtype=jnp.int32)
        scores = reduced_backward(jnp.einsum('bkgd,tkd->kgbt', query_block, every_key, precision=highest) * HEAD_SIZE ** (-0.5))
        scores = jnp.where(visible(query_index, place_block, SEQUENCE_LENGTH), scores, masked_score)
        weights = jnp.exp(scores - lax.optimization_barrier(jnp.max(scores, -1, keepdims=True)))
        shares = weights / lax.optimization_barrier(jnp.sum(weights, -1, keepdims=True))
        return jnp.einsum('kgbt,tkd->bkgd', reduced_output(shares), every_value, precision=highest)
    blocks = lax.map(jax.checkpoint(one_block), starts)
    return blocks.reshape(query_rows.shape)

def layer(stream, norm1_gain, w_query, key_weight, value_weight, w_out, norm2_gain, w_gate, w_up, w_down, places):
    cosine_table, sine_table = spin_tables(places)
    attention_input = reduced_output(normalize(stream, norm1_gain))
    query_rows = reduced_output(apply_rotation(reduced_backward(matrix_product(attention_input, w_query)).reshape(SEQUENCE_LENGTH, QUERY_HEADS, HEAD_SIZE), cosine_table, sine_table))
    query_rows = query_rows.reshape(SEQUENCE_LENGTH, KEY_VALUE_HEADS, QUERY_HEADS // KEY_VALUE_HEADS, HEAD_SIZE)
    every_key = reduced_output(apply_rotation(reduced_backward(matrix_product(attention_input, key_weight)).reshape(SEQUENCE_LENGTH, KEY_VALUE_HEADS, HEAD_SIZE), cosine_table, sine_table))
    every_value = reduced_output(reduced_backward(matrix_product(attention_input, value_weight))).reshape(SEQUENCE_LENGTH, KEY_VALUE_HEADS, HEAD_SIZE)
    heads_out = reduced_output(reduced_backward(attend(query_rows, every_key, every_value, places).reshape(SEQUENCE_LENGTH, QUERY_HEADS * HEAD_SIZE)))
    middle_stream = stream + reduced_backward(matrix_product(heads_out, w_out.T))
    ff_in = reduced_output(normalize(middle_stream, norm2_gain))
    gate_value = reduced_backward(matrix_product(ff_in, w_gate))
    up_value = reduced_backward(matrix_product(ff_in, w_up))
    hidden = reduced_output(gate_value * jax.nn.sigmoid(gate_value) * up_value)
    return middle_stream + matrix_product(hidden, w_down.T)

def reference(tokens, positions, norm1_gain, w_query, key_weight, value_weight, w_out, norm2_gain, w_gate, w_up, w_down, cotangent):
    seq_count = TOKENS // SEQUENCE_LENGTH
    params = tuple((weight.astype(jnp.float32) for weight in (norm1_gain, w_query, key_weight, value_weight, w_out, norm2_gain, w_gate, w_up, w_down)))
    streams = tokens.astype(jnp.float32).reshape(seq_count, SEQUENCE_LENGTH, MODEL_WIDTH)
    place_rows = positions.reshape(seq_count, SEQUENCE_LENGTH)
    cot_rows = cotangent.astype(jnp.float32).reshape(seq_count, SEQUENCE_LENGTH, MODEL_WIDTH)

    def one_sequence(running, sequence_item):
        stream, places, incoming = sequence_item

        def forward(values, *weights):
            return layer(values, *weights, places)
        result, pullback = jax.vjp(forward, stream, *params)
        gradients = pullback(incoming)
        updated = tuple((old_sum + fresh for old_sum, fresh in zip(running, gradients[1:])))
        return (updated, (result.astype(jnp.bfloat16), gradients[0]))
    start_sums = tuple((jnp.zeros(weight.shape, jnp.float32) for weight in params))
    totals, (outputs, input_grads) = lax.scan(one_sequence, start_sums, (streams, place_rows, cot_rows))
    return (outputs.reshape(TOKENS, MODEL_WIDTH), input_grads.reshape(TOKENS, MODEL_WIDTH), totals[0], totals[1], totals[2], totals[3], totals[4], totals[5], totals[6], totals[7], totals[8])
```

```python
import functools
import math

import jax
import jax.numpy as jnp
from jax import lax
from jax.experimental import pallas as pl
from jax.experimental.pallas import tpu as pltpu
from jax.sharding import Mesh
from jax.sharding import PartitionSpec as P

HEAD_SIZE = 96
SEQUENCE_LENGTH = 2048
LANES = 128

epsilon = 1e-05
rope_base = 100000.0
masked_score = -1e30
query_scale = math.log2(math.e) * HEAD_SIZE ** (-0.5)
rows_both = (((0,), (0,)), ((), ()))
cols_both = (((1,), (1,)), ((), ()))
f32 = jnp.float32
bf16 = jnp.bfloat16


def local_block(g, place_ref, ring):
    other = lax.rem(g // ring + place_ref[0], 2)
    step = lax.rem(lax.rem(g, ring) - place_ref[1] + ring, ring)
    return 2 * step + other


def attend_kernel(ring, block, place_ref, q_ref, k_ref, v_ref, start_ref, o_ref, lse_ref):
    g = pl.program_id(1)
    share = q_ref.shape[1] // LANES
    start = start_ref[...]
    row = lax.broadcasted_iota(jnp.int32, (block, block), 0)
    col = lax.broadcasted_iota(jnp.int32, (block, block), 1)
    queries = [q_ref[:, h * LANES : (h + 1) * LANES] for h in range(share)]

    def step(kb, carry, diagonal):
        offset = pl.multiple_of(local_block(kb, place_ref, ring) * block, block)
        keys = k_ref[pl.ds(offset, block), :]
        values = v_ref[pl.ds(offset, block), :]
        shown = row >= start - kb * block
        if diagonal:
            shown = shown & (row <= col)
        out = []
        for h in range(share):
            largest, total, acc = carry[h]
            s = lax.dot_general(keys, queries[h], cols_both, preferred_element_type=f32)
            s = jnp.where(shown, s, masked_score)
            newest = jnp.maximum(largest, jnp.max(s, 0, keepdims=True))
            fade = jnp.exp2(largest - newest)
            p = jnp.exp2(s - newest)
            total = total * fade + jnp.sum(p, 0, keepdims=True)
            acc = acc * fade + lax.dot_general(
                values, p.astype(bf16), rows_both, preferred_element_type=f32
            )
            out.append((newest, total, acc))
        return tuple(out)

    carry = tuple(
        (
            jnp.full((1, block), masked_score, f32),
            jnp.zeros((1, block), f32),
            jnp.zeros((LANES, block), f32),
        )
        for _ in range(share)
    )
    carry = step(g, carry, True)
    carry = lax.fori_loop(0, g, lambda kb, c: step(kb, c, False), carry)
    for h in range(share):
        largest, total, acc = carry[h]
        o_ref[:, h * LANES : (h + 1) * LANES] = jnp.transpose(acc / total).astype(bf16)
        lse_ref[0, h : h + 1, :] = largest + jnp.log2(total)


def attend(place, q, k, v, start, ring):
    length = q.shape[0]
    block = length // (2 * ring)
    kv = k.shape[1] // LANES
    share = q.shape[1] // k.shape[1]

    def at(g, place_ref):
        return local_block(g, place_ref, ring)

    return pl.pallas_call(
        functools.partial(attend_kernel, ring, block),
        grid_spec=pltpu.PrefetchScalarGridSpec(
            num_scalar_prefetch=1,
            grid=(kv, 2 * ring),
            in_specs=[
                pl.BlockSpec((block, share * LANES), lambda h, g, z: (at(g, z), h)),
                pl.BlockSpec((length, LANES), lambda h, g, z: (0, h)),
                pl.BlockSpec((length, LANES), lambda h, g, z: (0, h)),
                pl.BlockSpec((1, block), lambda h, g, z: (0, at(g, z))),
            ],
            out_specs=[
                pl.BlockSpec((block, share * LANES), lambda h, g, z: (at(g, z), h)),
                pl.BlockSpec((1, share, block), lambda h, g, z: (h, 0, at(g, z))),
            ],
        ),
        out_shape=[
            jax.ShapeDtypeStruct(q.shape, bf16),
            jax.ShapeDtypeStruct((kv, share, length), f32),
        ],
        compiler_params=pltpu.CompilerParams(
            vmem_limit_bytes=40 * 2**20, dimension_semantics=("arbitrary", "arbitrary")
        ),
        cost_estimate=pl.CostEstimate(
            flops=10 * length * length * q.shape[1], bytes_accessed=8 * length * q.shape[1], transcendentals=0
        ),
        name="attend",
    )(place, q, k, v, start)


def attend_back_kernel(
    ring,
    block,
    place_ref,
    q_ref,
    k_ref,
    v_ref,
    o_ref,
    do_ref,
    lse_ref,
    start_ref,
    cosq_ref,
    sinq_ref,
    cosk_ref,
    sink_ref,
    dq_ref,
    dk_ref,
    dv_ref,
    dk_acc,
    dv_acc,
):
    g = pl.program_id(1)
    share = q_ref.shape[1] // LANES

    @pl.when(g == 0)
    def _():
        dk_acc[...] = jnp.zeros_like(dk_acc)
        dv_acc[...] = jnp.zeros_like(dv_acc)

    start = start_ref[...]
    row = lax.broadcasted_iota(jnp.int32, (block, block), 0)
    col = lax.broadcasted_iota(jnp.int32, (block, block), 1)
    heads = [slice(h * LANES, (h + 1) * LANES) for h in range(share)]
    queries = [q_ref[:, h] for h in heads]
    grads = [do_ref[:, h] for h in heads]
    lses = [lse_ref[0, h : h + 1, :] for h in range(share)]
    inner = [
        jnp.sum(
            jnp.transpose(do_ref[:, h].astype(f32) * o_ref[:, h].astype(f32)), 0, keepdims=True
        )
        for h in heads
    ]

    def step(kb, carry, diagonal):
        offset = pl.multiple_of(local_block(kb, place_ref, ring) * block, block)
        keys = k_ref[pl.ds(offset, block), :]
        values = v_ref[pl.ds(offset, block), :]
        shown = row >= start - kb * block
        if diagonal:
            shown = shown & (row <= col)
        out = []
        dk = jnp.zeros((block, LANES), f32)
        dv = jnp.zeros((block, LANES), f32)
        for h in range(share):
            s = lax.dot_general(keys, queries[h], cols_both, preferred_element_type=f32)
            p = jnp.where(shown, jnp.exp2(s - lses[h]), 0.0)
            dp = lax.dot_general(values, grads[h], cols_both, preferred_element_type=f32)
            ds = (p * (dp - inner[h])).astype(bf16)
            dv += jnp.dot(p.astype(bf16), grads[h], preferred_element_type=f32)
            dk += jnp.dot(ds, queries[h], preferred_element_type=f32)
            out.append(carry[h] + lax.dot_general(keys, ds, rows_both, preferred_element_type=f32))
        dk_acc[pl.ds(offset, block), :] += dk
        dv_acc[pl.ds(offset, block), :] += dv
        return tuple(out)

    carry = step(g, tuple(jnp.zeros((LANES, block), f32) for _ in range(share)), True)
    carry = lax.fori_loop(0, g, lambda kb, c: step(kb, c, False), carry)
    for h in range(share):
        u = jnp.transpose(carry[h]) * HEAD_SIZE ** (-0.5)
        turned = u * cosq_ref[...] - pltpu.roll(u, LANES // 2, 1) * sinq_ref[...]
        dq_ref[:, heads[h]] = turned.astype(bf16)

    @pl.when(g == pl.num_programs(1) - 1)
    def _():
        def finish(i, _):
            r = pl.ds(pl.multiple_of(i * block, block), block)
            u = dk_acc[r, :] * math.log(2.0)
            turned = u * cosk_ref[r, :] - pltpu.roll(u, LANES // 2, 1) * sink_ref[r, :]
            dk_ref[r, :] = turned.astype(bf16)
            dv_ref[r, :] = dv_acc[r, :].astype(bf16)
            return 0

        lax.fori_loop(0, 2 * ring, finish, 0)


def attend_back(place, q, k, v, o, do, lse, start, cos, sin, ring):
    length = q.shape[0]
    block = length // (2 * ring)
    kv = k.shape[1] // LANES
    share = q.shape[1] // k.shape[1]

    def at(g, place_ref):
        return local_block(g, place_ref, ring)

    qspec = pl.BlockSpec((block, share * LANES), lambda h, g, z: (at(g, z), h))
    kspec = pl.BlockSpec((length, LANES), lambda h, g, z: (0, h))
    tableq = pl.BlockSpec((block, LANES), lambda h, g, z: (at(g, z), 0))
    tablek = pl.BlockSpec((length, LANES), lambda h, g, z: (0, 0))
    return pl.pallas_call(
        functools.partial(attend_back_kernel, ring, block),
        grid_spec=pltpu.PrefetchScalarGridSpec(
            num_scalar_prefetch=1,
            grid=(kv, 2 * ring),
            in_specs=[
                qspec,
                kspec,
                kspec,
                qspec,
                qspec,
                pl.BlockSpec((1, share, block), lambda h, g, z: (h, 0, at(g, z))),
                pl.BlockSpec((1, block), lambda h, g, z: (0, at(g, z))),
                tableq,
                tableq,
                tablek,
                tablek,
            ],
            out_specs=[qspec, kspec, kspec],
            scratch_shapes=[pltpu.VMEM((length, LANES), f32), pltpu.VMEM((length, LANES), f32)],
        ),
        out_shape=[
            jax.ShapeDtypeStruct(q.shape, bf16),
            jax.ShapeDtypeStruct(k.shape, bf16),
            jax.ShapeDtypeStruct(k.shape, bf16),
        ],
        compiler_params=pltpu.CompilerParams(
            vmem_limit_bytes=40 * 2**20, dimension_semantics=("arbitrary", "arbitrary")
        ),
        cost_estimate=pl.CostEstimate(
            flops=20 * length * length * q.shape[1], bytes_accessed=16 * length * q.shape[1], transcendentals=0
        ),
        name="attend_back",
    )(place, q, k, v, o, do, lse, start, cos, sin, cos, sin)


def project_kernel(
    widths, x_ref, gain_ref, w_ref, cos_ref, sin_ref, a_ref, q_ref, k_ref, v_ref
):
    x = x_ref[...].astype(f32)
    root = lax.rsqrt(jnp.mean(x * x, -1, keepdims=True) + epsilon)
    a = (x * root * gain_ref[...]).astype(bf16)
    a_ref[...] = a
    cos = cos_ref[...]
    sin = sin_ref[...]
    whole = jnp.dot(a, w_ref[...], preferred_element_type=f32)
    qw, kw = widths
    for h in range((qw + kw) // LANES):
        u = whole[:, h * LANES : (h + 1) * LANES]
        turned = u * cos + pltpu.roll(u, LANES // 2, 1) * sin
        if h < qw // LANES:
            q_ref[:, h * LANES : (h + 1) * LANES] = (turned * query_scale).astype(bf16)
        else:
            j = h - qw // LANES
            k_ref[:, j * LANES : (j + 1) * LANES] = turned.astype(bf16)
    v_ref[...] = whole[:, qw + kw :].astype(bf16)


def project(x, gain, w, cos, sin, qw, kw):
    rows, width = x.shape
    block = min(256, rows)

    def row(n):
        return pl.BlockSpec((block, n), lambda i: (i, 0))

    def whole(a):
        return pl.BlockSpec(a.shape, lambda i: (0, 0))

    return pl.pallas_call(
        functools.partial(project_kernel, (qw, kw)),
        grid=(rows // block,),
        in_specs=[row(width), whole(gain), whole(w), row(LANES), row(LANES)],
        out_specs=[row(width), row(qw), row(kw), row(kw)],
        out_shape=[jax.ShapeDtypeStruct((rows, n), bf16) for n in (width, qw, kw, kw)],
        compiler_params=pltpu.CompilerParams(
            vmem_limit_bytes=40 * 2**20, dimension_semantics=("arbitrary",)
        ),
        cost_estimate=pl.CostEstimate(
            flops=2 * rows * width * w.shape[1], bytes_accessed=8 * rows * width, transcendentals=0
        ),
        name="project",
    )(x, gain, w, cos, sin)


def hidden_kernel(chunk, a_ref, dy_ref, wg_ref, wu_ref, wd_ref, hid_ref, dg_ref, du_ref):
    a = a_ref[...]
    dy = dy_ref[...]
    for j in range(wg_ref.shape[1] // chunk):
        at = slice(j * chunk, (j + 1) * chunk)
        g = jnp.dot(a, wg_ref[:, at], preferred_element_type=f32)
        u = jnp.dot(a, wu_ref[:, at], preferred_element_type=f32)
        dh = jnp.dot(dy, wd_ref[:, at], preferred_element_type=f32)
        sig = jax.nn.sigmoid(g)
        silu = g * sig
        hid_ref[:, at] = (silu * u).astype(bf16)
        dg_ref[:, at] = (dh * u * (sig + silu * (1.0 - sig))).astype(bf16)
        du_ref[:, at] = (dh * silu).astype(bf16)


def hidden_pass(a, dy, wg, wu, wd):
    rows, width = a.shape
    units = wg.shape[1]
    block = min(256, rows)
    row = pl.BlockSpec((block, width), lambda i: (i, 0))
    out = pl.BlockSpec((block, units), lambda i: (i, 0))
    whole = pl.BlockSpec((width, units), lambda i: (0, 0))
    return pl.pallas_call(
        functools.partial(hidden_kernel, min(256, units)),
        grid=(rows // block,),
        in_specs=[row, row, whole, whole, whole],
        out_specs=[out, out, out],
        out_shape=[jax.ShapeDtypeStruct((rows, units), bf16)] * 3,
        compiler_params=pltpu.CompilerParams(
            vmem_limit_bytes=48 * 2**20, dimension_semantics=("arbitrary",)
        ),
        cost_estimate=pl.CostEstimate(
            flops=6 * rows * width * units, bytes_accessed=4 * rows * width, transcendentals=0
        ),
        name="hidden",
    )(a, dy, wg, wu, wd)


def pad_heads(w):
    half = HEAD_SIZE // 2
    parts = w.reshape(w.shape[0], -1, half)
    return jnp.pad(parts, ((0, 0), (0, 0), (0, LANES // 2 - half))).reshape(w.shape[0], -1)


def cut_heads(w):
    half = HEAD_SIZE // 2
    parts = w.reshape(w.shape[0], -1, LANES // 2)
    return parts[:, :, :half].reshape(w.shape[0], -1)


swap_two = [(0, 1), (1, 0)]
cross_pairs = [(0, 0), (1, 2), (2, 1), (3, 3)]
slant_pairs = [(2 * c + zh, 2 * zh + (1 - c)) for c in range(2) for zh in range(2)]
slant_back = [(b, a) for a, b in slant_pairs]


def relay(a):
    return lax.ppermute(a, ("c", "zh"), cross_pairs)


def other_core(a):
    return lax.ppermute(a, "c", swap_two)


def from_neighbour(a, k, ring):
    return lax.ppermute(a, "zl", [(i, (i - k) % ring) for i in range(ring)])


def both_cores(a):
    return jnp.concatenate([a, other_core(a)], 0)


def gather_weight(w):
    straight = lax.ppermute(w, ("c", "zh"), cross_pairs)
    slanted = lax.ppermute(w, ("c", "zh"), slant_pairs)
    first = lax.axis_index("zh") == 0
    both = jnp.concatenate(
        [jnp.where(first, straight, slanted), jnp.where(first, slanted, straight)], 0
    )
    return lax.all_gather(both, "d", axis=0, tiled=True)


def settle_weight(grad):
    part = lax.psum_scatter(grad.astype(bf16), "d", scatter_dimension=0, tiled=True)
    rows = part.shape[0] // 2
    first = lax.axis_index("zh") == 0
    upper, lower = part[:rows], part[rows:]
    straight = lax.ppermute(jnp.where(first, upper, lower), ("c", "zh"), cross_pairs)
    slanted = lax.ppermute(jnp.where(first, lower, upper), ("c", "zh"), slant_back)
    return straight.astype(f32) + slanted.astype(f32)


def dot(a, b):
    return jnp.dot(a, b, preferred_element_type=f32)


def dot_cols(a, b):
    return lax.dot_general(a, b, cols_both, preferred_element_type=f32)


def dot_rows(a, b):
    return lax.dot_general(a, b, rows_both, preferred_element_type=f32)


def sum_steps(first, second):
    out = first
    for item in second:
        out = out + item
    return out


def per_device(
    ring,
    tokens,
    positions,
    norm1_gain,
    w_query,
    key_weight,
    value_weight,
    w_out,
    norm2_gain,
    w_gate,
    w_up,
    w_down,
    cotangent,
):
    steps = range(ring)
    core = lax.axis_index("c")
    column = lax.axis_index("zl")
    place = jnp.stack([core, column]).astype(jnp.int32)
    rows = tokens.shape[0]
    length = 2 * ring * rows

    def gather_chip(own):
        return [both_cores(own if k == 0 else from_neighbour(own, k, ring)) for k in steps]

    def scatter_sum(partials, kind):
        kept = []
        for k in reversed(steps):
            p = partials[k]
            joined = p[:rows].astype(f32) + other_core(p[rows:].astype(kind)).astype(f32)
            if k:
                moved = lax.ppermute(
                    joined.astype(kind), "zl", [(i, (i + k) % ring) for i in steps]
                )
                joined = moved.astype(f32)
            kept.append(joined)
        return sum_steps(kept[-1], kept[:-1])

    stream_own = relay(tokens)
    attn_shard = jnp.concatenate([w_query, key_weight, value_weight, w_out], 1)
    gains = lax.all_gather(
        jnp.stack([norm1_gain, norm2_gain]), ("d", "c"), axis=1, tiled=True
    ).astype(f32)
    attn_full = gather_weight(attn_shard)
    places = relay(positions).reshape(2, ring, rows)
    chips = gather_chip(stream_own)

    ordered = [
        lax.dynamic_index_in_dim(
            lax.dynamic_index_in_dim(places, (core + j) % 2, 0, keepdims=False),
            (column + k) % ring,
            0,
            keepdims=False,
        )
        for k in steps
        for j in range(2)
    ]
    firsts = [
        ((core + j) % 2 * ring + (column + k) % ring) * rows for k in steps for j in range(2)
    ]
    start = jnp.concatenate(
        [f + jnp.arange(rows, dtype=jnp.int32) - o for f, o in zip(firsts, ordered)]
    )[None, :]
    spots = jnp.concatenate(ordered).astype(f32)
    inverse = rope_base ** (-(2.0 / HEAD_SIZE) * jnp.arange(HEAD_SIZE // 2, dtype=f32))
    angles = spots[:, None] * inverse[None, :]
    gap = jnp.zeros((length, LANES // 2 - HEAD_SIZE // 2), f32)
    cos_half, sin_half = jnp.cos(angles), jnp.sin(angles)
    cos = jnp.concatenate([cos_half, gap, cos_half, gap], 1)
    sin = jnp.concatenate([-sin_half, gap, sin_half, gap], 1)

    qcols, kcols = w_query.shape[1], key_weight.shape[1]
    padded = pad_heads(attn_full)
    qw = qcols // HEAD_SIZE * LANES
    kw = kcols // HEAD_SIZE * LANES
    w_qkv = padded[:, : qw + 2 * kw]
    w_o = padded[:, qw + 2 * kw :]
    gain_first, gain_second = gains[0:1], gains[1:2]

    pieces = [
        project(
            x,
            gain_first,
            w_qkv,
            cos[2 * rows * k : 2 * rows * (k + 1)],
            sin[2 * rows * k : 2 * rows * (k + 1)],
            qw,
            kw,
        )
        for k, x in enumerate(chips)
    ]
    normed_first = [p[0] for p in pieces]
    q, k, v = (jnp.concatenate([p[i] for p in pieces], 0) for i in (1, 2, 3))
    o, lse = attend(place, q, k, v, start, ring)

    stream = stream_own.astype(f32)
    chip_rows = [slice(2 * rows * i, 2 * rows * (i + 1)) for i in steps]
    middle = stream + scatter_sum([dot_cols(o[r], w_o) for r in chip_rows], bf16)
    root_second = lax.rsqrt(jnp.mean(middle * middle, -1, keepdims=True) + epsilon)
    normed_second = (middle * root_second * gain_second).astype(bf16)

    wg_full = gather_weight(w_gate)
    wu_full = gather_weight(w_up)
    wd_full = gather_weight(w_down)
    cot_own = relay(cotangent)
    out_grads = gather_chip(cot_own)
    ff_in = gather_chip(normed_second)

    hidden = [
        hidden_pass(a, dy, wg_full, wu_full, wd_full) for a, dy in zip(ff_in, out_grads)
    ]
    second_grad = scatter_sum(
        [dot_cols(h[1], wg_full) + dot_cols(h[2], wu_full) for h in hidden], bf16
    )
    mixed = middle + scatter_sum([dot_cols(h[0], wd_full) for h in hidden], bf16)
    mixed = relay(mixed.astype(bf16))

    down_wgrad = sum_steps(0.0, [dot_rows(dy, h[0]) for dy, h in zip(out_grads, hidden)])
    gate_wgrad = sum_steps(0.0, [dot_rows(a, h[1]) for a, h in zip(ff_in, hidden)])
    up_wgrad = sum_steps(0.0, [dot_rows(a, h[2]) for a, h in zip(ff_in, hidden)])

    scaled = second_grad * gain_second
    middle_grad = (
        cot_own.astype(f32)
        + root_second * scaled
        - middle * root_second**3 * jnp.mean(scaled * middle, -1, keepdims=True)
    )
    branch = gather_chip(middle_grad.astype(bf16))
    do = jnp.concatenate([dot(b, w_o).astype(bf16) for b in branch], 0)
    out_wgrad = sum_steps(0.0, [dot_rows(b, o[r]) for b, r in zip(branch, chip_rows)])
    dq, dk, dv = attend_back(place, q, k, v, o, do, lse, start, cos, sin, ring)
    dqkv = jnp.concatenate([dq, dk, dv], 1)
    first_grad = scatter_sum([dot_cols(dqkv[r], w_qkv) for r in chip_rows], bf16)
    qkv_wgrad = sum_steps(0.0, [dot_rows(a, dqkv[r]) for a, r in zip(normed_first, chip_rows)])

    root_first = lax.rsqrt(jnp.mean(stream * stream, -1, keepdims=True) + epsilon)
    scaled = first_grad * gain_first
    input_grad = (
        middle_grad
        + root_first * scaled
        - stream * root_first**3 * jnp.mean(scaled * stream, -1, keepdims=True)
    )
    input_grad = relay(input_grad.astype(bf16)).astype(f32)

    grad_down = settle_weight(down_wgrad)
    grad_gate = settle_weight(gate_wgrad)
    grad_up = settle_weight(up_wgrad)
    grad_attn = settle_weight(cut_heads(jnp.concatenate([qkv_wgrad, out_wgrad], 1)))
    grad_query = grad_attn[:, :qcols]
    grad_key = grad_attn[:, qcols : qcols + kcols]
    grad_value = grad_attn[:, qcols + kcols : qcols + 2 * kcols]
    grad_output = grad_attn[:, qcols + 2 * kcols :]

    def weighed(*pairs):
        return sum_steps(0.0, [jnp.sum(w.astype(f32) * g, 1) for w, g in pairs])

    gain_grads = lax.psum(
        jnp.stack(
            [
                weighed((w_query, grad_query), (key_weight, grad_key), (value_weight, grad_value)),
                weighed((w_gate, grad_gate), (w_up, grad_up)),
            ]
        ),
        ("zh", "zl"),
    )
    return (
        mixed,
        input_grad,
        gain_grads[0] / norm1_gain.astype(f32),
        grad_query,
        grad_key,
        grad_value,
        grad_output,
        gain_grads[1] / norm2_gain.astype(f32),
        grad_gate,
        grad_up,
        grad_down,
    )


def solution(mesh):
    dp, tensor = mesh.devices.shape
    ring = tensor // 2
    regrouped = Mesh(mesh.devices.reshape(dp // 2, 2, 2, ring), ("d", "c", "zh", "zl"))
    data, parts = ("d", "c"), ("zh", "zl")
    tokens_spec = P(data + parts, None)
    weight_spec = P(data, parts)
    in_specs = (
        tokens_spec,
        P(data),
        P(data),
        weight_spec,
        weight_spec,
        weight_spec,
        weight_spec,
        P(data),
        weight_spec,
        weight_spec,
        weight_spec,
        tokens_spec,
    )
    out_specs = (
        tokens_spec,
        tokens_spec,
        P(data),
        weight_spec,
        weight_spec,
        weight_spec,
        weight_spec,
        P(data),
        weight_spec,
        weight_spec,
        weight_spec,
    )
    return jax.shard_map(
        functools.partial(per_device, ring),
        mesh=regrouped,
        in_specs=in_specs,
        out_specs=out_specs,
        check_vma=False,
    )
```

```python
import functools
import math

import jax
import jax.numpy as jnp
from jax import lax
from jax.experimental import pallas as pl
from jax.experimental.pallas import tpu as pltpu
from jax.sharding import Mesh
from jax.sharding import PartitionSpec as P

HEAD_SIZE = 96
SEQUENCE_LENGTH = 2048
LANES = 128

epsilon = 1e-05
rope_base = 100000.0
masked_score = -1e30
query_scale = math.log2(math.e) * HEAD_SIZE ** (-0.5)
rows_both = (((0,), (0,)), ((), ()))
cols_both = (((1,), (1,)), ((), ()))
plain = (((1,), (0,)), ((), ()))
f32 = jnp.float32
light = pl.CostEstimate(flops=1, bytes_accessed=1, transcendentals=0)
bf16 = jnp.bfloat16


def local_block(g, place_ref, ring):
    other = lax.rem(g // ring + place_ref[0], 2)
    step = lax.rem(lax.rem(g, ring) - place_ref[1] + ring, ring)
    return 2 * step + other


def attend_kernel(ring, block, place_ref, q_ref, k_ref, v_ref, start_ref, o_ref, lse_ref):
    g = pl.program_id(1)
    share = q_ref.shape[1] // LANES
    start = start_ref[...]
    row = lax.broadcasted_iota(jnp.int32, (block, block), 0)
    col = lax.broadcasted_iota(jnp.int32, (block, block), 1)
    queries = [q_ref[:, h * LANES : (h + 1) * LANES] for h in range(share)]

    def step(kb, carry, diagonal):
        offset = pl.multiple_of(local_block(kb, place_ref, ring) * block, block)
        keys = k_ref[pl.ds(offset, block), :]
        values = v_ref[pl.ds(offset, block), :]
        shown = row >= start - kb * block
        if diagonal:
            shown = shown & (row <= col)
        out = []
        for h in range(share):
            largest, total, acc = carry[h]
            s = lax.dot_general(keys, queries[h], cols_both, preferred_element_type=f32)
            s = jnp.where(shown, s, masked_score)
            newest = jnp.maximum(largest, jnp.max(s, 0, keepdims=True))
            fade = jnp.exp2(largest - newest)
            p = jnp.exp2(s - newest)
            total = total * fade + jnp.sum(p, 0, keepdims=True)
            acc = acc * fade + lax.dot_general(
                values, p.astype(bf16), rows_both, preferred_element_type=f32
            )
            out.append((newest, total, acc))
        return tuple(out)

    carry = tuple(
        (
            jnp.full((1, block), masked_score, f32),
            jnp.zeros((1, block), f32),
            jnp.zeros((LANES, block), f32),
        )
        for _ in range(share)
    )
    carry = step(g, carry, True)
    carry = lax.fori_loop(0, g, lambda kb, c: step(kb, c, False), carry)
    for h in range(share):
        largest, total, acc = carry[h]
        o_ref[:, h * LANES : (h + 1) * LANES] = jnp.transpose(acc / total).astype(bf16)
        lse_ref[0, h : h + 1, :] = largest + jnp.log2(total)


def attend(place, q, k, v, start, ring):
    length = q.shape[0]
    block = length // (2 * ring)
    kv = k.shape[1] // LANES
    share = q.shape[1] // k.shape[1]

    def at(g, place_ref):
        return local_block(g, place_ref, ring)

    return pl.pallas_call(
        functools.partial(attend_kernel, ring, block),
        grid_spec=pltpu.PrefetchScalarGridSpec(
            num_scalar_prefetch=1,
            grid=(kv, 2 * ring),
            in_specs=[
                pl.BlockSpec((block, share * LANES), lambda h, g, z: (at(g, z), h)),
                pl.BlockSpec((length, LANES), lambda h, g, z: (0, h)),
                pl.BlockSpec((length, LANES), lambda h, g, z: (0, h)),
                pl.BlockSpec((1, block), lambda h, g, z: (0, at(g, z))),
            ],
            out_specs=[
                pl.BlockSpec((block, share * LANES), lambda h, g, z: (at(g, z), h)),
                pl.BlockSpec((1, share, block), lambda h, g, z: (h, 0, at(g, z))),
            ],
        ),
        out_shape=[
            jax.ShapeDtypeStruct(q.shape, bf16),
            jax.ShapeDtypeStruct((kv, share, length), f32),
        ],
        compiler_params=pltpu.CompilerParams(
            vmem_limit_bytes=40 * 2**20, dimension_semantics=("arbitrary", "arbitrary")
        ),
        cost_estimate=light,
        name="attend",
    )(place, q, k, v, start)


def attend_back_kernel(
    ring,
    block,
    place_ref,
    q_ref,
    k_ref,
    v_ref,
    o_ref,
    do_ref,
    lse_ref,
    start_ref,
    cosq_ref,
    sinq_ref,
    cosk_ref,
    sink_ref,
    dq_ref,
    dk_ref,
    dv_ref,
    dk_acc,
    dv_acc,
):
    g = pl.program_id(1)
    share = q_ref.shape[1] // LANES

    @pl.when(g == 0)
    def _():
        dk_acc[...] = jnp.zeros_like(dk_acc)
        dv_acc[...] = jnp.zeros_like(dv_acc)

    start = start_ref[...]
    row = lax.broadcasted_iota(jnp.int32, (block, block), 0)
    col = lax.broadcasted_iota(jnp.int32, (block, block), 1)
    heads = [slice(h * LANES, (h + 1) * LANES) for h in range(share)]
    queries = [q_ref[:, h] for h in heads]
    grads = [do_ref[:, h] for h in heads]
    lses = [lse_ref[0, h : h + 1, :] for h in range(share)]
    inner = [
        jnp.sum(
            jnp.transpose(do_ref[:, h].astype(f32) * o_ref[:, h].astype(f32)), 0, keepdims=True
        )
        for h in heads
    ]

    def step(kb, carry, diagonal):
        offset = pl.multiple_of(local_block(kb, place_ref, ring) * block, block)
        keys = k_ref[pl.ds(offset, block), :]
        values = v_ref[pl.ds(offset, block), :]
        shown = row >= start - kb * block
        if diagonal:
            shown = shown & (row <= col)
        out = []
        dk = jnp.zeros((block, LANES), f32)
        dv = jnp.zeros((block, LANES), f32)
        for h in range(share):
            s = lax.dot_general(keys, queries[h], cols_both, preferred_element_type=f32)
            p = jnp.where(shown, jnp.exp2(s - lses[h]), 0.0)
            dp = lax.dot_general(values, grads[h], cols_both, preferred_element_type=f32)
            ds = (p * (dp - inner[h])).astype(bf16)
            dv += jnp.dot(p.astype(bf16), grads[h], preferred_element_type=f32)
            dk += jnp.dot(ds, queries[h], preferred_element_type=f32)
            out.append(carry[h] + lax.dot_general(keys, ds, rows_both, preferred_element_type=f32))
        dk_acc[pl.ds(offset, block), :] += dk
        dv_acc[pl.ds(offset, block), :] += dv
        return tuple(out)

    carry = step(g, tuple(jnp.zeros((LANES, block), f32) for _ in range(share)), True)
    carry = lax.fori_loop(0, g, lambda kb, c: step(kb, c, False), carry)
    for h in range(share):
        u = jnp.transpose(carry[h]) * HEAD_SIZE ** (-0.5)
        turned = u * cosq_ref[...] - pltpu.roll(u, LANES // 2, 1) * sinq_ref[...]
        dq_ref[:, heads[h]] = turned.astype(bf16)

    @pl.when(g == pl.num_programs(1) - 1)
    def _():
        def finish(i, _):
            r = pl.ds(pl.multiple_of(i * block, block), block)
            u = dk_acc[r, :] * math.log(2.0)
            turned = u * cosk_ref[r, :] - pltpu.roll(u, LANES // 2, 1) * sink_ref[r, :]
            dk_ref[r, :] = turned.astype(bf16)
            dv_ref[r, :] = dv_acc[r, :].astype(bf16)
            return 0

        lax.fori_loop(0, 2 * ring, finish, 0)


def attend_back(place, q, k, v, o, do, lse, start, cos, sin, ring, head):
    length = q.shape[0]
    block = length // (2 * ring)
    share = q.shape[1] // k.shape[1]

    def at(g, place_ref):
        return local_block(g, place_ref, ring)

    qspec = pl.BlockSpec((block, share * LANES), lambda h, g, z: (at(g, z), head))
    kspec = pl.BlockSpec((length, LANES), lambda h, g, z: (0, head))
    qout = pl.BlockSpec((block, share * LANES), lambda h, g, z: (at(g, z), 0))
    kout = pl.BlockSpec((length, LANES), lambda h, g, z: (0, 0))
    tableq = pl.BlockSpec((block, LANES), lambda h, g, z: (at(g, z), 0))
    tablek = pl.BlockSpec((length, LANES), lambda h, g, z: (0, 0))
    return pl.pallas_call(
        functools.partial(attend_back_kernel, ring, block),
        grid_spec=pltpu.PrefetchScalarGridSpec(
            num_scalar_prefetch=1,
            grid=(1, 2 * ring),
            in_specs=[
                qspec,
                kspec,
                kspec,
                qspec,
                qspec,
                pl.BlockSpec((1, share, block), lambda h, g, z: (head, 0, at(g, z))),
                pl.BlockSpec((1, block), lambda h, g, z: (0, at(g, z))),
                tableq,
                tableq,
                tablek,
                tablek,
            ],
            out_specs=[qout, kout, kout],
            scratch_shapes=[pltpu.VMEM((length, LANES), f32), pltpu.VMEM((length, LANES), f32)],
        ),
        out_shape=[
            jax.ShapeDtypeStruct((length, share * LANES), bf16),
            jax.ShapeDtypeStruct((length, LANES), bf16),
            jax.ShapeDtypeStruct((length, LANES), bf16),
        ],
        compiler_params=pltpu.CompilerParams(
            vmem_limit_bytes=40 * 2**20, dimension_semantics=("arbitrary", "arbitrary")
        ),
        cost_estimate=light,
        name="attend_back",
    )(place, q, k, v, o, do, lse, start, cos, sin, cos, sin)


def pieces_spec(block, width, count):
    return [
        pl.BlockSpec((block, width), lambda i: (jnp.minimum(i, count - 1), 0)),
        pl.BlockSpec((block, width), lambda i: (jnp.maximum(i - count, 0), 0)),
    ]


def picked(count, first_ref, second_ref):
    return jnp.where(pl.program_id(0) < count, first_ref[...], second_ref[...])


def project_kernel(
    widths, count, x_ref, y_ref, gain_ref, w_ref, cos_ref, sin_ref, *refs
):
    a_ref, q_ref, k_ref, v_ref = refs[-4:]
    x = picked(count, x_ref, y_ref).astype(f32)
    root = lax.rsqrt(jnp.mean(x * x, -1, keepdims=True) + epsilon)
    a = (x * root * gain_ref[...]).astype(bf16)
    a_ref[...] = a
    cos = cos_ref[...]
    sin = sin_ref[...]
    whole = jnp.dot(a, w_ref[...], preferred_element_type=f32)
    qw, kw = widths
    for h in range((qw + kw) // LANES):
        u = whole[:, h * LANES : (h + 1) * LANES]
        turned = u * cos + pltpu.roll(u, LANES // 2, 1) * sin
        if h < qw // LANES:
            q_ref[:, h * LANES : (h + 1) * LANES] = (turned * query_scale).astype(bf16)
        else:
            j = h - qw // LANES
            k_ref[:, j * LANES : (j + 1) * LANES] = turned.astype(bf16)
    v_ref[...] = whole[:, qw + kw :].astype(bf16)


def project(pair, gain, w, cos, sin, qw, kw, step, before):
    rows, width = pair[0].shape
    length = cos.shape[0]
    block = min(256, rows)
    count = rows // block
    base = step * 2 * count
    widths = (width, qw, kw, kw)

    def row(n):
        return pl.BlockSpec((block, n), lambda i: (base + i, 0))

    def whole(shape):
        return pl.BlockSpec(shape, lambda i: (0, 0))

    return pl.pallas_call(
        functools.partial(project_kernel, (qw, kw), count),
        grid=(2 * count,),
        in_specs=pieces_spec(block, width, count)
        + [whole(gain.shape), whole((width, qw + 2 * kw)), row(LANES), row(LANES)]
        + [pl.BlockSpec(memory_space=pl.ANY)] * len(before),
        out_specs=[row(n) for n in widths],
        out_shape=[jax.ShapeDtypeStruct((length, n), bf16) for n in widths],
        input_output_aliases={6 + i: i for i in range(len(before))},
        compiler_params=pltpu.CompilerParams(
            vmem_limit_bytes=40 * 2**20, dimension_semantics=("arbitrary",)
        ),
        cost_estimate=light,
        name="project",
    )(*pair, gain, w, cos, sin, *before)


def hidden_kernel(
    chunk, count, a_ref, b_ref, dy_ref, dz_ref, w_ref, hid_ref, dgu_ref, da_ref, mixed_ref
):
    a = picked(count, a_ref, b_ref)
    dy = picked(count, dy_ref, dz_ref)
    units = hid_ref.shape[1]
    for j in range(units // chunk):
        at = slice(j * chunk, (j + 1) * chunk)
        up = slice(units + j * chunk, units + (j + 1) * chunk)
        down = slice(2 * units + j * chunk, 2 * units + (j + 1) * chunk)
        g = jnp.dot(a, w_ref[:, at], preferred_element_type=f32)
        u = jnp.dot(a, w_ref[:, up], preferred_element_type=f32)
        dh = jnp.dot(dy, w_ref[:, down], preferred_element_type=f32)
        sig = jax.nn.sigmoid(g)
        silu = g * sig
        hid_ref[:, at] = (silu * u).astype(bf16)
        dgu_ref[:, at] = (dh * u * (sig + silu * (1.0 - sig))).astype(bf16)
        dgu_ref[:, up] = (dh * silu).astype(bf16)
    da_ref[...] = lax.dot_general(
        dgu_ref[...], w_ref[:, : 2 * units], cols_both, preferred_element_type=f32
    ).astype(bf16)
    mixed_ref[...] = lax.dot_general(
        hid_ref[...], w_ref[:, 2 * units :], cols_both, preferred_element_type=f32
    ).astype(bf16)


def hidden_pass(a, dy, w):
    rows, width = a[0].shape
    units = w.shape[1] // 3
    block = min(256, rows)
    count = rows // block
    widths = [units, 2 * units, width, width]

    def row(n):
        return pl.BlockSpec((block, n), lambda i: (i, 0))

    return pl.pallas_call(
        functools.partial(hidden_kernel, min(256, units), count),
        grid=(2 * count,),
        in_specs=pieces_spec(block, width, count)
        + pieces_spec(block, width, count)
        + [pl.BlockSpec(w.shape, lambda i: (0, 0), pipeline_mode=pl.Buffered(1))],
        out_specs=[row(n) for n in widths],
        out_shape=[jax.ShapeDtypeStruct((2 * rows, n), bf16) for n in widths],
        compiler_params=pltpu.CompilerParams(
            vmem_limit_bytes=40 * 2**20, dimension_semantics=("arbitrary",)
        ),
        cost_estimate=light,
        name="hidden",
    )(*a, *dy, w)


def product_kernel(dims, x_ref, w_ref, *refs):
    p = lax.dot_general(x_ref[...], w_ref[...], dims, preferred_element_type=f32)
    out_ref = refs[-1]
    for ref in refs[:-1]:
        p = p + ref[...].astype(f32)
    out_ref[...] = p.astype(out_ref.dtype)


def product(x, w, dims, kind=bf16, rows=None, columns=(0, 1), add=None):
    first, last = (0, x.shape[0]) if rows is None else (rows.start, rows.stop)
    block = min(256, last - first)
    wide = w.shape[1] // columns[1]
    out = w.shape[0] if dims == cols_both else wide
    row = pl.BlockSpec((block, out), lambda i: (i, 0))
    extra = [] if add is None else [add]
    return pl.pallas_call(
        functools.partial(product_kernel, dims),
        grid=((last - first) // block,),
        in_specs=[
            pl.BlockSpec((block, x.shape[1]), lambda i: (first // block + i, 0)),
            pl.BlockSpec((w.shape[0], wide), lambda i: (0, columns[0])),
        ]
        + [row] * len(extra),
        out_specs=row,
        out_shape=jax.ShapeDtypeStruct((last - first, out), kind),
        compiler_params=pltpu.CompilerParams(
            vmem_limit_bytes=40 * 2**20, dimension_semantics=("arbitrary",)
        ),
        cost_estimate=light,
        name="product",
    )(x, w, *extra)


def wgrad_kernel(counts, *refs):
    out_ref = refs[-1]
    j = pl.program_id(0)
    first = 0
    refs = refs[:-1]
    for pieces, blocks in counts:
        lefts, rights, refs = refs[:pieces], refs[pieces : 2 * pieces], refs[2 * pieces :]

        @pl.when((j >= first) & (j < first + blocks))
        def _():
            total = None
            for a, b in zip(lefts, rights):
                p = lax.dot_general(a[...], b[...], rows_both, preferred_element_type=f32)
                total = p if total is None else total + p
            out_ref[...] = total.astype(bf16)

        first += blocks


def wgrad(groups, rows):
    width = groups[0][0][0].shape[1]
    block = min([512] + [group[0][2].shape[1] for group in groups])
    counts, specs, args = [], [], []
    first = 0
    for group in groups:
        blocks = group[0][2].shape[1] // block
        counts.append((len(group), blocks))
        for a, at, _, _ in group:
            specs.append(
                pl.BlockSpec(
                    (rows, width), lambda j, at=at: (at, 0), pipeline_mode=pl.Buffered(1)
                )
            )
            args.append(a)
        for _, _, b, at in group:

            def spot(j, at=at, first=first, blocks=blocks):
                return (at, jnp.clip(j - first, 0, blocks - 1))

            specs.append(pl.BlockSpec((rows, block), spot))
            args.append(b)
        first += blocks
    return pl.pallas_call(
        functools.partial(wgrad_kernel, counts),
        grid=(first,),
        in_specs=specs,
        out_specs=pl.BlockSpec((width, block), lambda j: (0, j)),
        out_shape=jax.ShapeDtypeStruct((width, first * block), bf16),
        compiler_params=pltpu.CompilerParams(
            vmem_limit_bytes=40 * 2**20, dimension_semantics=("arbitrary",)
        ),
        cost_estimate=light,
        name="wgrad",
    )(*args)


def row_pass(body, name, inputs, whole, kinds):
    width = inputs[0][0].shape[1]
    rows = min(a.shape[0] - first for a, first in inputs)
    block = min(256, rows)

    def kernel(*refs):
        count = len(inputs) + len(whole)
        values = [ref[...].astype(f32) for ref in refs[:count]]
        for ref, value in zip(refs[count:], body(*values)):
            ref[...] = value.astype(ref.dtype)

    return pl.pallas_call(
        kernel,
        grid=(rows // block,),
        in_specs=[
            pl.BlockSpec((block, width), lambda i, first=first: (first // block + i, 0))
            for _, first in inputs
        ]
        + [pl.BlockSpec(a.shape, lambda i: (0, 0)) for a in whole],
        out_specs=[pl.BlockSpec((block, width), lambda i: (i, 0)) for _ in kinds],
        out_shape=[jax.ShapeDtypeStruct((rows, width), kind) for kind in kinds],
        compiler_params=pltpu.CompilerParams(dimension_semantics=("arbitrary",)),
        cost_estimate=light,
        name=name,
    )(*[a for a, _ in inputs], *whole)


def inverse_root(x):
    return lax.rsqrt(jnp.mean(x * x, -1, keepdims=True) + epsilon)


def add_rows(*items):
    return (sum_steps(items[0], items[1:]),)


def norm_forward(stream, *rest):
    *terms, gain = rest
    middle = sum_steps(stream, terms)
    return middle, middle * inverse_root(middle) * gain


def norm_back(residual, values, *rest):
    *terms, gain = rest
    root = inverse_root(values)
    scaled = sum_steps(terms[0], terms[1:]) * gain
    out = (
        residual
        + root * scaled
        - values * root**3 * jnp.mean(scaled * values, -1, keepdims=True)
    )
    return out, out


def pad_heads(w):
    half = HEAD_SIZE // 2
    parts = w.reshape(w.shape[0], -1, half)
    return jnp.pad(parts, ((0, 0), (0, 0), (0, LANES // 2 - half))).reshape(w.shape[0], -1)


def cut_heads(w):
    half = HEAD_SIZE // 2
    parts = w.reshape(w.shape[0], -1, LANES // 2)
    return parts[:, :, :half].reshape(w.shape[0], -1)


swap_two = [(0, 1), (1, 0)]
cross_pairs = [(1, 2), (2, 1)]
slant_pairs = [(2 * c + zh, 2 * zh + (1 - c)) for c in range(2) for zh in range(2)]
slant_back = [(b, a) for a, b in slant_pairs]


def stays():
    return lax.axis_index("c") == lax.axis_index("zh")


def cross(a):
    return lax.ppermute(a, ("c", "zh"), cross_pairs)


def relay(a):
    return jnp.where(stays(), a, cross(a))


def other_core(a):
    return lax.ppermute(a, "c", swap_two)


def from_neighbour(a, k, ring):
    return lax.ppermute(a, "zl", [(i, (i - k) % ring) for i in range(ring)])


def both_cores(a):
    return jnp.concatenate([a, other_core(a)], 0)


def spread_pair(w):
    return w, cross(w), lax.ppermute(w, ("c", "zh"), slant_pairs)


def arrange(own, crossed, slanted):
    first = lax.axis_index("zh") == 0
    straight = jnp.where(stays(), own, crossed)
    return jnp.concatenate(
        [jnp.where(first, straight, slanted), jnp.where(first, slanted, straight)], 0
    )


def gather_rows(w):
    return lax.all_gather(w, "d", axis=0, tiled=True)


def send_blocks(part):
    rows = part.shape[0] // 2
    first = lax.axis_index("zh") == 0
    upper, lower = part[:rows], part[rows:]
    straight = jnp.where(first, upper, lower)
    slanted = lax.ppermute(jnp.where(first, lower, upper), ("c", "zh"), slant_back)
    return straight, cross(straight), slanted


def add_blocks(blocks):
    straight, crossed, slanted = blocks
    return jnp.where(stays(), straight, crossed).astype(f32) + slanted.astype(f32)


def sum_rows(grad):
    return lax.psum_scatter(grad.astype(bf16), "d", scatter_dimension=0, tiled=True)


def after(first, then):
    return lax.optimization_barrier((first, then))[1]


def together(a, b):
    return lax.optimization_barrier((a, b))


def dot(a, b):
    return jnp.dot(a, b, preferred_element_type=f32)


def dot_cols(a, b):
    return lax.dot_general(a, b, cols_both, preferred_element_type=f32)


def dot_rows(a, b):
    return lax.dot_general(a, b, rows_both, preferred_element_type=f32)


def sum_steps(first, second):
    out = first
    for item in second:
        out = out + item
    return out


def per_device(
    ring,
    tokens,
    positions,
    norm1_gain,
    w_query,
    key_weight,
    value_weight,
    w_out,
    norm2_gain,
    w_gate,
    w_up,
    w_down,
    cotangent,
):
    steps = range(ring)
    core = lax.axis_index("c")
    column = lax.axis_index("zl")
    place = jnp.stack([core, column]).astype(jnp.int32)
    rows = tokens.shape[0]
    length = 2 * ring * rows

    def swap_chips(own):
        return [from_neighbour(own, k, ring) for k in steps[1:]]

    def join_cores(partial, kind=bf16):
        theirs = other_core(partial(slice(rows, 2 * rows), bf16))
        return partial(slice(0, rows), kind, theirs)

    def join(mine, theirs):
        return row_pass(add_rows, "join", [(mine, 0), (theirs, 0)], [], [bf16])[0]

    def chip_slice(k, r):
        return slice(2 * rows * k + r.start, 2 * rows * k + r.stop)

    def send_chips(joined):
        return [
            lax.ppermute(p.astype(bf16), "zl", [(i, (i + k) % ring) for i in steps])
            for k, p in zip(steps[1:], joined)
        ]

    def pairs_of(kept, k):
        out = []
        for c in range(2):
            for zh in range(2):
                if (c == zh) == kept:
                    base = (2 * c + zh) * ring
                    out += [(base + i, base + (i - k) % ring) for i in steps]
        return out

    def early_neighbours(original):
        return [
            lax.ppermute(original, ("c", "zh", "zl"), pairs_of(True, k)) for k in steps if k
        ]

    def late_neighbours(moved):
        return [lax.ppermute(moved, ("c", "zh", "zl"), pairs_of(False, k)) for k in steps[1:]]

    def choose(early, late):
        return [jnp.where(stays(), e, l) for e, l in zip(early, late)]

    qcols, kcols = w_query.shape[1], key_weight.shape[1]
    qw = qcols // HEAD_SIZE * LANES
    kw = kcols // HEAD_SIZE * LANES
    half = HEAD_SIZE // 2
    attn_shard = pad_heads(jnp.concatenate([w_query, key_weight, value_weight, w_out], 1))
    attn_shard = jnp.concatenate(
        [
            attn_shard[:, :half],
            norm1_gain[:, None],
            norm2_gain[:, None],
            attn_shard[:, half + 2 :],
        ],
        1,
    )
    places = jnp.where(stays(), positions, other_core(positions)).reshape(2, ring, rows)
    attn_shard = after(places, attn_shard)
    attn_pair = spread_pair(attn_shard)
    attn_rows = arrange(*attn_pair)
    tokens = after(attn_rows, tokens)
    attn_full = gather_rows(attn_rows)
    stream_raw = cross(tokens)
    tokens_early = early_neighbours(tokens)

    ordered = [
        lax.dynamic_index_in_dim(
            lax.dynamic_index_in_dim(places, (core + j) % 2, 0, keepdims=False),
            (column + k) % ring,
            0,
            keepdims=False,
        )
        for k in steps
        for j in range(2)
    ]
    firsts = [
        ((core + j) % 2 * ring + (column + k) % ring) * rows for k in steps for j in range(2)
    ]
    start = jnp.concatenate(
        [f + jnp.arange(rows, dtype=jnp.int32) - o for f, o in zip(firsts, ordered)]
    )[None, :]
    spots = jnp.concatenate(ordered).astype(f32)
    inverse = rope_base ** (-(2.0 / HEAD_SIZE) * jnp.arange(half, dtype=f32))
    angles = spots[:, None] * inverse[None, :]
    gap = jnp.zeros((length, LANES // 2 - half), f32)
    cos_half, sin_half = jnp.cos(angles), jnp.sin(angles)
    cos = jnp.concatenate([cos_half, gap, cos_half, gap], 1)
    sin = jnp.concatenate([-sin_half, gap, sin_half, gap], 1)

    stream_raw, tokens_early = after((cos, sin, start), (stream_raw, tokens_early))
    ff_cols = after((stream_raw, tokens_early), jnp.concatenate([w_gate, w_up, w_down], 1))
    stream_own = jnp.where(stays(), tokens, stream_raw)
    tokens_late = late_neighbours(stream_raw)
    ff_pair = spread_pair(ff_cols)

    out_columns = ((qw + 2 * kw) // qw, (qw + 2 * kw) // qw + 1)
    gain_first = attn_full[:, half].astype(f32)[None, :]
    gain_second = attn_full[:, half + 1].astype(f32)[None, :]

    projected = project(
        (stream_own, other_core(stream_own)), gain_first, attn_full, cos, sin, qw, kw, 0, ()
    )
    (tokens_late, ff_pair), projected = together((tokens_late, ff_pair), projected)
    others = [(x, other_core(x)) for x in choose(tokens_early, tokens_late)]
    others, ff_pair = together(others, ff_pair)
    ff_rows = arrange(*ff_pair)
    ff_full = gather_rows(ff_rows)
    cot_sent = after(others, cotangent)
    cot_raw = cross(cot_sent)
    cot_early = early_neighbours(cot_sent)
    for k, pair in enumerate(others, 1):
        projected = project(pair, gain_first, attn_full, cos, sin, qw, kw, k, projected)
    normed_first, q, k, v = projected
    o, lse = attend(place, q, k, v, start, ring)
    o, (cot_raw, cot_early) = together(o, (cot_raw, cot_early))

    def out_product(k):
        return lambda r, kind, add=None: product(
            o, attn_full, cols_both, kind, chip_slice(k, r), out_columns, add
        )

    def whole_rows(*arrays):
        return [(a, 0) for a in arrays]

    sent = send_chips([join_cores(out_product(k)) for k in steps[1:]])
    joined = join_cores(out_product(0))
    cot_own = after(joined, jnp.where(stays(), cotangent, cot_raw))
    sent = after((joined, cot_own), sent)
    middle, normed_second = row_pass(
        norm_forward,
        "norm_forward",
        whole_rows(stream_own, joined, *sent),
        [gain_second],
        [f32, bf16],
    )

    ff_others = swap_chips(normed_second)
    cot_late = late_neighbours(after(normed_second, cot_own))
    ff_in = [(normed_second, other_core(normed_second))]
    out_grads = [(cot_own, other_core(cot_own))]
    hidden = [hidden_pass(ff_in[0], out_grads[0], ff_full)]
    hidden[0], (ff_others, cot_late) = together(hidden[0], (ff_others, cot_late))

    def halves(array):
        return [array, other_core(array[rows:])]

    second_own = halves(hidden[0][2])
    mixed_own = halves(hidden[0][3])
    for a, dy in zip(ff_others, choose(cot_early, cot_late)):
        ff_in.append((a, other_core(a)))
        out_grads.append((dy, other_core(dy)))
        hidden.append(hidden_pass(ff_in[-1], out_grads[-1], ff_full))

    def pieces(pairs, hidden, i):
        return [(a, 0, h[i], j) for pair, h in zip(pairs, hidden) for j, a in enumerate(pair)]

    joined = [join(*halves(h[2])) for h in hidden[1:]]
    mixed_joined = [join(*halves(h[3])) for h in hidden[1:]]
    sent = send_chips(joined)
    (mixed_joined, second_own, mixed_own), hidden = after(
        joined, ((mixed_joined, second_own, mixed_own), hidden)
    )
    down_wgrad = wgrad([pieces(out_grads, hidden, 0)], rows)
    sent = after((mixed_joined, down_wgrad), sent)
    down_part = sum_rows(after(sent, down_wgrad))
    middle_grad, db = row_pass(
        norm_back,
        "norm_back",
        whole_rows(cot_own, middle, *second_own, *sent),
        [gain_second],
        [f32, bf16],
    )
    branch_others = swap_chips(db)
    branch = [(db, other_core(db))]
    do = [product(b, attn_full, plain, columns=out_columns) for b in branch[0]]
    gate_up_wgrad = wgrad([pieces(ff_in, after(do, hidden), 1)], rows)
    branch_others = after(gate_up_wgrad, branch_others)
    gate_up_part = sum_rows(after(branch_others, gate_up_wgrad))
    mixed_joined, down_part = after(branch_others, (mixed_joined, down_part))
    mixed_sent = send_chips(mixed_joined)
    down_blocks = send_blocks(down_part)
    for b in branch_others:
        branch.append((b, other_core(b)))
        do += [product(b, attn_full, plain, columns=out_columns) for b in branch[-1]]
    do = jnp.concatenate(do, 0)
    heads = []
    kvheads = kw // LANES
    for h in range(kvheads):
        part = attend_back(place, q, k, v, o, do, lse, start, cos, sin, ring, h)
        if h == 0:
            (mixed_sent, down_blocks), (part, do) = together(
                (mixed_sent, down_blocks), (part, do)
            )
            mixed = row_pass(
                add_rows, "mixed", whole_rows(middle, *mixed_own, *mixed_sent), [], [bf16]
            )[0]
            mixed_raw = cross(mixed)
        heads.append(part)
    mixed_raw, heads = together(mixed_raw, heads)
    mixed = jnp.where(stays(), mixed, mixed_raw)
    gate_up_blocks = send_blocks(after(heads, gate_up_part))
    dqkv = jnp.concatenate([h[i] for i in range(3) for h in heads], 1)
    grad_down = add_blocks(down_blocks)

    def first_product(k, dqkv):
        return lambda r, kind, add=None: product(
            dqkv, w_qkv, cols_both, kind, chip_slice(k, r), add=add
        )

    w_qkv = attn_full[:, : qw + 2 * kw]
    blocks = range(2 * ring)
    attn_wgrad = wgrad(
        [
            [(normed_first, i, dqkv, i) for i in blocks],
            [(b, 0, o, i) for i, b in zip(blocks, sum(branch, ()))],
        ],
        rows,
    )
    attn_part = sum_rows(after(gate_up_part, attn_wgrad))
    dqkv = after(attn_wgrad, dqkv)
    joined = [join_cores(first_product(k, dqkv)) for k in steps[1:]]
    sent = send_chips(joined)
    dqkv = after(joined, dqkv)
    first_own = join_cores(first_product(0, dqkv))
    sent, (first_own, gate_up_blocks) = together(sent, (first_own, gate_up_blocks))
    input_grad = row_pass(
        norm_back,
        "norm_back",
        whole_rows(middle_grad, stream_own, first_own, *sent),
        [gain_first],
        [bf16, bf16],
    )[0]
    input_raw = cross(input_grad)
    attn_blocks = send_blocks(attn_part)

    def weighed(weights, part):
        weights = weights[:, : part.shape[1]]
        return jnp.sum(weights.astype(f32) * part.astype(f32), 1).reshape(2, -1)

    gain_parts = jnp.stack(
        [
            weighed(attn_rows, attn_part[:, : qw + 2 * kw]),
            weighed(ff_rows, gate_up_part),
        ]
    )
    gain_parts = jnp.where(core == 0, gain_parts, gain_parts[:, ::-1])
    gain_grads = gain_parts[:, 0] + other_core(gain_parts[:, 1])
    for k in steps[1:]:
        gain_parts = from_neighbour(gain_grads, k, ring) + (gain_parts if k > 1 else gain_grads)
    gain_grads = gain_parts if ring > 1 else gain_grads
    gain_grads = gain_grads + lax.ppermute(gain_grads, "zh", swap_two)
    (input_raw, attn_blocks), gain_grads = together((input_raw, attn_blocks), gain_grads)
    input_grad = jnp.where(stays(), input_grad, input_raw).astype(f32)
    grad_gate_up = add_blocks(gate_up_blocks)
    grad_attn = cut_heads(add_blocks(attn_blocks))
    grad_query = grad_attn[:, :qcols]
    grad_key = grad_attn[:, qcols : qcols + kcols]
    grad_value = grad_attn[:, qcols + kcols : qcols + 2 * kcols]
    grad_output = grad_attn[:, qcols + 2 * kcols :]
    grad_gate = grad_gate_up[:, : w_gate.shape[1]]
    grad_up = grad_gate_up[:, w_gate.shape[1] :]

    return (
        mixed,
        input_grad,
        gain_grads[0] / norm1_gain.astype(f32),
        grad_query,
        grad_key,
        grad_value,
        grad_output,
        gain_grads[1] / norm2_gain.astype(f32),
        grad_gate,
        grad_up,
        grad_down,
    )


def solution(mesh):
    dp, tensor = mesh.devices.shape
    ring = tensor // 2
    regrouped = Mesh(mesh.devices.reshape(dp // 2, 2, 2, ring), ("d", "c", "zh", "zl"))
    data, parts = ("d", "c"), ("zh", "zl")
    tokens_spec = P(data + parts, None)
    weight_spec = P(data, parts)
    in_specs = (
        tokens_spec,
        P(data),
        P(data),
        weight_spec,
        weight_spec,
        weight_spec,
        weight_spec,
        P(data),
        weight_spec,
        weight_spec,
        weight_spec,
        tokens_spec,
    )
    out_specs = (
        tokens_spec,
        tokens_spec,
        P(data),
        weight_spec,
        weight_spec,
        weight_spec,
        weight_spec,
        P(data),
        weight_spec,
        weight_spec,
        weight_spec,
    )
    return jax.shard_map(
        functools.partial(per_device, ring),
        mesh=regrouped,
        in_specs=in_specs,
        out_specs=out_specs,
        check_vma=False,
    )
```

```python
import functools
import math

import jax
import jax.numpy as jnp
from jax import lax
from jax.experimental import pallas as pl
from jax.experimental.pallas import tpu as pltpu
from jax.sharding import Mesh
from jax.sharding import PartitionSpec as P

HEAD_SIZE = 96
SEQUENCE_LENGTH = 2048
LANES = 128

epsilon = 1e-05
rope_base = 100000.0
masked_score = -1e30
query_scale = math.log2(math.e) * HEAD_SIZE ** (-0.5)
rows_both = (((0,), (0,)), ((), ()))
cols_both = (((1,), (1,)), ((), ()))
plain = (((1,), (0,)), ((), ()))
f32 = jnp.float32
light = pl.CostEstimate(flops=1, bytes_accessed=1, transcendentals=0)
bf16 = jnp.bfloat16


def flipped(core, column, place, ring):
    return jnp.where(core == place[2], column, ring - 1 - column)


def local_block(g, place, ring):
    core = g // ring
    column = flipped(core, lax.rem(g, ring), place, ring)
    step = lax.rem(column - place[1] + ring, ring)
    return 2 * step + lax.rem(core + place[0], 2)


def global_block(l, place, ring):
    core = lax.rem(lax.rem(l, 2) + place[0], 2)
    column = lax.rem(l // 2 + place[1], ring)
    return core * ring + flipped(core, column, place, ring)


def in_hbm(*arrays):
    return [pltpu.with_memory_space_constraint(a, pltpu.HBM) for a in arrays]


def attend_kernel(ring, block, chip, place_ref, q_ref, k_ref, v_ref, start_ref, o_ref, lse_ref):
    g = global_block(2 * chip + pl.program_id(1), place_ref, ring)
    share = q_ref.shape[1] // LANES
    start = start_ref[...]
    row = lax.broadcasted_iota(jnp.int32, (block, block), 0)
    col = lax.broadcasted_iota(jnp.int32, (block, block), 1)
    queries = [q_ref[:, h * LANES : (h + 1) * LANES] for h in range(share)]

    def step(kb, carry, diagonal):
        offset = pl.multiple_of(local_block(kb, place_ref, ring) * block, block)
        keys = k_ref[pl.ds(offset, block), :]
        values = v_ref[pl.ds(offset, block), :]
        shown = row >= start - kb * block
        if diagonal:
            shown = shown & (row <= col)
        out = []
        for h in range(share):
            largest, total, acc = carry[h]
            s = lax.dot_general(keys, queries[h], cols_both, preferred_element_type=f32)
            s = jnp.where(shown, s, masked_score)
            newest = jnp.maximum(largest, jnp.max(s, 0, keepdims=True))
            fade = jnp.exp2(largest - newest)
            p = jnp.exp2(s - newest)
            total = total * fade + jnp.sum(p, 0, keepdims=True)
            acc = acc * fade + lax.dot_general(
                values, p.astype(bf16), rows_both, preferred_element_type=f32
            )
            out.append((newest, total, acc))
        return tuple(out)

    carry = tuple(
        (
            jnp.full((1, block), masked_score, f32),
            jnp.zeros((1, block), f32),
            jnp.zeros((LANES, block), f32),
        )
        for _ in range(share)
    )
    carry = step(g, carry, 8)
    carry = lax.fori_loop(0, g, lambda kb, c: step(kb, c, False), carry)
    for h in range(share):
        largest, total, acc = carry[h]
        o_ref[:, h * LANES : (h + 1) * LANES] = jnp.transpose(acc / total).astype(bf16)
        lse_ref[0, h : h + 1, :] = largest + jnp.log2(total)


def attend(chip, place, q, k, v, start, ring):
    length = q.shape[0]
    block = length // (2 * ring)
    kv = k.shape[1] // LANES
    share = q.shape[1] // k.shape[1]
    return pl.pallas_call(
        functools.partial(attend_kernel, ring, block, chip),
        grid_spec=pltpu.PrefetchScalarGridSpec(
            num_scalar_prefetch=1,
            grid=(kv, 2),
            in_specs=[
                pl.BlockSpec((block, share * LANES), lambda h, j, z: (2 * chip + j, h)),
                pl.BlockSpec((length, LANES), lambda h, j, z: (0, h)),
                pl.BlockSpec((length, LANES), lambda h, j, z: (0, h)),
                pl.BlockSpec((1, block), lambda h, j, z: (0, 2 * chip + j)),
            ],
            out_specs=[
                pl.BlockSpec((block, share * LANES), lambda h, j, z: (j, h)),
                pl.BlockSpec((1, share, block), lambda h, j, z: (h, 0, j)),
            ],
        ),
        out_shape=[
            jax.ShapeDtypeStruct((2 * block, q.shape[1]), bf16),
            jax.ShapeDtypeStruct((kv, share, 2 * block), f32),
        ],
        compiler_params=pltpu.CompilerParams(
            vmem_limit_bytes=40 * 2**20, dimension_semantics=("arbitrary", "arbitrary")
        ),
        cost_estimate=light,
        name="attend",
    )(place, q, k, v, start)


def attend_back_kernel(
    ring,
    block,
    chip,
    final,
    place_ref,
    q_ref,
    k_ref,
    v_ref,
    o_ref,
    do_ref,
    lse_ref,
    start_ref,
    cosq_ref,
    sinq_ref,
    *refs,
):
    if final:
        cosk_ref, sink_ref = refs[:2]
    before = refs[2 * final : -5]
    dq_ref, dk_ref, dv_ref, dk_acc, dv_acc = refs[-5:]
    j = pl.program_id(1)
    g = global_block(2 * chip + j, place_ref, ring)
    share = q_ref.shape[1] // LANES

    @pl.when(j == 0)
    def _():
        if before:
            dk_acc[...] = before[0][...]
            dv_acc[...] = before[1][...]
        else:
            dk_acc[...] = jnp.zeros_like(dk_acc)
            dv_acc[...] = jnp.zeros_like(dv_acc)

    start = start_ref[...]
    row = lax.broadcasted_iota(jnp.int32, (block, block), 0)
    col = lax.broadcasted_iota(jnp.int32, (block, block), 1)
    heads = [slice(h * LANES, (h + 1) * LANES) for h in range(share)]
    queries = [q_ref[:, h] for h in heads]
    grads = [do_ref[:, h] for h in heads]
    lses = [lse_ref[0, h : h + 1, :] for h in range(share)]
    inner = [
        jnp.sum(
            jnp.transpose(do_ref[:, h].astype(f32) * o_ref[:, h].astype(f32)), 0, keepdims=True
        )
        for h in heads
    ]

    def step(kb, carry, diagonal):
        offset = pl.multiple_of(local_block(kb, place_ref, ring) * block, block)
        keys = k_ref[pl.ds(offset, block), :]
        values = v_ref[pl.ds(offset, block), :]
        shown = row >= start - kb * block
        if diagonal:
            shown = shown & (row <= col)
        out = []
        dk = jnp.zeros((block, LANES), f32)
        dv = jnp.zeros((block, LANES), f32)
        for h in range(share):
            s = lax.dot_general(keys, queries[h], cols_both, preferred_element_type=f32)
            p = jnp.where(shown, jnp.exp2(s - lses[h]), 0.0)
            dp = lax.dot_general(values, grads[h], cols_both, preferred_element_type=f32)
            ds = (p * (dp - inner[h])).astype(bf16)
            dv += jnp.dot(p.astype(bf16), grads[h], preferred_element_type=f32)
            dk += jnp.dot(ds, queries[h], preferred_element_type=f32)
            out.append(carry[h] + lax.dot_general(keys, ds, rows_both, preferred_element_type=f32))
        dk_acc[pl.ds(offset, block), :] += dk
        dv_acc[pl.ds(offset, block), :] += dv
        return tuple(out)

    carry = step(g, tuple(jnp.zeros((LANES, block), f32) for _ in range(share)), 8)
    carry = lax.fori_loop(0, g, lambda kb, c: step(kb, c, False), carry)
    for h in range(share):
        u = jnp.transpose(carry[h]) * HEAD_SIZE ** (-0.5)
        turned = u * cosq_ref[...] - pltpu.roll(u, LANES // 2, 1) * sinq_ref[...]
        dq_ref[:, heads[h]] = turned.astype(bf16)

    @pl.when(j == 1)
    def _():
        def finish(i, _):
            r = pl.ds(pl.multiple_of(i * block, block), block)
            u = dk_acc[r, :]
            if final:
                u = u * math.log(2.0)
                u = u * cosk_ref[r, :] - pltpu.roll(u, LANES // 2, 1) * sink_ref[r, :]
            dk_ref[r, :] = u.astype(dk_ref.dtype)
            dv_ref[r, :] = dv_acc[r, :].astype(dv_ref.dtype)
            return 0

        lax.fori_loop(0, 2 * ring, finish, 0)


def attend_back(chip, place, q, k, v, o, do, lse, start, cos, sin, ring, before):
    length = q.shape[0]
    block = length // (2 * ring)
    kv = k.shape[1] // LANES
    share = q.shape[1] // k.shape[1]
    final = chip == ring - 1
    kind = bf16 if final else f32
    qspec = pl.BlockSpec((block, share * LANES), lambda h, j, z: (2 * chip + j, h))
    own = pl.BlockSpec((block, share * LANES), lambda h, j, z: (j, h))
    kspec = pl.BlockSpec((length, LANES), lambda h, j, z: (0, h))
    table = pl.BlockSpec((block, LANES), lambda h, j, z: (2 * chip + j, 0))
    whole = pl.BlockSpec((length, LANES), lambda h, j, z: (0, 0))
    return pl.pallas_call(
        functools.partial(attend_back_kernel, ring, block, chip, final),
        grid_spec=pltpu.PrefetchScalarGridSpec(
            num_scalar_prefetch=1,
            grid=(kv, 2),
            in_specs=[
                qspec,
                kspec,
                kspec,
                own,
                own,
                pl.BlockSpec((1, share, block), lambda h, j, z: (h, 0, j)),
                pl.BlockSpec((1, block), lambda h, j, z: (0, 2 * chip + j)),
                table,
                table,
            ]
            + [whole, whole] * final
            + [kspec] * len(before),
            out_specs=[own, kspec, kspec],
            scratch_shapes=[pltpu.VMEM((length, LANES), f32), pltpu.VMEM((length, LANES), f32)],
        ),
        out_shape=[
            jax.ShapeDtypeStruct((2 * block, q.shape[1]), bf16),
            jax.ShapeDtypeStruct(k.shape, kind),
            jax.ShapeDtypeStruct(k.shape, kind),
        ],
        compiler_params=pltpu.CompilerParams(
            vmem_limit_bytes=40 * 2**20, dimension_semantics=("arbitrary", "arbitrary")
        ),
        cost_estimate=light,
        name="attend_back",
    )(place, q, k, v, o, do, lse, start, cos, sin, *[cos, sin] * final, *before)


def pieces_spec(block, width, count):
    return [
        pl.BlockSpec((block, width), lambda i: (jnp.minimum(i, count - 1), 0)),
        pl.BlockSpec((block, width), lambda i: (jnp.maximum(i - count, 0), 0)),
    ]


def picked(count, first_ref, second_ref):
    return jnp.where(pl.program_id(0) < count, first_ref[...], second_ref[...])


def project_kernel(
    widths, count, x_ref, y_ref, gain_ref, w_ref, cos_ref, sin_ref, *refs
):
    a_ref, q_ref, k_ref, v_ref = refs[-4:]
    x = picked(count, x_ref, y_ref).astype(f32)
    root = lax.rsqrt(jnp.mean(x * x, -1, keepdims=True) + epsilon)
    a = (x * root * gain_ref[...]).astype(bf16)
    a_ref[...] = a
    cos = cos_ref[...]
    sin = sin_ref[...]
    whole = jnp.dot(a, w_ref[...], preferred_element_type=f32)
    qw, kw = widths
    for h in range((qw + kw) // LANES):
        u = whole[:, h * LANES : (h + 1) * LANES]
        turned = u * cos + pltpu.roll(u, LANES // 2, 1) * sin
        if h < qw // LANES:
            q_ref[:, h * LANES : (h + 1) * LANES] = (turned * query_scale).astype(bf16)
        else:
            j = h - qw // LANES
            k_ref[:, j * LANES : (j + 1) * LANES] = turned.astype(bf16)
    v_ref[...] = whole[:, qw + kw :].astype(bf16)


def project(pair, gain, w, cos, sin, qw, kw, step, before):
    rows, width = pair[0].shape
    length = cos.shape[0]
    block = min(256, rows)
    count = rows // block
    base = step * 2 * count
    widths = (width, qw, kw, kw)

    def row(n):
        return pl.BlockSpec((block, n), lambda i: (base + i, 0))

    def whole(shape):
        return pl.BlockSpec(shape, lambda i: (0, 0))

    return pl.pallas_call(
        functools.partial(project_kernel, (qw, kw), count),
        grid=(2 * count,),
        in_specs=pieces_spec(block, width, count)
        + [whole(gain.shape), whole((width, qw + 2 * kw)), row(LANES), row(LANES)]
        + [pl.BlockSpec(memory_space=pl.ANY)] * len(before),
        out_specs=[row(n) for n in widths],
        out_shape=[jax.ShapeDtypeStruct((length, n), bf16) for n in widths],
        input_output_aliases={6 + i: i for i in range(len(before))},
        compiler_params=pltpu.CompilerParams(
            vmem_limit_bytes=40 * 2**20, dimension_semantics=("arbitrary",)
        ),
        cost_estimate=light,
        name="project",
    )(*in_hbm(*pair), gain, *in_hbm(w), cos, sin, *in_hbm(*before))


def hidden_kernel(
    chunk, count, a_ref, b_ref, dy_ref, dz_ref, w_ref, hid_ref, dgu_ref, *refs
):
    a = picked(count, a_ref, b_ref)
    dy = picked(count, dy_ref, dz_ref)
    units = hid_ref.shape[1]
    for j in range(units // chunk):
        at = slice(j * chunk, (j + 1) * chunk)
        up = slice(units + j * chunk, units + (j + 1) * chunk)
        down = slice(2 * units + j * chunk, 2 * units + (j + 1) * chunk)
        g = jnp.dot(a, w_ref[:, at], preferred_element_type=f32)
        u = jnp.dot(a, w_ref[:, up], preferred_element_type=f32)
        dh = jnp.dot(dy, w_ref[:, down], preferred_element_type=f32)
        sig = jax.nn.sigmoid(g)
        silu = g * sig
        hid_ref[:, at] = (silu * u).astype(bf16)
        dgu_ref[:, at] = (dh * u * (sig + silu * (1.0 - sig))).astype(bf16)
        dgu_ref[:, up] = (dh * silu).astype(bf16)
    da = lax.dot_general(
        dgu_ref[...], w_ref[:, : 2 * units], cols_both, preferred_element_type=f32
    ).astype(bf16)
    mixed = lax.dot_general(
        hid_ref[...], w_ref[:, 2 * units :], cols_both, preferred_element_type=f32
    ).astype(bf16)
    mine = pl.program_id(0) < count

    @pl.when(mine)
    def _():
        refs[0][...] = da
        refs[2][...] = mixed

    @pl.when(jnp.logical_not(mine))
    def _():
        refs[1][...] = da
        refs[3][...] = mixed


def hidden_pass(a, dy, w):
    rows, width = a[0].shape
    units = w.shape[1] // 3
    block = min(256, rows)
    count = rows // block
    widths = [units, 2 * units]

    def row(n):
        return pl.BlockSpec((block, n), lambda i: (i, 0))

    return pl.pallas_call(
        functools.partial(hidden_kernel, min(256, units), count),
        grid=(2 * count,),
        in_specs=pieces_spec(block, width, count)
        + pieces_spec(block, width, count)
        + [pl.BlockSpec(w.shape, lambda i: (0, 0), pipeline_mode=pl.Buffered(1))],
        out_specs=[row(n) for n in widths] + 2 * pieces_spec(block, width, count),
        out_shape=[jax.ShapeDtypeStruct((2 * rows, n), bf16) for n in widths]
        + [jax.ShapeDtypeStruct((rows, width), bf16)] * 4,
        compiler_params=pltpu.CompilerParams(
            vmem_limit_bytes=40 * 2**20, dimension_semantics=("arbitrary",)
        ),
        cost_estimate=light,
        name="hidden",
    )(*a, *dy, w)


def product_kernel(dims, parts, *refs):
    x = refs[0][...]
    if parts > 1:
        x = jnp.concatenate([ref[...] for ref in refs[:parts]], 1)
    p = lax.dot_general(x, refs[parts][...], dims, preferred_element_type=f32)
    out_ref = refs[-1]
    for ref in refs[parts + 1 : -1]:
        p = p + ref[...].astype(f32)
    out_ref[...] = p.astype(out_ref.dtype)


def product(parts, rows, w, dims, kind=bf16, columns=None, add=None):
    block = min(256, rows)
    columns = columns or (0, w.shape[1])
    wide = columns[1]
    out = w.shape[0] if dims == cols_both else wide
    row = pl.BlockSpec((block, out), lambda i: (i, 0))
    extra = [] if add is None else [add]
    return pl.pallas_call(
        functools.partial(product_kernel, dims, len(parts)),
        grid=(rows // block,),
        in_specs=[
            pl.BlockSpec((block, x.shape[1]), lambda i, first=first: (first // block + i, 0))
            for x, first in parts
        ]
        + [pl.BlockSpec((w.shape[0], wide), lambda i: (0, columns[0]))]
        + [row] * len(extra),
        out_specs=row,
        out_shape=jax.ShapeDtypeStruct((rows, out), kind),
        compiler_params=pltpu.CompilerParams(
            vmem_limit_bytes=40 * 2**20, dimension_semantics=("arbitrary",)
        ),
        cost_estimate=light,
        name="product",
    )(*[x for x, _ in parts], *in_hbm(w), *extra)


def wgrad_kernel(counts, *refs):
    out_ref = refs[-1]
    j = pl.program_id(0)
    first = 0
    refs = refs[:-1]
    for pieces, blocks in counts:
        lefts, rights, refs = refs[:pieces], refs[pieces : 2 * pieces], refs[2 * pieces :]

        @pl.when((j >= first) & (j < first + blocks))
        def _():
            total = None
            for a, b in zip(lefts, rights):
                p = lax.dot_general(a[...], b[...], rows_both, preferred_element_type=f32)
                total = p if total is None else total + p
            out_ref[...] = total.astype(bf16)

        first += blocks


def wgrad(groups, rows):
    width = groups[0][0][0].shape[1]
    block = min([512] + [group[0][2].shape[1] for group in groups])
    counts, specs, args = [], [], []
    first = 0
    for group in groups:
        blocks = group[0][2].shape[1] // block
        counts.append((len(group), blocks))
        for a, at, _, _ in group:
            specs.append(
                pl.BlockSpec(
                    (rows, width), lambda j, at=at: (at, 0), pipeline_mode=pl.Buffered(1)
                )
            )
            args.append(a)
        for _, _, b, at in group:

            def spot(j, at=at, first=first, blocks=blocks):
                return (at, jnp.clip(j - first, 0, blocks - 1))

            specs.append(pl.BlockSpec((rows, block), spot))
            args.append(b)
        first += blocks
    return pl.pallas_call(
        functools.partial(wgrad_kernel, counts),
        grid=(first,),
        in_specs=specs,
        out_specs=pl.BlockSpec((width, block), lambda j: (0, j)),
        out_shape=jax.ShapeDtypeStruct((width, first * block), bf16),
        compiler_params=pltpu.CompilerParams(
            vmem_limit_bytes=40 * 2**20, dimension_semantics=("arbitrary",)
        ),
        cost_estimate=light,
        name="wgrad",
    )(*args)


def row_pass(body, name, inputs, whole, kinds):
    width = inputs[0][0].shape[1]
    rows = min(a.shape[0] - first for a, first in inputs)
    block = min(256, rows)

    def kernel(*refs):
        count = len(inputs) + len(whole)
        values = [ref[...].astype(f32) for ref in refs[:count]]
        for ref, value in zip(refs[count:], body(*values)):
            ref[...] = value.astype(ref.dtype)

    return pl.pallas_call(
        kernel,
        grid=(rows // block,),
        in_specs=[
            pl.BlockSpec((block, width), lambda i, first=first: (first // block + i, 0))
            for _, first in inputs
        ]
        + [pl.BlockSpec(a.shape, lambda i: (0, 0)) for a in whole],
        out_specs=[pl.BlockSpec((block, width), lambda i: (i, 0)) for _ in kinds],
        out_shape=[jax.ShapeDtypeStruct((rows, width), kind) for kind in kinds],
        compiler_params=pltpu.CompilerParams(dimension_semantics=("arbitrary",)),
        cost_estimate=light,
        name=name,
    )(*[a for a, _ in inputs], *whole)


def inverse_root(x):
    return lax.rsqrt(jnp.mean(x * x, -1, keepdims=True) + epsilon)


def add_rows(*items):
    return (sum_steps(items[0], items[1:]),)


def norm_forward(stream, *rest):
    *terms, gain = rest
    middle = sum_steps(stream, terms)
    return middle, middle * inverse_root(middle) * gain


def norm_back(residual, values, *rest):
    *terms, gain = rest
    root = inverse_root(values)
    scaled = sum_steps(terms[0], terms[1:]) * gain
    out = (
        residual
        + root * scaled
        - values * root**3 * jnp.mean(scaled * values, -1, keepdims=True)
    )
    return out, out


def pad_heads(w):
    half = HEAD_SIZE // 2
    parts = w.reshape(w.shape[0], -1, half)
    return jnp.pad(parts, ((0, 0), (0, 0), (0, LANES // 2 - half))).reshape(w.shape[0], -1)


def cut_heads(w):
    half = HEAD_SIZE // 2
    parts = w.reshape(w.shape[0], -1, LANES // 2)
    return parts[:, :, :half].reshape(w.shape[0], -1)


swap_two = [(0, 1), (1, 0)]
cross_pairs = [(1, 2), (2, 1)]
slant_pairs = [(2 * c + zh, 2 * zh + (1 - c)) for c in range(2) for zh in range(2)]
slant_back = [(b, a) for a, b in slant_pairs]


def stays():
    return lax.axis_index("c") == lax.axis_index("zh")


def cross(a):
    return lax.ppermute(a, ("c", "zh"), cross_pairs)


def other_core(a):
    return lax.ppermute(a, "c", swap_two)


def from_neighbour(a, k, ring):
    return lax.ppermute(a, "zl", [(i, (i - k) % ring) for i in range(ring)])


def both_cores(a):
    return jnp.concatenate([a, other_core(a)], 0)


def spread_pair(w):
    return w, cross(w), lax.ppermute(w, ("c", "zh"), slant_pairs)


def arrange(own, crossed, slanted):
    first = lax.axis_index("zh") == 0
    straight = jnp.where(stays(), own, crossed)
    return jnp.concatenate(
        [jnp.where(first, straight, slanted), jnp.where(first, slanted, straight)], 0
    )


def gather_rows(w):
    return lax.all_gather(w, "d", axis=0, tiled=True)


def send_blocks(part):
    rows = part.shape[0] // 2
    first = lax.axis_index("zh") == 0
    upper, lower = part[:rows], part[rows:]
    straight = jnp.where(first, upper, lower)
    slanted = lax.ppermute(jnp.where(first, lower, upper), ("c", "zh"), slant_back)
    return straight, cross(straight), slanted


def add_blocks(blocks):
    straight, crossed, slanted = blocks
    return jnp.where(stays(), straight, crossed).astype(f32) + slanted.astype(f32)


def sum_rows(grad):
    return lax.psum_scatter(grad, "d", scatter_dimension=0, tiled=True)


def together(*items):
    return lax.optimization_barrier(items)


def mark_kernel(*refs):
    refs[-1][...] = jnp.zeros_like(refs[-1])


def mark(arrays, before, long):
    whole = pl.BlockSpec(before.shape, lambda: (0, 0))
    cost = pl.CostEstimate(flops=1 + long * 10**9, bytes_accessed=1, transcendentals=0)
    return pl.pallas_call(
        mark_kernel,
        in_specs=[pl.BlockSpec(memory_space=pl.ANY)] * len(arrays) + [whole],
        out_specs=whole,
        out_shape=jax.ShapeDtypeStruct(before.shape, before.dtype),
        cost_estimate=cost,
        name="mark",
    )(*arrays, before)


def dot(a, b):
    return jnp.dot(a, b, preferred_element_type=f32)


def dot_cols(a, b):
    return lax.dot_general(a, b, cols_both, preferred_element_type=f32)


def dot_rows(a, b):
    return lax.dot_general(a, b, rows_both, preferred_element_type=f32)


def sum_steps(first, second):
    out = first
    for item in second:
        out = out + item
    return out


def per_device(
    ring,
    tokens,
    positions,
    norm1_gain,
    w_query,
    key_weight,
    value_weight,
    w_out,
    norm2_gain,
    w_gate,
    w_up,
    w_down,
    cotangent,
):
    steps = range(ring)
    core = lax.axis_index("c")
    column = lax.axis_index("zl")
    place = jnp.stack([core, column, lax.axis_index("zh")]).astype(jnp.int32)
    rows = tokens.shape[0]
    length = 2 * ring * rows
    marks = [jnp.zeros((8, LANES), f32)]

    def order(first, then, long=0):
        marks[0], then = together(mark(first, marks[0], long), then)
        return then

    def swap_chips(own):
        return [from_neighbour(own, k, ring) for k in steps[1:]]

    def join_cores(partial, kind=bf16):
        theirs = other_core(partial(rows, bf16, None))
        return partial(0, kind, theirs)

    def join(mine, theirs):
        return row_pass(add_rows, "join", [(mine, 0), (theirs, 0)], [], [bf16])[0]

    def split_cores(partial):
        return [partial(0, bf16, None), other_core(partial(rows, bf16, None))]

    def send_chips(joined):
        return [
            lax.ppermute(p.astype(bf16), "zl", [(i, (i + k) % ring) for i in steps])
            for k, p in zip(steps[1:], joined)
        ]

    def pairs_of(kept, k):
        out = []
        for c in range(2):
            for zh in range(2):
                if (c == zh) == kept:
                    base = (2 * c + zh) * ring
                    out += [(base + i, base + (i - k) % ring) for i in steps]
        return out

    def cross_tokens(a):
        pairs = []
        for c, zh in ((0, 1), (1, 0)):
            pairs += [
                ((2 * c + zh) * ring + i, (2 * zh + c) * ring + ring - 1 - i) for i in steps
            ]
        return lax.ppermute(a, ("c", "zh", "zl"), pairs)

    def early_neighbours(original):
        return [
            lax.ppermute(original, ("c", "zh", "zl"), pairs_of(True, k)) for k in steps if k
        ]

    def late_neighbours(moved):
        return [lax.ppermute(moved, ("c", "zh", "zl"), pairs_of(False, k)) for k in steps[1:]]

    def choose(early, late):
        return [jnp.where(stays(), e, l) for e, l in zip(early, late)]

    qcols, kcols = w_query.shape[1], key_weight.shape[1]
    qw = qcols // HEAD_SIZE * LANES
    kw = kcols // HEAD_SIZE * LANES
    half = HEAD_SIZE // 2
    attn_shard = pad_heads(jnp.concatenate([w_query, key_weight, value_weight, w_out], 1))
    attn_shard = jnp.concatenate(
        [
            attn_shard[:, :half],
            norm1_gain[:, None],
            norm2_gain[:, None],
            attn_shard[:, half + 2 :],
        ],
        1,
    )
    other_positions = other_core(positions)
    attn_pair = spread_pair(attn_shard)
    cot_early = early_neighbours(cotangent)
    attn_pair, cot_early, tokens, other_positions = together(
        attn_pair, cot_early, tokens, other_positions
    )
    places = jnp.where(stays(), positions, other_positions).reshape(2 * ring, rows)
    attn_rows = arrange(*attn_pair)
    attn_full = gather_rows(attn_rows)
    stream_raw = cross_tokens(tokens)
    tokens_early = early_neighbours(tokens)

    blocks = [global_block(l, place, ring) for l in range(2 * ring)]
    ordered = [lax.dynamic_index_in_dim(places, g, 0, keepdims=False) for g in blocks]
    start = jnp.concatenate(
        [g * rows + jnp.arange(rows, dtype=jnp.int32) - o for g, o in zip(blocks, ordered)]
    )[None, :]
    spots = jnp.concatenate(ordered).astype(f32)
    inverse = rope_base ** (-(2.0 / HEAD_SIZE) * jnp.arange(half, dtype=f32))
    angles = spots[:, None] * inverse[None, :]
    gap = jnp.zeros((length, LANES // 2 - half), f32)
    cos_half, sin_half = jnp.cos(angles), jnp.sin(angles)
    cos = jnp.concatenate([cos_half, gap, cos_half, gap], 1)
    sin = jnp.concatenate([-sin_half, gap, sin_half, gap], 1)

    ff_cols = jnp.concatenate([w_gate, w_up, w_down], 1)
    cos, sin, start, stream_raw, tokens_early, ff_cols = together(
        cos, sin, start, stream_raw, tokens_early, ff_cols
    )
    stream_own = jnp.where(stays(), tokens, stream_raw)
    tokens_late = late_neighbours(stream_raw)
    ff_pair = spread_pair(ff_cols)

    out_columns = ((qw + 2 * kw) // qw, qw)
    qkv_columns = (0, qw + 2 * kw)
    gain_first = attn_full[:, half].astype(f32)[None, :]
    gain_second = attn_full[:, half + 1].astype(f32)[None, :]

    projected = project(
        (stream_own, other_core(stream_own)), gain_first, attn_full, cos, sin, qw, kw, 0, ()
    )
    tokens_late, ff_pair, projected, cot_sent = together(
        tokens_late, ff_pair, projected, cotangent
    )
    others = [(x, other_core(x)) for x in choose(tokens_early, tokens_late)]
    ff_rows = arrange(*ff_pair)
    ff_full = gather_rows(ff_rows)
    cot_raw = cross_tokens(cot_sent)
    others, projected = order([others[0][1], ff_rows], (others, projected), 8)
    for k, pair in enumerate(others, 1):
        projected = project(pair, gain_first, attn_full, cos, sin, qw, kw, k, projected)
    normed_first, q, k, v = projected

    def out_product(o):
        return lambda first, kind, add: product(
            [(o, first)], rows, attn_full, cols_both, kind, out_columns, add
        )

    def whole_rows(*arrays):
        return [(a, 0) for a in arrays]

    attended = [attend(i, place, q, k, v, start, ring) for i in steps[1:]]
    attended, cot_raw = together(attended, cot_raw)
    joined = [join_cores(out_product(o)) for o, _ in attended]
    sent = send_chips(joined)
    q, k, v = order(joined, (q, k, v), 8)
    attended.insert(0, attend(0, place, q, k, v, start, ring))
    out_own = split_cores(out_product(attended[0][0]))
    sent, out_own[0] = together(sent, out_own[0])
    middle, normed_second = row_pass(
        norm_forward,
        "norm_forward",
        whole_rows(stream_own, *out_own, *sent),
        [gain_second],
        [f32, bf16],
    )
    normed_second, cot_raw = together(normed_second, cot_raw)
    cot_own = jnp.where(stays(), cotangent, cot_raw)
    ff_others = swap_chips(normed_second)
    cot_late = late_neighbours(cot_raw)
    ff_in = [(normed_second, other_core(normed_second))]
    out_grads = [(cot_own, other_core(cot_own))]
    ff_in, out_grads = order([normed_second], (ff_in, out_grads), 8)
    hidden = [hidden_pass(ff_in[0], out_grads[0], ff_full)]
    hidden, ff_others, cot_late = together(hidden, ff_others, cot_late)

    second_own = [hidden[0][2], other_core(hidden[0][3])]
    mixed_own = [hidden[0][4], other_core(hidden[0][5])]
    for a, dy in zip(ff_others, choose(cot_early, cot_late)):
        a, dy = (a, other_core(a)), (dy, other_core(dy))
        ff_in.append(a)
        out_grads.append(dy)
        hidden.append(hidden_pass(a, dy, ff_full))

    def pieces(pairs, hidden, i):
        return [(a, 0, h[i], j) for pair, h in zip(pairs, hidden) for j, a in enumerate(pair)]

    joined = [join(h[2], other_core(h[3])) for h in hidden[1:]]
    sent = send_chips(joined)
    mixed_halves = [(h[4], other_core(h[5])) for h in hidden[1:]]
    hidden, mixed_halves = order(joined, (hidden, mixed_halves), 8)
    mixed_joined = [join(*pair) for pair in mixed_halves]
    ff_wgrad = wgrad([pieces(ff_in, hidden, 1), pieces(out_grads, hidden, 0)], rows)
    sent, mixed_joined, ff_wgrad = order([ff_wgrad], (sent, mixed_joined, ff_wgrad))
    ff_part = sum_rows(ff_wgrad)
    middle_grad, db = row_pass(
        norm_back,
        "norm_back",
        whole_rows(cot_own, middle, *second_own, *sent),
        [gain_second],
        [f32, bf16],
    )
    branch_others = swap_chips(db)
    branch = [(db, other_core(db))]
    branch = order([db], branch, 8)

    def heads_grad(pair):
        return jnp.concatenate(
            [product([(b, 0)], rows, attn_full, plain, columns=out_columns) for b in pair], 0
        )

    def queries_back(i, do, before):
        o, lse = attended[i]
        return attend_back(i, place, q, k, v, o, do, lse, start, cos, sin, ring, before)

    dq, *dkv = queries_back(0, heads_grad(branch[0]), ())
    dqs = [dq]
    branch_others, mixed_joined, dqs, dkv = together(branch_others, mixed_joined, dqs, dkv)
    mixed_sent = send_chips(mixed_joined)
    branch += order(
        [branch_others[0]], [(b, other_core(b)) for b in branch_others], True
    )
    for i in steps[1:]:
        dq, *dkv = queries_back(i, heads_grad(branch[i]), tuple(dkv))
        dqs.append(dq)
    mixed_sent, dqs, dkv = together(mixed_sent, dqs, dkv)
    mixed = row_pass(add_rows, "mixed", whole_rows(middle, *mixed_own, *mixed_sent), [], [bf16])[0]
    mixed_raw = cross_tokens(mixed)

    def first_product(i, dqs, dkv):
        base = 2 * rows * i
        return lambda first, kind, add: product(
            [(dqs[i], first)] + [(d, base + first) for d in dkv],
            rows,
            attn_full,
            cols_both,
            kind,
            qkv_columns,
            add,
        )

    joined = [join_cores(first_product(i, dqs, dkv)) for i in steps[1:]]
    sent = send_chips(joined)
    ff_blocks = send_blocks(ff_part)
    dqs, dkv = order([*joined, mixed, ff_blocks[0]], (dqs, dkv), 8)
    first_own = split_cores(first_product(0, dqs, dkv))
    attn_wgrad = wgrad(
        [[(normed_first, 2 * i + j, dqs[i], j) for i in steps for j in range(2)]]
        + [[(normed_first, i, d, i) for i in range(2 * ring)] for d in dkv]
        + [[(branch[i][j], 0, attended[i][0], j) for i in steps for j in range(2)]],
        rows,
    )
    attn_part = sum_rows(attn_wgrad)
    sent, mixed_raw, ff_blocks, first_own[0] = order(
        [attn_wgrad], (sent, mixed_raw, ff_blocks, first_own[0])
    )

    input_grad = row_pass(
        norm_back,
        "norm_back",
        whole_rows(middle_grad, stream_own, *first_own, *sent),
        [gain_first],
        [bf16, bf16],
    )[0]
    input_raw = cross_tokens(input_grad)
    attn_part, mixed_raw, ff_blocks = order([input_grad], (attn_part, mixed_raw, ff_blocks), 400)
    attn_blocks = send_blocks(attn_part)
    attn_part = order([attn_part, attn_blocks[0]], attn_part, 8)
    mixed = jnp.where(stays(), mixed, mixed_raw)
    grad_ff = add_blocks(ff_blocks)
    units = w_gate.shape[1]
    grad_gate, grad_up, grad_down = (grad_ff[:, units * i : units * (i + 1)] for i in range(3))

    def weighed(weights, part, width):
        product = weights[:, :width].astype(f32) * part[:, :width].astype(f32)
        return jnp.sum(product, 1).reshape(2, -1)

    gain_parts = jnp.stack(
        [weighed(attn_rows, attn_part, qw + 2 * kw), weighed(ff_rows, ff_part, 2 * units)]
    )
    gain_parts = jnp.where(core == 0, gain_parts, gain_parts[:, ::-1])
    gain_parts = gain_parts[:, 0] + other_core(gain_parts[:, 1]) + marks[0][0, 0]
    count = 2 * ring
    gain_grads = sum_steps(
        gain_parts,
        [
            lax.ppermute(gain_parts, ("zh", "zl"), [(i, (i + j) % count) for i in range(count)])
            for j in range(1, count)
        ],
    )
    gain_grads, input_raw, attn_blocks = together(gain_grads, input_raw, attn_blocks)
    input_grad = jnp.where(stays(), input_grad, input_raw).astype(f32)
    grad_attn = cut_heads(add_blocks(attn_blocks))
    grad_query = grad_attn[:, :qcols]
    grad_key = grad_attn[:, qcols : qcols + kcols]
    grad_value = grad_attn[:, qcols + kcols : qcols + 2 * kcols]
    grad_output = grad_attn[:, qcols + 2 * kcols :]
    return (
        mixed,
        input_grad,
        gain_grads[0] / norm1_gain.astype(f32),
        grad_query,
        grad_key,
        grad_value,
        grad_output,
        gain_grads[1] / norm2_gain.astype(f32),
        grad_gate,
        grad_up,
        grad_down,
    )


def solution(mesh):
    dp, tensor = mesh.devices.shape
    ring = tensor // 2
    regrouped = Mesh(mesh.devices.reshape(dp // 2, 2, 2, ring), ("d", "c", "zh", "zl"))
    data, parts = ("d", "c"), ("zh", "zl")
    tokens_spec = P(data + parts, None)
    weight_spec = P(data, parts)
    in_specs = (
        tokens_spec,
        P(data),
        P(data),
        weight_spec,
        weight_spec,
        weight_spec,
        weight_spec,
        P(data),
        weight_spec,
        weight_spec,
        weight_spec,
        tokens_spec,
    )
    out_specs = (
        tokens_spec,
        tokens_spec,
        P(data),
        weight_spec,
        weight_spec,
        weight_spec,
        weight_spec,
        P(data),
        weight_spec,
        weight_spec,
        weight_spec,
    )
    return jax.shard_map(
        functools.partial(per_device, ring),
        mesh=regrouped,
        in_specs=in_specs,
        out_specs=out_specs,
        check_vma=False,
    )
```

```python
import functools
import math

import jax
import jax.numpy as jnp
from jax import lax
from jax.experimental import pallas as pl
from jax.experimental.pallas import tpu as pltpu
from jax.sharding import Mesh
from jax.sharding import PartitionSpec as P

HEAD_SIZE = 96
SEQUENCE_LENGTH = 2048
LANES = 128

epsilon = 1e-05
rope_base = 100000.0
masked_score = -1e30
query_scale = math.log2(math.e) * HEAD_SIZE ** (-0.5)
rows_both = (((0,), (0,)), ((), ()))
cols_both = (((1,), (1,)), ((), ()))
plain = (((1,), (0,)), ((), ()))
f32 = jnp.float32
light = pl.CostEstimate(flops=1, bytes_accessed=1, transcendentals=0)
heavy = pl.CostEstimate(flops=8 * 10**9, bytes_accessed=1, transcendentals=0)
unread = pl.BlockSpec(memory_space=pl.ANY)
bf16 = jnp.bfloat16


def flipped(core, column, place, ring):
    return jnp.where(core == place[2], column, ring - 1 - column)


def local_block(g, place, ring):
    core = g // ring
    column = flipped(core, lax.rem(g, ring), place, ring)
    step = lax.rem(column - place[1] + ring, ring)
    return 2 * step + lax.rem(core + place[0], 2)


def global_block(l, place, ring):
    core = lax.rem(lax.rem(l, 2) + place[0], 2)
    column = lax.rem(l // 2 + place[1], ring)
    return core * ring + flipped(core, column, place, ring)


def in_hbm(*arrays):
    return [pltpu.with_memory_space_constraint(a, pltpu.HBM) for a in arrays]


def attend_kernel(ring, block, chip, place_ref, q_ref, k_ref, v_ref, start_ref, *refs):
    o_ref, lse_ref = refs[-2:]
    g = global_block(2 * chip + pl.program_id(1), place_ref, ring)
    share = q_ref.shape[1] // LANES
    start = start_ref[...]
    row = lax.broadcasted_iota(jnp.int32, (block, block), 0)
    col = lax.broadcasted_iota(jnp.int32, (block, block), 1)
    queries = [q_ref[:, h * LANES : (h + 1) * LANES] for h in range(share)]

    def step(kb, carry, diagonal):
        offset = pl.multiple_of(local_block(kb, place_ref, ring) * block, block)
        keys = k_ref[pl.ds(offset, block), :]
        values = v_ref[pl.ds(offset, block), :]
        shown = row >= start - kb * block
        if diagonal:
            shown = shown & (row <= col)
        out = []
        for h in range(share):
            largest, total, acc = carry[h]
            s = lax.dot_general(keys, queries[h], cols_both, preferred_element_type=f32)
            s = jnp.where(shown, s, masked_score)
            newest = jnp.maximum(largest, jnp.max(s, 0, keepdims=True))
            fade = jnp.exp2(largest - newest)
            p = jnp.exp2(s - newest)
            total = total * fade + jnp.sum(p, 0, keepdims=True)
            acc = acc * fade + lax.dot_general(
                values, p.astype(bf16), rows_both, preferred_element_type=f32
            )
            out.append((newest, total, acc))
        return tuple(out)

    carry = tuple(
        (
            jnp.full((1, block), masked_score, f32),
            jnp.zeros((1, block), f32),
            jnp.zeros((LANES, block), f32),
        )
        for _ in range(share)
    )
    carry = step(g, carry, True)
    carry = lax.fori_loop(0, g, lambda kb, c: step(kb, c, False), carry)
    for h in range(share):
        largest, total, acc = carry[h]
        o_ref[:, h * LANES : (h + 1) * LANES] = jnp.transpose(acc / total).astype(bf16)
        lse_ref[0, h : h + 1, :] = largest + jnp.log2(total)


def attend(chip, place, q, k, v, start, ring, first=()):
    length = q.shape[0]
    block = length // (2 * ring)
    kv = k.shape[1] // LANES
    share = q.shape[1] // k.shape[1]
    return pl.pallas_call(
        functools.partial(attend_kernel, ring, block, chip),
        grid_spec=pltpu.PrefetchScalarGridSpec(
            num_scalar_prefetch=1,
            grid=(kv, 2),
            in_specs=[
                pl.BlockSpec((block, share * LANES), lambda h, j, z: (2 * chip + j, h)),
                pl.BlockSpec((length, LANES), lambda h, j, z: (0, h)),
                pl.BlockSpec((length, LANES), lambda h, j, z: (0, h)),
                pl.BlockSpec((1, block), lambda h, j, z: (0, 2 * chip + j)),
            ]
            + [unread] * len(first),
            out_specs=[
                pl.BlockSpec((block, share * LANES), lambda h, j, z: (j, h)),
                pl.BlockSpec((1, share, block), lambda h, j, z: (h, 0, j)),
            ],
        ),
        out_shape=[
            jax.ShapeDtypeStruct((2 * block, q.shape[1]), bf16),
            jax.ShapeDtypeStruct((kv, share, 2 * block), f32),
        ],
        compiler_params=pltpu.CompilerParams(
            vmem_limit_bytes=40 * 2**20, dimension_semantics=("arbitrary", "arbitrary")
        ),
        cost_estimate=heavy if first else light,
        name="attend",
    )(place, q, k, v, start, *first)


def attend_back_kernel(
    ring,
    block,
    chip,
    final,
    place_ref,
    q_ref,
    k_ref,
    v_ref,
    o_ref,
    do_ref,
    lse_ref,
    start_ref,
    cosq_ref,
    sinq_ref,
    *refs,
):
    if final:
        cosk_ref, sink_ref = refs[:2]
    before = refs[2 * final : -5]
    dq_ref, dk_ref, dv_ref, dk_acc, dv_acc = refs[-5:]
    j = pl.program_id(1)
    g = global_block(2 * chip + j, place_ref, ring)
    share = q_ref.shape[1] // LANES

    @pl.when(j == 0)
    def _():
        if before:
            dk_acc[...] = before[0][...]
            dv_acc[...] = before[1][...]
        else:
            dk_acc[...] = jnp.zeros_like(dk_acc)
            dv_acc[...] = jnp.zeros_like(dv_acc)

    start = start_ref[...]
    row = lax.broadcasted_iota(jnp.int32, (block, block), 0)
    col = lax.broadcasted_iota(jnp.int32, (block, block), 1)
    heads = [slice(h * LANES, (h + 1) * LANES) for h in range(share)]
    queries = [q_ref[:, h] for h in heads]
    grads = [do_ref[:, h] for h in heads]
    lses = [lse_ref[0, h : h + 1, :] for h in range(share)]
    inner = [
        jnp.sum(
            jnp.transpose(do_ref[:, h].astype(f32) * o_ref[:, h].astype(f32)), 0, keepdims=True
        )
        for h in heads
    ]

    def step(kb, carry, diagonal):
        offset = pl.multiple_of(local_block(kb, place_ref, ring) * block, block)
        keys = k_ref[pl.ds(offset, block), :]
        values = v_ref[pl.ds(offset, block), :]
        shown = row >= start - kb * block
        if diagonal:
            shown = shown & (row <= col)
        out = []
        dk = jnp.zeros((block, LANES), f32)
        dv = jnp.zeros((block, LANES), f32)
        for h in range(share):
            s = lax.dot_general(keys, queries[h], cols_both, preferred_element_type=f32)
            p = jnp.where(shown, jnp.exp2(s - lses[h]), 0.0)
            dp = lax.dot_general(values, grads[h], cols_both, preferred_element_type=f32)
            ds = (p * (dp - inner[h])).astype(bf16)
            dv += jnp.dot(p.astype(bf16), grads[h], preferred_element_type=f32)
            dk += jnp.dot(ds, queries[h], preferred_element_type=f32)
            out.append(carry[h] + lax.dot_general(keys, ds, rows_both, preferred_element_type=f32))
        dk_acc[pl.ds(offset, block), :] += dk
        dv_acc[pl.ds(offset, block), :] += dv
        return tuple(out)

    carry = step(g, tuple(jnp.zeros((LANES, block), f32) for _ in range(share)), True)
    carry = lax.fori_loop(0, g, lambda kb, c: step(kb, c, False), carry)
    for h in range(share):
        u = jnp.transpose(carry[h]) * HEAD_SIZE ** (-0.5)
        turned = u * cosq_ref[...] - pltpu.roll(u, LANES // 2, 1) * sinq_ref[...]
        dq_ref[:, heads[h]] = turned.astype(bf16)

    @pl.when(j == 1)
    def _():
        def finish(i, _):
            r = pl.ds(pl.multiple_of(i * block, block), block)
            u = dk_acc[r, :]
            if final:
                u = u * math.log(2.0)
                u = u * cosk_ref[r, :] - pltpu.roll(u, LANES // 2, 1) * sink_ref[r, :]
            dk_ref[r, :] = u.astype(dk_ref.dtype)
            dv_ref[r, :] = dv_acc[r, :].astype(dv_ref.dtype)
            return 0

        lax.fori_loop(0, 2 * ring, finish, 0)


def attend_back(chip, place, q, k, v, o, do, lse, start, cos, sin, ring, before):
    length = q.shape[0]
    block = length // (2 * ring)
    kv = k.shape[1] // LANES
    share = q.shape[1] // k.shape[1]
    final = chip == ring - 1
    kind = bf16 if final else f32
    qspec = pl.BlockSpec((block, share * LANES), lambda h, j, z: (2 * chip + j, h))
    own = pl.BlockSpec((block, share * LANES), lambda h, j, z: (j, h))
    kspec = pl.BlockSpec((length, LANES), lambda h, j, z: (0, h))
    table = pl.BlockSpec((block, LANES), lambda h, j, z: (2 * chip + j, 0))
    whole = pl.BlockSpec((length, LANES), lambda h, j, z: (0, 0))
    return pl.pallas_call(
        functools.partial(attend_back_kernel, ring, block, chip, final),
        grid_spec=pltpu.PrefetchScalarGridSpec(
            num_scalar_prefetch=1,
            grid=(kv, 2),
            in_specs=[
                qspec,
                kspec,
                kspec,
                own,
                own,
                pl.BlockSpec((1, share, block), lambda h, j, z: (h, 0, j)),
                pl.BlockSpec((1, block), lambda h, j, z: (0, 2 * chip + j)),
                table,
                table,
            ]
            + [whole, whole] * final
            + [kspec] * len(before),
            out_specs=[own, kspec, kspec],
            scratch_shapes=[pltpu.VMEM((length, LANES), f32), pltpu.VMEM((length, LANES), f32)],
        ),
        out_shape=[
            jax.ShapeDtypeStruct((2 * block, q.shape[1]), bf16),
            jax.ShapeDtypeStruct(k.shape, kind),
            jax.ShapeDtypeStruct(k.shape, kind),
        ],
        compiler_params=pltpu.CompilerParams(
            vmem_limit_bytes=40 * 2**20, dimension_semantics=("arbitrary", "arbitrary")
        ),
        cost_estimate=light,
        name="attend_back",
    )(place, q, k, v, o, do, lse, start, cos, sin, *[cos, sin] * final, *before)


def pieces_spec(block, width, count):
    return [
        pl.BlockSpec((block, width), lambda i: (jnp.minimum(i, count - 1), 0)),
        pl.BlockSpec((block, width), lambda i: (jnp.maximum(i - count, 0), 0)),
    ]


def picked(count, first_ref, second_ref):
    return jnp.where(pl.program_id(0) < count, first_ref[...], second_ref[...])


def project_kernel(
    widths, count, x_ref, y_ref, gain_ref, w_ref, cos_ref, sin_ref, *refs
):
    a_ref, q_ref, k_ref, v_ref = refs[-4:]
    x = picked(count, x_ref, y_ref).astype(f32)
    root = lax.rsqrt(jnp.mean(x * x, -1, keepdims=True) + epsilon)
    a = (x * root * gain_ref[...]).astype(bf16)
    a_ref[...] = a
    cos = cos_ref[...]
    sin = sin_ref[...]
    whole = jnp.dot(a, w_ref[...], preferred_element_type=f32)
    qw, kw = widths
    for h in range((qw + kw) // LANES):
        u = whole[:, h * LANES : (h + 1) * LANES]
        turned = u * cos + pltpu.roll(u, LANES // 2, 1) * sin
        if h < qw // LANES:
            q_ref[:, h * LANES : (h + 1) * LANES] = (turned * query_scale).astype(bf16)
        else:
            j = h - qw // LANES
            k_ref[:, j * LANES : (j + 1) * LANES] = turned.astype(bf16)
    v_ref[...] = whole[:, qw + kw :].astype(bf16)


def project(pair, gain, w, cos, sin, qw, kw, step, before, first=()):
    rows, width = pair[0].shape
    length = cos.shape[0]
    block = min(256, rows)
    count = rows // block
    base = step * 2 * count
    widths = (width, qw, kw, kw)

    def row(n):
        return pl.BlockSpec((block, n), lambda i: (base + i, 0))

    def whole(shape):
        return pl.BlockSpec(shape, lambda i: (0, 0))

    return pl.pallas_call(
        functools.partial(project_kernel, (qw, kw), count),
        grid=(2 * count,),
        in_specs=pieces_spec(block, width, count)
        + [whole(gain.shape), whole((width, qw + 2 * kw)), row(LANES), row(LANES)]
        + [unread] * (len(before) + len(first)),
        out_specs=[row(n) for n in widths],
        out_shape=[jax.ShapeDtypeStruct((length, n), bf16) for n in widths],
        input_output_aliases={6 + i: i for i in range(len(before))},
        compiler_params=pltpu.CompilerParams(
            vmem_limit_bytes=40 * 2**20, dimension_semantics=("arbitrary",)
        ),
        cost_estimate=heavy if first else light,
        name="project",
    )(*in_hbm(*pair), gain, *in_hbm(w), cos, sin, *in_hbm(*before), *first)


def hidden_kernel(
    chunk, count, a_ref, b_ref, dy_ref, dz_ref, w_ref, hid_ref, dgu_ref, *refs
):
    a = picked(count, a_ref, b_ref)
    dy = picked(count, dy_ref, dz_ref)
    units = hid_ref.shape[1]
    for j in range(units // chunk):
        at = slice(j * chunk, (j + 1) * chunk)
        up = slice(units + j * chunk, units + (j + 1) * chunk)
        down = slice(2 * units + j * chunk, 2 * units + (j + 1) * chunk)
        g = jnp.dot(a, w_ref[:, at], preferred_element_type=f32)
        u = jnp.dot(a, w_ref[:, up], preferred_element_type=f32)
        dh = jnp.dot(dy, w_ref[:, down], preferred_element_type=f32)
        sig = jax.nn.sigmoid(g)
        silu = g * sig
        hid_ref[:, at] = (silu * u).astype(bf16)
        dgu_ref[:, at] = (dh * u * (sig + silu * (1.0 - sig))).astype(bf16)
        dgu_ref[:, up] = (dh * silu).astype(bf16)
    da = lax.dot_general(
        dgu_ref[...], w_ref[:, : 2 * units], cols_both, preferred_element_type=f32
    ).astype(bf16)
    mixed = lax.dot_general(
        hid_ref[...], w_ref[:, 2 * units :], cols_both, preferred_element_type=f32
    ).astype(bf16)
    mine = pl.program_id(0) < count

    @pl.when(mine)
    def _():
        refs[0][...] = da
        refs[2][...] = mixed

    @pl.when(jnp.logical_not(mine))
    def _():
        refs[1][...] = da
        refs[3][...] = mixed


def hidden_pass(a, dy, w):
    rows, width = a[0].shape
    units = w.shape[1] // 3
    block = min(256, rows)
    count = rows // block
    widths = [units, 2 * units]

    def row(n):
        return pl.BlockSpec((block, n), lambda i: (i, 0))

    return pl.pallas_call(
        functools.partial(hidden_kernel, min(256, units), count),
        grid=(2 * count,),
        in_specs=pieces_spec(block, width, count)
        + pieces_spec(block, width, count)
        + [pl.BlockSpec(w.shape, lambda i: (0, 0), pipeline_mode=pl.Buffered(1))],
        out_specs=[row(n) for n in widths] + 2 * pieces_spec(block, width, count),
        out_shape=[jax.ShapeDtypeStruct((2 * rows, n), bf16) for n in widths]
        + [jax.ShapeDtypeStruct((rows, width), bf16)] * 4,
        compiler_params=pltpu.CompilerParams(
            vmem_limit_bytes=40 * 2**20, dimension_semantics=("arbitrary",)
        ),
        cost_estimate=heavy,
        name="hidden",
    )(*a, *dy, w)


def product_kernel(dims, parts, unused, *refs):
    x = refs[0][...]
    if parts > 1:
        x = jnp.concatenate([ref[...] for ref in refs[:parts]], 1)
    p = lax.dot_general(x, refs[parts][...], dims, preferred_element_type=f32)
    out_ref = refs[-1]
    for ref in refs[parts + 1 + unused : -1]:
        p = p + ref[...].astype(f32)
    out_ref[...] = p.astype(out_ref.dtype)


def product(parts, rows, w, dims, kind=bf16, columns=None, add=None, cost=light, after=()):
    block = min(256, rows)
    columns = columns or (0, w.shape[1])
    wide = columns[1]
    out = w.shape[0] if dims == cols_both else wide
    row = pl.BlockSpec((block, out), lambda i: (i, 0))
    extra = [] if add is None else [add]
    return pl.pallas_call(
        functools.partial(product_kernel, dims, len(parts), len(after)),
        grid=(rows // block,),
        in_specs=[
            pl.BlockSpec((block, x.shape[1]), lambda i, first=first: (first // block + i, 0))
            for x, first in parts
        ]
        + [pl.BlockSpec((w.shape[0], wide), lambda i: (0, columns[0]))]
        + [unread] * len(after)
        + [row] * len(extra),
        out_specs=row,
        out_shape=jax.ShapeDtypeStruct((rows, out), kind),
        compiler_params=pltpu.CompilerParams(
            vmem_limit_bytes=40 * 2**20, dimension_semantics=("arbitrary",)
        ),
        cost_estimate=cost,
        name="product",
    )(*[x for x, _ in parts], *in_hbm(w), *after, *extra)


def wgrad_kernel(counts, *refs):
    out_ref = refs[-1]
    j = pl.program_id(0)
    first = 0
    refs = refs[:-1]
    for pieces, blocks in counts:
        lefts, rights, refs = refs[:pieces], refs[pieces : 2 * pieces], refs[2 * pieces :]

        @pl.when((j >= first) & (j < first + blocks))
        def _():
            total = None
            for a, b in zip(lefts, rights):
                p = lax.dot_general(a[...], b[...], rows_both, preferred_element_type=f32)
                total = p if total is None else total + p
            out_ref[...] = total.astype(bf16)

        first += blocks


def wgrad(groups, rows, first=()):
    width = groups[0][0][0].shape[1]
    block = min([512] + [group[0][2].shape[1] for group in groups])
    counts, specs, args = [], [], []
    column = 0
    for group in groups:
        blocks = group[0][2].shape[1] // block
        counts.append((len(group), blocks))
        for a, at, _, _ in group:
            specs.append(
                pl.BlockSpec(
                    (rows, width), lambda j, at=at: (at, 0), pipeline_mode=pl.Buffered(1)
                )
            )
            args.append(a)
        for _, _, b, at in group:

            def spot(j, at=at, column=column, blocks=blocks):
                return (at, jnp.clip(j - column, 0, blocks - 1))

            specs.append(pl.BlockSpec((rows, block), spot))
            args.append(b)
        column += blocks
    return pl.pallas_call(
        functools.partial(wgrad_kernel, counts),
        grid=(column,),
        in_specs=specs + [unread] * len(first),
        out_specs=pl.BlockSpec((width, block), lambda j: (0, j)),
        out_shape=pltpu.HBM((width, column * block), bf16),
        compiler_params=pltpu.CompilerParams(
            vmem_limit_bytes=40 * 2**20, dimension_semantics=("arbitrary",)
        ),
        cost_estimate=heavy if first else light,
        name="wgrad",
    )(*in_hbm(*args), *first)


def row_pass(body, name, inputs, whole, kinds, after=()):
    width = inputs[0][0].shape[1]
    rows = min(a.shape[0] - first for a, first in inputs)
    block = min(256, rows)

    def kernel(*refs):
        count = len(inputs) + len(whole)
        values = [ref[...].astype(f32) for ref in refs[:count]]
        for ref, value in zip(refs[count + len(after) :], body(*values)):
            ref[...] = value.astype(ref.dtype)

    return pl.pallas_call(
        kernel,
        grid=(rows // block,),
        in_specs=[
            pl.BlockSpec((block, width), lambda i, first=first: (first // block + i, 0))
            for _, first in inputs
        ]
        + [pl.BlockSpec(a.shape, lambda i: (0, 0)) for a in whole]
        + [unread] * len(after),
        out_specs=[pl.BlockSpec((block, width), lambda i: (i, 0)) for _ in kinds],
        out_shape=[jax.ShapeDtypeStruct((rows, width), kind) for kind in kinds],
        compiler_params=pltpu.CompilerParams(dimension_semantics=("arbitrary",)),
        cost_estimate=light,
        name=name,
    )(*[a for a, _ in inputs], *whole, *after)


def inverse_root(x):
    return lax.rsqrt(jnp.mean(x * x, -1, keepdims=True) + epsilon)


def add_rows(*items):
    return (sum_steps(items[0], items[1:]),)


def norm_forward(stream, *rest):
    *terms, gain = rest
    middle = sum_steps(stream, terms)
    return middle, middle * inverse_root(middle) * gain


def norm_back(residual, values, *rest):
    *terms, gain = rest
    root = inverse_root(values)
    scaled = sum_steps(terms[0], terms[1:]) * gain
    mean = jnp.mean(scaled * values, -1, keepdims=True)
    return (residual + root * scaled - values * root**3 * mean,)


def pad_kernel(counts, *refs):
    out_ref = refs[-1]
    gains = refs[-2][...]
    half = HEAD_SIZE // 2
    rows = out_ref.shape[0]
    at = 0
    for ref, heads in zip(refs[:-2], counts):
        w = ref[...]
        for h in range(heads):
            gap = jnp.zeros((rows, LANES // 2 - half), bf16)
            first = w[:, h * HEAD_SIZE : h * HEAD_SIZE + half]
            second = w[:, h * HEAD_SIZE + half : (h + 1) * HEAD_SIZE]
            free = gap if at else jnp.concatenate([gains, gap[:, 2:]], 1)
            out_ref[:, at : at + LANES] = jnp.concatenate([first, free, second, gap], 1)
            at += LANES


def pad_heads(weights, gains):
    counts = [w.shape[1] // HEAD_SIZE for w in weights]
    return pl.pallas_call(
        functools.partial(pad_kernel, counts),
        out_shape=jax.ShapeDtypeStruct((weights[0].shape[0], sum(counts) * LANES), bf16),
        cost_estimate=light,
        name="pad",
    )(*weights, gains)


def cut_kernel(counts, keep_ref, own_ref, crossed_ref, slanted_ref, *out_refs):
    half = HEAD_SIZE // 2
    kept = keep_ref[0] == 1
    at = 0
    for ref, heads in zip(out_refs, counts):
        parts = []
        for _ in range(heads):
            lanes = slice(at, at + LANES)
            w = jnp.where(kept, own_ref[:, lanes], crossed_ref[:, lanes]).astype(f32)
            w = w + slanted_ref[:, lanes].astype(f32)
            parts += [w[:, :half], w[:, LANES // 2 : LANES // 2 + half]]
            at += LANES
        ref[...] = jnp.concatenate(parts, 1)


def cut_heads(blocks, widths):
    counts = [width // HEAD_SIZE for width in widths]
    rows = blocks[0].shape[0]
    keep = stays().astype(jnp.int32).reshape(1)
    return pl.pallas_call(
        functools.partial(cut_kernel, counts),
        in_specs=[pl.BlockSpec(memory_space=pltpu.SMEM)]
        + [pl.BlockSpec(memory_space=pltpu.VMEM)] * 3,
        out_shape=[jax.ShapeDtypeStruct((rows, width), f32) for width in widths],
        cost_estimate=light,
        name="cut",
    )(keep, *blocks)


swap_two = [(0, 1), (1, 0)]
cross_pairs = [(1, 2), (2, 1)]
slant_pairs = [(2 * c + zh, 2 * zh + (1 - c)) for c in range(2) for zh in range(2)]
slant_back = [(b, a) for a, b in slant_pairs]


def stays():
    return lax.axis_index("c") == lax.axis_index("zh")


def cross(a):
    return lax.ppermute(a, ("c", "zh"), cross_pairs)


def other_core(a):
    return lax.ppermute(a, "c", swap_two)


def from_neighbour(a, k, ring):
    return lax.ppermute(a, "zl", [(i, (i - k) % ring) for i in range(ring)])


def both_cores(a):
    return jnp.concatenate([a, other_core(a)], 0)


def spread_pair(w):
    return w, cross(w), lax.ppermute(w, ("c", "zh"), slant_pairs)


def arrange(own, crossed, slanted):
    first = lax.axis_index("zh") == 0
    straight = jnp.where(stays(), own, crossed)
    return jnp.concatenate(
        [jnp.where(first, straight, slanted), jnp.where(first, slanted, straight)], 0
    )


def gather_rows(w):
    return lax.all_gather(w, "d", axis=0, tiled=True)


def send_blocks(part):
    rows = part.shape[0] // 2
    first = lax.axis_index("zh") == 0
    upper, lower = part[:rows], part[rows:]
    straight = jnp.where(first, upper, lower)
    slanted = lax.ppermute(jnp.where(first, lower, upper), ("c", "zh"), slant_back)
    return straight, cross(straight), slanted


def add_blocks(blocks):
    straight, crossed, slanted = blocks
    return jnp.where(stays(), straight, crossed).astype(f32) + slanted.astype(f32)


def sum_rows(grad):
    return lax.psum_scatter(grad, "d", scatter_dimension=0, tiled=True)


def together(*items):
    return lax.optimization_barrier(items)


def mark_kernel(*refs):
    refs[-1][...] = jnp.zeros_like(refs[-1])


def mark(arrays, before, long):
    whole = pl.BlockSpec(before.shape, lambda: (0, 0))
    cost = pl.CostEstimate(flops=1 + long * 10**9, bytes_accessed=1, transcendentals=0)
    return pl.pallas_call(
        mark_kernel,
        in_specs=[pl.BlockSpec(memory_space=pl.ANY)] * len(arrays) + [whole],
        out_specs=whole,
        out_shape=jax.ShapeDtypeStruct(before.shape, before.dtype),
        cost_estimate=cost,
        name="mark",
    )(*arrays, before)


def dot(a, b):
    return jnp.dot(a, b, preferred_element_type=f32)


def dot_cols(a, b):
    return lax.dot_general(a, b, cols_both, preferred_element_type=f32)


def dot_rows(a, b):
    return lax.dot_general(a, b, rows_both, preferred_element_type=f32)


def sum_steps(first, second):
    out = first
    for item in second:
        out = out + item
    return out


def per_device(
    ring,
    tokens,
    positions,
    norm1_gain,
    w_query,
    key_weight,
    value_weight,
    w_out,
    norm2_gain,
    w_gate,
    w_up,
    w_down,
    cotangent,
):
    steps = range(ring)
    core = lax.axis_index("c")
    column = lax.axis_index("zl")
    place = jnp.stack([core, column, lax.axis_index("zh")]).astype(jnp.int32)
    rows = tokens.shape[0]
    length = 2 * ring * rows
    marks = [jnp.zeros((8, LANES), f32)]

    def order(first, then, long=0):
        marks[0], then = together(mark(first, marks[0], long), then)
        return then

    def swap_chips(own):
        return [from_neighbour(own, k, ring) for k in steps[1:]]

    def join_cores(partial, kind=bf16):
        theirs = other_core(partial(rows, bf16, None))
        return partial(0, kind, theirs)

    def join(mine, theirs):
        return row_pass(add_rows, "join", [(mine, 0), (theirs, 0)], [], [bf16])[0]

    def split_cores(partial):
        return [partial(0, bf16, None), other_core(partial(rows, bf16, None))]

    def send_chips(joined):
        return [
            lax.ppermute(p.astype(bf16), "zl", [(i, (i + k) % ring) for i in steps])
            for k, p in zip(steps[1:], joined)
        ]

    def pairs_of(kept, k):
        out = []
        for c in range(2):
            for zh in range(2):
                if (c == zh) == kept:
                    base = (2 * c + zh) * ring
                    out += [(base + i, base + (i - k) % ring) for i in steps]
        return out

    def cross_tokens(a):
        pairs = []
        for c, zh in ((0, 1), (1, 0)):
            pairs += [
                ((2 * c + zh) * ring + i, (2 * zh + c) * ring + ring - 1 - i) for i in steps
            ]
        return lax.ppermute(a, ("c", "zh", "zl"), pairs)

    def home_pairs(k):
        pairs = []
        for c in range(2):
            for zh in range(2):
                for i in steps:
                    at = (i + k) % ring
                    home = (2 * c + zh) * ring + at
                    if c != zh:
                        home = (2 * zh + c) * ring + ring - 1 - at
                    pairs.append(((2 * c + zh) * ring + i, home))
        return pairs

    def early_neighbours(original):
        return [
            lax.ppermute(original, ("c", "zh", "zl"), pairs_of(True, k)) for k in steps if k
        ]

    def late_neighbours(moved):
        return [lax.ppermute(moved, ("c", "zh", "zl"), pairs_of(False, k)) for k in steps[1:]]

    def choose(early, late):
        return [jnp.where(stays(), e, l) for e, l in zip(early, late)]

    qcols, kcols = w_query.shape[1], key_weight.shape[1]
    qw = qcols // HEAD_SIZE * LANES
    kw = kcols // HEAD_SIZE * LANES
    half = HEAD_SIZE // 2
    attn_shard = pad_heads(
        [w_query, key_weight, value_weight, w_out], jnp.stack([norm1_gain, norm2_gain], 1)
    )
    other_positions = other_core(positions)
    attn_pair = spread_pair(attn_shard)
    cot_early = early_neighbours(cotangent)
    attn_pair, cot_early, tokens, other_positions = together(
        attn_pair, cot_early, tokens, other_positions
    )
    places = jnp.where(stays(), positions, other_positions).reshape(2 * ring, rows)
    attn_rows = arrange(*attn_pair)
    attn_full = gather_rows(attn_rows)
    stream_raw = cross_tokens(tokens)
    tokens_early = early_neighbours(tokens)

    blocks = [global_block(l, place, ring) for l in range(2 * ring)]
    ordered = [lax.dynamic_index_in_dim(places, g, 0, keepdims=False) for g in blocks]
    start = jnp.concatenate(
        [g * rows + jnp.arange(rows, dtype=jnp.int32) - o for g, o in zip(blocks, ordered)]
    )[None, :]
    spots = jnp.concatenate(ordered).astype(f32)
    inverse = rope_base ** (-(2.0 / HEAD_SIZE) * jnp.arange(half, dtype=f32))
    angles = spots[:, None] * inverse[None, :]
    gap = jnp.zeros((length, LANES // 2 - half), f32)
    cos_half, sin_half = jnp.cos(angles), jnp.sin(angles)
    cos = jnp.concatenate([cos_half, gap, cos_half, gap], 1)
    sin = jnp.concatenate([-sin_half, gap, sin_half, gap], 1)

    ff_cols = jnp.concatenate([w_gate, w_up, w_down], 1)
    cos, sin, start, stream_raw, tokens_early, ff_cols = together(
        cos, sin, start, stream_raw, tokens_early, ff_cols
    )
    stream_own = jnp.where(stays(), tokens, stream_raw)
    tokens_late = late_neighbours(stream_raw)
    ff_pair = spread_pair(ff_cols)

    out_columns = ((qw + 2 * kw) // qw, qw)
    qkv_columns = (0, qw + 2 * kw)
    gain_first = attn_full[:, half].astype(f32)[None, :]
    gain_second = attn_full[:, half + 1].astype(f32)[None, :]

    projected = project(
        (stream_own, other_core(stream_own)), gain_first, attn_full, cos, sin, qw, kw, 0, ()
    )
    tokens_late, ff_pair, projected, cot_sent = together(
        tokens_late, ff_pair, projected, cotangent
    )
    others = [(x, other_core(x)) for x in choose(tokens_early, tokens_late)]
    ff_rows = arrange(*ff_pair)
    ff_full = gather_rows(ff_rows)
    cot_raw = cross_tokens(cot_sent)
    for k, pair in enumerate(others, 1):
        projected = project(
            pair, gain_first, attn_full, cos, sin, qw, kw, k, projected, (ff_rows,)
        )
    normed_first, q, k, v = projected

    def out_product(o):
        return lambda first, kind, add: product(
            [(o, first)], rows, attn_full, cols_both, kind, out_columns, add
        )

    def whole_rows(*arrays):
        return [(a, 0) for a in arrays]

    attended = [attend(i, place, q, k, v, start, ring) for i in steps[1:]]
    attended, cot_raw = together(attended, cot_raw)
    joined = [join_cores(out_product(o)) for o, _ in attended]
    sent = send_chips(joined)
    cot_late = late_neighbours(cot_raw)
    q, k, v = order(joined, (q, k, v), 8)
    attended.insert(0, attend(0, place, q, k, v, start, ring))
    out_own = split_cores(out_product(attended[0][0]))
    sent, out_own[0], cot_late = together(sent, out_own[0], cot_late)
    middle, normed_second = row_pass(
        norm_forward,
        "norm_forward",
        whole_rows(stream_own, *out_own, *sent),
        [gain_second],
        [bf16, bf16],
    )
    normed_second, cot_raw = together(normed_second, cot_raw)
    cot_own = jnp.where(stays(), cotangent, cot_raw)
    ff_others = swap_chips(normed_second)
    ff_in = [(normed_second, other_core(normed_second))]
    out_grads = [(cot_own, other_core(cot_own))]
    ff_in, out_grads = order([normed_second], (ff_in, out_grads), 8)
    hidden = [hidden_pass(ff_in[0], out_grads[0], ff_full)]
    hidden, ff_others = together(hidden, ff_others)

    second_own = [hidden[0][2], other_core(hidden[0][3])]
    mixed_own = [hidden[0][4], other_core(hidden[0][5])]
    mixed_own = row_pass(add_rows, "mixed", whole_rows(middle, *mixed_own), [], [bf16])[0]
    mixed_raw = cross_tokens(mixed_own)
    for a, dy in zip(ff_others, choose(cot_early, cot_late)):
        a, dy = (a, other_core(a)), (dy, other_core(dy))
        a, dy, second_own, mixed_own = together(a, dy, second_own, mixed_own)
        ff_in.append(a)
        out_grads.append(dy)
        hidden.append(hidden_pass(a, dy, ff_full))

    def pieces(pairs, hidden, i):
        return [(a, 0, h[i], j) for pair, h in zip(pairs, hidden) for j, a in enumerate(pair)]

    hidden, mixed_raw = together(hidden, mixed_raw)
    joined = [join(h[2], other_core(h[3])) for h in hidden[1:]]
    sent = send_chips(joined)
    mixed_halves = [(h[4], other_core(h[5])) for h in hidden[1:]]
    mixed_joined = [join(*pair) for pair in mixed_halves]
    ff_wgrad = wgrad([pieces(ff_in, hidden, 1), pieces(out_grads, hidden, 0)], rows, joined)
    sent, mixed_joined, ff_wgrad = together(sent, mixed_joined, ff_wgrad)
    ff_part = sum_rows(ff_wgrad)
    db = row_pass(
        norm_back,
        "norm_back",
        whole_rows(cot_own, middle, *second_own, *sent),
        [gain_second],
        [bf16],
    )[0]
    branch_others = swap_chips(db)
    branch = [(db, other_core(db))]

    def heads_grad(pair):
        return jnp.concatenate(
            [
                product([(b, 0)], rows, attn_full, plain, columns=out_columns, cost=cost)
                for b, cost in zip(pair, (heavy, light))
            ],
            0,
        )

    def queries_back(i, do, before):
        o, lse = attended[i]
        return attend_back(i, place, q, k, v, o, do, lse, start, cos, sin, ring, before)

    dq, *dkv = queries_back(0, heads_grad(branch[0]), ())
    dqs = [dq]
    branch_others, mixed_joined, dqs, dkv = together(branch_others, mixed_joined, dqs, dkv)
    mixed_others = [
        lax.ppermute(p, ("c", "zh", "zl"), home_pairs(k)) for k, p in zip(steps[1:], mixed_joined)
    ]
    branch += [(b, other_core(b)) for b in branch_others]
    for i in steps[1:]:
        dq, *dkv = queries_back(i, heads_grad(branch[i]), tuple(dkv))
        dqs.append(dq)
    mixed_others, dqs, dkv = together(mixed_others, dqs, dkv)
    def first_product(i, after=()):
        base = 2 * rows * i
        return lambda first, kind, add: product(
            [(dqs[i], first)] + [(d, base + first) for d in dkv],
            rows,
            attn_full,
            cols_both,
            kind,
            qkv_columns,
            add,
            after=after,
        )

    joined = [join_cores(first_product(i)) for i in steps[1:]]
    sent = send_chips(joined)
    ff_blocks = send_blocks(ff_part)
    first_own = split_cores(first_product(0, joined))
    attn_wgrad = wgrad(
        [[(normed_first, 2 * i + j, dqs[i], j) for i in steps for j in range(2)]]
        + [[(normed_first, i, d, i) for i in range(2 * ring)] for d in dkv]
        + [[(branch[i][j], 0, attended[i][0], j) for i in steps for j in range(2)]],
        rows,
        (*joined, ff_blocks[0]),
    )
    attn_part = sum_rows(attn_wgrad)
    sent, ff_blocks, first_own[0] = together(sent, ff_blocks, first_own[0])

    input_grad = row_pass(
        norm_back,
        "norm_back",
        whole_rows(db, stream_own, *first_own, *sent),
        [gain_first],
        [bf16],
        [attn_wgrad],
    )[0]
    input_raw = cross_tokens(input_grad)
    attn_part, ff_blocks, mixed_others = order(
        [input_grad], (attn_part, ff_blocks, mixed_others), 400
    )
    attn_part, input_raw = together(attn_part, input_raw)
    attn_blocks = send_blocks(attn_part)
    attn_part = order([attn_part, attn_blocks[0]], attn_part, 8)
    mixed = jnp.where(stays(), mixed_own, mixed_raw)
    mixed = row_pass(add_rows, "mixed", whole_rows(mixed, *mixed_others), [], [bf16])[0]
    grad_ff = add_blocks(ff_blocks)
    units = w_gate.shape[1]
    grad_gate, grad_up, grad_down = (grad_ff[:, units * i : units * (i + 1)] for i in range(3))
    input_grad = jnp.where(stays(), input_grad, input_raw).astype(f32)

    def weighed(weights, part, width):
        product = weights[:, :width].astype(f32) * part[:, :width].astype(f32)
        return jnp.sum(product, 1).reshape(2, -1)

    gain_parts = jnp.stack(
        [weighed(attn_rows, attn_part, qw + 2 * kw), weighed(ff_rows, ff_part, 2 * units)]
    )
    gain_parts = jnp.where(core == 0, gain_parts, gain_parts[:, ::-1])
    gain_parts = gain_parts[:, 0] + other_core(gain_parts[:, 1]) + marks[0][0, 0]
    count = 2 * ring
    gain_grads = sum_steps(
        gain_parts,
        [
            lax.ppermute(gain_parts, ("zh", "zl"), [(i, (i + j) % count) for i in range(count)])
            for j in range(1, count)
        ],
    )
    gain_first_grad = gain_grads[0] / norm1_gain.astype(f32)
    gain_second_grad = gain_grads[1] / norm2_gain.astype(f32)
    mixed, input_grad, gain_first_grad, gain_second_grad, grad_gate, grad_up, grad_down, attn_blocks = (
        together(
            mixed,
            input_grad,
            gain_first_grad,
            gain_second_grad,
            grad_gate,
            grad_up,
            grad_down,
            attn_blocks,
        )
    )
    grad_query, grad_key, grad_value, grad_output = cut_heads(
        attn_blocks, [qcols, kcols, kcols, qcols]
    )
    return (
        mixed,
        input_grad,
        gain_first_grad,
        grad_query,
        grad_key,
        grad_value,
        grad_output,
        gain_second_grad,
        grad_gate,
        grad_up,
        grad_down,
    )


def solution(mesh):
    dp, tensor = mesh.devices.shape
    ring = tensor // 2
    regrouped = Mesh(mesh.devices.reshape(dp // 2, 2, 2, ring), ("d", "c", "zh", "zl"))
    data, parts = ("d", "c"), ("zh", "zl")
    tokens_spec = P(data + parts, None)
    weight_spec = P(data, parts)
    in_specs = (
        tokens_spec,
        P(data),
        P(data),
        weight_spec,
        weight_spec,
        weight_spec,
        weight_spec,
        P(data),
        weight_spec,
        weight_spec,
        weight_spec,
        tokens_spec,
    )
    out_specs = (
        tokens_spec,
        tokens_spec,
        P(data),
        weight_spec,
        weight_spec,
        weight_spec,
        weight_spec,
        P(data),
        weight_spec,
        weight_spec,
        weight_spec,
    )
    return jax.shard_map(
        functools.partial(per_device, ring),
        mesh=regrouped,
        in_specs=in_specs,
        out_specs=out_specs,
        check_vma=False,
    )
```

```python
import functools
import math

import jax
import jax.numpy as jnp
from jax import lax
from jax.experimental import pallas as pl
from jax.experimental.pallas import tpu as pltpu
from jax.sharding import Mesh
from jax.sharding import PartitionSpec as P

HEAD_SIZE = 96
SEQUENCE_LENGTH = 2048
LANES = 128

epsilon = 1e-05
rope_base = 100000.0
masked_score = -1e30
query_scale = math.log2(math.e) * HEAD_SIZE ** (-0.5)
rows_both = (((0,), (0,)), ((), ()))
cols_both = (((1,), (1,)), ((), ()))
plain = (((1,), (0,)), ((), ()))
f32 = jnp.float32
light = pl.CostEstimate(flops=1, bytes_accessed=1, transcendentals=0)
heavy = pl.CostEstimate(flops=8 * 10**9, bytes_accessed=1, transcendentals=0)
unread = pl.BlockSpec(memory_space=pl.ANY)
bf16 = jnp.bfloat16


def flipped(core, column, place, ring):
    return jnp.where(core == place[2], column, ring - 1 - column)


def local_block(g, place, ring):
    core = g // ring
    column = flipped(core, lax.rem(g, ring), place, ring)
    step = lax.rem(column - place[1] + ring, ring)
    return 2 * step + lax.rem(core + place[0], 2)


def global_block(l, place, ring):
    core = lax.rem(lax.rem(l, 2) + place[0], 2)
    column = lax.rem(l // 2 + place[1], ring)
    return core * ring + flipped(core, column, place, ring)


def in_hbm(*arrays):
    return [pltpu.with_memory_space_constraint(a, pltpu.HBM) for a in arrays]


def attend_kernel(ring, block, chip, place_ref, q_ref, k_ref, v_ref, start_ref, *refs):
    o_ref, lse_ref = refs[-2:]
    g = global_block(2 * chip + pl.program_id(1), place_ref, ring)
    share = q_ref.shape[1] // LANES
    start = start_ref[...]
    row = lax.broadcasted_iota(jnp.int32, (block, block), 0)
    col = lax.broadcasted_iota(jnp.int32, (block, block), 1)
    queries = [q_ref[:, h * LANES : (h + 1) * LANES] for h in range(share)]

    def step(kb, carry, diagonal):
        offset = pl.multiple_of(local_block(kb, place_ref, ring) * block, block)
        keys = k_ref[pl.ds(offset, block), :]
        values = v_ref[pl.ds(offset, block), :]
        shown = row >= start - kb * block
        if diagonal:
            shown = shown & (row <= col)
        out = []
        for h in range(share):
            largest, total, acc = carry[h]
            s = lax.dot_general(keys, queries[h], cols_both, preferred_element_type=f32)
            s = jnp.where(shown, s, masked_score)
            newest = jnp.maximum(largest, jnp.max(s, 0, keepdims=True))
            fade = jnp.exp2(largest - newest)
            p = jnp.exp2(s - newest)
            total = total * fade + jnp.sum(p, 0, keepdims=True)
            acc = acc * fade + lax.dot_general(
                values, p.astype(bf16), rows_both, preferred_element_type=f32
            )
            out.append((newest, total, acc))
        return tuple(out)

    carry = tuple(
        (
            jnp.full((1, block), masked_score, f32),
            jnp.zeros((1, block), f32),
            jnp.zeros((LANES, block), f32),
        )
        for _ in range(share)
    )
    carry = step(g, carry, True)
    carry = lax.fori_loop(0, g, lambda kb, c: step(kb, c, False), carry)
    for h in range(share):
        largest, total, acc = carry[h]
        o_ref[:, h * LANES : (h + 1) * LANES] = jnp.transpose(acc / total).astype(bf16)
        lse_ref[0, h : h + 1, :] = largest + jnp.log2(total)


def attend(chip, place, q, k, v, start, ring, first=()):
    length = q.shape[0]
    block = length // (2 * ring)
    kv = k.shape[1] // LANES
    share = q.shape[1] // k.shape[1]
    return pl.pallas_call(
        functools.partial(attend_kernel, ring, block, chip),
        grid_spec=pltpu.PrefetchScalarGridSpec(
            num_scalar_prefetch=1,
            grid=(kv, 2),
            in_specs=[
                pl.BlockSpec((block, share * LANES), lambda h, j, z: (2 * chip + j, h)),
                pl.BlockSpec((length, LANES), lambda h, j, z: (0, h)),
                pl.BlockSpec((length, LANES), lambda h, j, z: (0, h)),
                pl.BlockSpec((1, block), lambda h, j, z: (0, 2 * chip + j)),
            ]
            + [unread] * len(first),
            out_specs=[
                pl.BlockSpec((block, share * LANES), lambda h, j, z: (j, h)),
                pl.BlockSpec((1, share, block), lambda h, j, z: (h, 0, j)),
            ],
        ),
        out_shape=[
            jax.ShapeDtypeStruct((2 * block, q.shape[1]), bf16),
            jax.ShapeDtypeStruct((kv, share, 2 * block), f32),
        ],
        compiler_params=pltpu.CompilerParams(
            vmem_limit_bytes=40 * 2**20, dimension_semantics=("arbitrary", "arbitrary")
        ),
        cost_estimate=heavy if first else light,
        name="attend",
    )(place, q, k, v, start, *first)


def attend_back_kernel(
    ring,
    block,
    chip,
    final,
    place_ref,
    q_ref,
    k_ref,
    v_ref,
    o_ref,
    do_ref,
    lse_ref,
    start_ref,
    cosq_ref,
    sinq_ref,
    *refs,
):
    if final:
        cosk_ref, sink_ref = refs[:2]
    before = refs[2 * final : -5]
    dq_ref, dk_ref, dv_ref, dk_acc, dv_acc = refs[-5:]
    j = pl.program_id(1)
    g = global_block(2 * chip + j, place_ref, ring)
    share = q_ref.shape[1] // LANES

    @pl.when(j == 0)
    def _():
        if before:
            dk_acc[...] = before[0][...]
            dv_acc[...] = before[1][...]
        else:
            dk_acc[...] = jnp.zeros_like(dk_acc)
            dv_acc[...] = jnp.zeros_like(dv_acc)

    start = start_ref[...]
    row = lax.broadcasted_iota(jnp.int32, (block, block), 0)
    col = lax.broadcasted_iota(jnp.int32, (block, block), 1)
    heads = [slice(h * LANES, (h + 1) * LANES) for h in range(share)]
    queries = [q_ref[:, h] for h in heads]
    grads = [do_ref[:, h] for h in heads]
    lses = [lse_ref[0, h : h + 1, :] for h in range(share)]
    inner = [
        jnp.sum(
            jnp.transpose(do_ref[:, h].astype(f32) * o_ref[:, h].astype(f32)), 0, keepdims=True
        )
        for h in heads
    ]

    def step(kb, carry, diagonal):
        offset = pl.multiple_of(local_block(kb, place_ref, ring) * block, block)
        keys = k_ref[pl.ds(offset, block), :]
        values = v_ref[pl.ds(offset, block), :]
        shown = row >= start - kb * block
        if diagonal:
            shown = shown & (row <= col)
        out = []
        dk = jnp.zeros((block, LANES), f32)
        dv = jnp.zeros((block, LANES), f32)
        for h in range(share):
            s = lax.dot_general(keys, queries[h], cols_both, preferred_element_type=f32)
            p = jnp.where(shown, jnp.exp2(s - lses[h]), 0.0)
            dp = lax.dot_general(values, grads[h], cols_both, preferred_element_type=f32)
            ds = (p * (dp - inner[h])).astype(bf16)
            dv += jnp.dot(p.astype(bf16), grads[h], preferred_element_type=f32)
            dk += jnp.dot(ds, queries[h], preferred_element_type=f32)
            out.append(carry[h] + lax.dot_general(keys, ds, rows_both, preferred_element_type=f32))
        dk_acc[pl.ds(offset, block), :] += dk
        dv_acc[pl.ds(offset, block), :] += dv
        return tuple(out)

    carry = step(g, tuple(jnp.zeros((LANES, block), f32) for _ in range(share)), True)
    carry = lax.fori_loop(0, g, lambda kb, c: step(kb, c, False), carry)
    for h in range(share):
        u = jnp.transpose(carry[h]) * HEAD_SIZE ** (-0.5)
        turned = u * cosq_ref[...] - pltpu.roll(u, LANES // 2, 1) * sinq_ref[...]
        dq_ref[:, heads[h]] = turned.astype(bf16)

    @pl.when(j == 1)
    def _():
        def finish(i, _):
            r = pl.ds(pl.multiple_of(i * block, block), block)
            u = dk_acc[r, :]
            if final:
                u = u * math.log(2.0)
                u = u * cosk_ref[r, :] - pltpu.roll(u, LANES // 2, 1) * sink_ref[r, :]
            dk_ref[r, :] = u.astype(dk_ref.dtype)
            dv_ref[r, :] = dv_acc[r, :].astype(dv_ref.dtype)
            return 0

        lax.fori_loop(0, 2 * ring, finish, 0)


def attend_back(chip, place, q, k, v, o, do, lse, start, cos, sin, ring, before):
    length = q.shape[0]
    block = length // (2 * ring)
    kv = k.shape[1] // LANES
    share = q.shape[1] // k.shape[1]
    final = chip == ring - 1
    kind = bf16 if final else f32
    qspec = pl.BlockSpec((block, share * LANES), lambda h, j, z: (2 * chip + j, h))
    own = pl.BlockSpec((block, share * LANES), lambda h, j, z: (j, h))
    kspec = pl.BlockSpec((length, LANES), lambda h, j, z: (0, h))
    table = pl.BlockSpec((block, LANES), lambda h, j, z: (2 * chip + j, 0))
    whole = pl.BlockSpec((length, LANES), lambda h, j, z: (0, 0))
    return pl.pallas_call(
        functools.partial(attend_back_kernel, ring, block, chip, final),
        grid_spec=pltpu.PrefetchScalarGridSpec(
            num_scalar_prefetch=1,
            grid=(kv, 2),
            in_specs=[
                qspec,
                kspec,
                kspec,
                own,
                own,
                pl.BlockSpec((1, share, block), lambda h, j, z: (h, 0, j)),
                pl.BlockSpec((1, block), lambda h, j, z: (0, 2 * chip + j)),
                table,
                table,
            ]
            + [whole, whole] * final
            + [kspec] * len(before),
            out_specs=[own, kspec, kspec],
            scratch_shapes=[pltpu.VMEM((length, LANES), f32), pltpu.VMEM((length, LANES), f32)],
        ),
        out_shape=[
            jax.ShapeDtypeStruct((2 * block, q.shape[1]), bf16),
            jax.ShapeDtypeStruct(k.shape, kind),
            jax.ShapeDtypeStruct(k.shape, kind),
        ],
        compiler_params=pltpu.CompilerParams(
            vmem_limit_bytes=40 * 2**20, dimension_semantics=("arbitrary", "arbitrary")
        ),
        cost_estimate=light,
        name="attend_back",
    )(place, q, k, v, o, do, lse, start, cos, sin, *[cos, sin] * final, *before)


def pieces_spec(block, width, count):
    return [
        pl.BlockSpec((block, width), lambda i: (jnp.minimum(i, count - 1), 0)),
        pl.BlockSpec((block, width), lambda i: (jnp.maximum(i - count, 0), 0)),
    ]


def picked(count, first_ref, second_ref):
    return jnp.where(pl.program_id(0) < count, first_ref[...], second_ref[...])


def project_kernel(
    widths, count, x_ref, y_ref, gain_ref, w_ref, cos_ref, sin_ref, *refs
):
    a_ref, q_ref, k_ref, v_ref = refs[-4:]
    x = picked(count, x_ref, y_ref).astype(f32)
    root = lax.rsqrt(jnp.mean(x * x, -1, keepdims=True) + epsilon)
    a = (x * root * gain_ref[...]).astype(bf16)
    a_ref[...] = a
    cos = cos_ref[...]
    sin = sin_ref[...]
    whole = jnp.dot(a, w_ref[...], preferred_element_type=f32)
    qw, kw = widths
    for h in range((qw + kw) // LANES):
        u = whole[:, h * LANES : (h + 1) * LANES]
        turned = u * cos + pltpu.roll(u, LANES // 2, 1) * sin
        if h < qw // LANES:
            q_ref[:, h * LANES : (h + 1) * LANES] = (turned * query_scale).astype(bf16)
        else:
            j = h - qw // LANES
            k_ref[:, j * LANES : (j + 1) * LANES] = turned.astype(bf16)
    v_ref[...] = whole[:, qw + kw :].astype(bf16)


def project(pair, gain, w, cos, sin, qw, kw, step, before, first=()):
    rows, width = pair[0].shape
    length = cos.shape[0]
    block = min(256, rows)
    count = rows // block
    base = step * 2 * count
    widths = (width, qw, kw, kw)

    def row(n):
        return pl.BlockSpec((block, n), lambda i: (base + i, 0))

    def whole(shape):
        return pl.BlockSpec(shape, lambda i: (0, 0))

    return pl.pallas_call(
        functools.partial(project_kernel, (qw, kw), count),
        grid=(2 * count,),
        in_specs=pieces_spec(block, width, count)
        + [whole(gain.shape), whole((width, qw + 2 * kw)), row(LANES), row(LANES)]
        + [unread] * (len(before) + len(first)),
        out_specs=[row(n) for n in widths],
        out_shape=[jax.ShapeDtypeStruct((length, n), bf16) for n in widths],
        input_output_aliases={6 + i: i for i in range(len(before))},
        compiler_params=pltpu.CompilerParams(
            vmem_limit_bytes=40 * 2**20, dimension_semantics=("arbitrary",)
        ),
        cost_estimate=heavy if first else light,
        name="project",
    )(*in_hbm(*pair), gain, *in_hbm(w), cos, sin, *in_hbm(*before), *first)


def hidden_kernel(
    chunk, count, a_ref, b_ref, dy_ref, dz_ref, w_ref, hid_ref, dgu_ref, *refs
):
    a = picked(count, a_ref, b_ref)
    dy = picked(count, dy_ref, dz_ref)
    units = hid_ref.shape[1]
    for j in range(units // chunk):
        at = slice(j * chunk, (j + 1) * chunk)
        up = slice(units + j * chunk, units + (j + 1) * chunk)
        down = slice(2 * units + j * chunk, 2 * units + (j + 1) * chunk)
        g = jnp.dot(a, w_ref[:, at], preferred_element_type=f32)
        u = jnp.dot(a, w_ref[:, up], preferred_element_type=f32)
        dh = jnp.dot(dy, w_ref[:, down], preferred_element_type=f32)
        sig = jax.nn.sigmoid(g)
        silu = g * sig
        hid_ref[:, at] = (silu * u).astype(bf16)
        dgu_ref[:, at] = (dh * u * (sig + silu * (1.0 - sig))).astype(bf16)
        dgu_ref[:, up] = (dh * silu).astype(bf16)
    da = lax.dot_general(
        dgu_ref[...], w_ref[:, : 2 * units], cols_both, preferred_element_type=f32
    ).astype(bf16)
    mixed = lax.dot_general(
        hid_ref[...], w_ref[:, 2 * units :], cols_both, preferred_element_type=f32
    ).astype(bf16)
    mine = pl.program_id(0) < count

    @pl.when(mine)
    def _():
        refs[0][...] = da
        refs[2][...] = mixed

    @pl.when(jnp.logical_not(mine))
    def _():
        refs[1][...] = da
        refs[3][...] = mixed


def hidden_pass(a, dy, w):
    rows, width = a[0].shape
    units = w.shape[1] // 3
    block = min(256, rows)
    count = rows // block
    widths = [units, 2 * units]

    def row(n):
        return pl.BlockSpec((block, n), lambda i: (i, 0))

    return pl.pallas_call(
        functools.partial(hidden_kernel, min(256, units), count),
        grid=(2 * count,),
        in_specs=pieces_spec(block, width, count)
        + pieces_spec(block, width, count)
        + [pl.BlockSpec(w.shape, lambda i: (0, 0), pipeline_mode=pl.Buffered(1))],
        out_specs=[row(n) for n in widths] + 2 * pieces_spec(block, width, count),
        out_shape=[jax.ShapeDtypeStruct((2 * rows, n), bf16) for n in widths]
        + [jax.ShapeDtypeStruct((rows, width), bf16)] * 4,
        compiler_params=pltpu.CompilerParams(
            vmem_limit_bytes=40 * 2**20, dimension_semantics=("arbitrary",)
        ),
        cost_estimate=heavy,
        name="hidden",
    )(*a, *dy, w)


def product_kernel(dims, parts, unused, *refs):
    x = refs[0][...]
    if parts > 1:
        x = jnp.concatenate([ref[...] for ref in refs[:parts]], 1)
    p = lax.dot_general(x, refs[parts][...], dims, preferred_element_type=f32)
    out_ref = refs[-1]
    for ref in refs[parts + 1 + unused : -1]:
        p = p + ref[...].astype(f32)
    out_ref[...] = p.astype(out_ref.dtype)


def product(parts, rows, w, dims, kind=bf16, columns=None, add=None, cost=light, after=()):
    block = min(256, rows)
    columns = columns or (0, w.shape[1])
    wide = columns[1]
    out = w.shape[0] if dims == cols_both else wide
    row = pl.BlockSpec((block, out), lambda i: (i, 0))
    extra = [] if add is None else [add]
    return pl.pallas_call(
        functools.partial(product_kernel, dims, len(parts), len(after)),
        grid=(rows // block,),
        in_specs=[
            pl.BlockSpec((block, x.shape[1]), lambda i, first=first: (first // block + i, 0))
            for x, first in parts
        ]
        + [pl.BlockSpec((w.shape[0], wide), lambda i: (0, columns[0]))]
        + [unread] * len(after)
        + [row] * len(extra),
        out_specs=row,
        out_shape=jax.ShapeDtypeStruct((rows, out), kind),
        compiler_params=pltpu.CompilerParams(
            vmem_limit_bytes=40 * 2**20, dimension_semantics=("arbitrary",)
        ),
        cost_estimate=cost,
        name="product",
    )(*[x for x, _ in parts], *in_hbm(w), *after, *extra)


def wgrad_kernel(counts, *refs):
    out_ref = refs[-1]
    j = pl.program_id(0)
    first = 0
    refs = refs[:-1]
    for pieces, blocks in counts:
        lefts, rights, refs = refs[:pieces], refs[pieces : 2 * pieces], refs[2 * pieces :]

        @pl.when((j >= first) & (j < first + blocks))
        def _():
            total = None
            for a, b in zip(lefts, rights):
                p = lax.dot_general(a[...], b[...], rows_both, preferred_element_type=f32)
                total = p if total is None else total + p
            out_ref[...] = total.astype(bf16)

        first += blocks


def wgrad(groups, rows, first=()):
    width = groups[0][0][0].shape[1]
    block = min([512] + [group[0][2].shape[1] for group in groups])
    counts, specs, args = [], [], []
    column = 0
    for group in groups:
        blocks = group[0][2].shape[1] // block
        counts.append((len(group), blocks))
        for a, at, _, _ in group:
            specs.append(
                pl.BlockSpec(
                    (rows, width), lambda j, at=at: (at, 0), pipeline_mode=pl.Buffered(1)
                )
            )
            args.append(a)
        for _, _, b, at in group:

            def spot(j, at=at, column=column, blocks=blocks):
                return (at, jnp.clip(j - column, 0, blocks - 1))

            specs.append(pl.BlockSpec((rows, block), spot))
            args.append(b)
        column += blocks
    return pl.pallas_call(
        functools.partial(wgrad_kernel, counts),
        grid=(column,),
        in_specs=specs + [unread] * len(first),
        out_specs=pl.BlockSpec((width, block), lambda j: (0, j)),
        out_shape=pltpu.HBM((width, column * block), bf16),
        compiler_params=pltpu.CompilerParams(
            vmem_limit_bytes=40 * 2**20, dimension_semantics=("arbitrary",)
        ),
        cost_estimate=heavy if first else light,
        name="wgrad",
    )(*in_hbm(*args), *first)


def row_pass(body, name, inputs, whole, kinds, after=()):
    width = inputs[0][0].shape[1]
    rows = min(a.shape[0] - first for a, first in inputs)
    block = min(256, rows)

    def kernel(*refs):
        count = len(inputs) + len(whole)
        values = [ref[...].astype(f32) for ref in refs[:count]]
        for ref, value in zip(refs[count + len(after) :], body(*values)):
            ref[...] = value.astype(ref.dtype)

    return pl.pallas_call(
        kernel,
        grid=(rows // block,),
        in_specs=[
            pl.BlockSpec((block, width), lambda i, first=first: (first // block + i, 0))
            for _, first in inputs
        ]
        + [pl.BlockSpec(a.shape, lambda i: (0, 0)) for a in whole]
        + [unread] * len(after),
        out_specs=[pl.BlockSpec((block, width), lambda i: (i, 0)) for _ in kinds],
        out_shape=[jax.ShapeDtypeStruct((rows, width), kind) for kind in kinds],
        compiler_params=pltpu.CompilerParams(dimension_semantics=("arbitrary",)),
        cost_estimate=light,
        name=name,
    )(*[a for a, _ in inputs], *whole, *after)


def inverse_root(x):
    return lax.rsqrt(jnp.mean(x * x, -1, keepdims=True) + epsilon)


def add_rows(*items):
    return (sum_steps(items[0], items[1:]),)


def norm_forward(stream, *rest):
    *terms, gain = rest
    middle = sum_steps(stream, terms)
    return middle, middle * inverse_root(middle) * gain


def norm_back(residual, values, *rest):
    *terms, gain = rest
    root = inverse_root(values)
    scaled = sum_steps(terms[0], terms[1:]) * gain
    mean = jnp.mean(scaled * values, -1, keepdims=True)
    return (residual + root * scaled - values * root**3 * mean,)


def pad_kernel(counts, *refs):
    out_ref = refs[-1]
    gains = refs[-2][...]
    half = HEAD_SIZE // 2
    rows = out_ref.shape[0]
    at = 0
    for ref, heads in zip(refs[:-2], counts):
        w = ref[...]
        for h in range(heads):
            gap = jnp.zeros((rows, LANES // 2 - half), bf16)
            first = w[:, h * HEAD_SIZE : h * HEAD_SIZE + half]
            second = w[:, h * HEAD_SIZE + half : (h + 1) * HEAD_SIZE]
            free = gap if at else jnp.concatenate([gains, gap[:, 2:]], 1)
            out_ref[:, at : at + LANES] = jnp.concatenate([first, free, second, gap], 1)
            at += LANES


def pad_heads(weights, gains):
    counts = [w.shape[1] // HEAD_SIZE for w in weights]
    return pl.pallas_call(
        functools.partial(pad_kernel, counts),
        out_shape=jax.ShapeDtypeStruct((weights[0].shape[0], sum(counts) * LANES), bf16),
        cost_estimate=light,
        name="pad",
    )(*weights, gains)


def cut_kernel(counts, keep_ref, own_ref, crossed_ref, slanted_ref, *out_refs):
    half = HEAD_SIZE // 2
    kept = keep_ref[0] == 1
    at = 0
    for ref, heads in zip(out_refs, counts):
        parts = []
        for _ in range(heads):
            lanes = slice(at, at + LANES)
            w = jnp.where(kept, own_ref[:, lanes], crossed_ref[:, lanes]).astype(f32)
            w = w + slanted_ref[:, lanes].astype(f32)
            parts += [w[:, :half], w[:, LANES // 2 : LANES // 2 + half]]
            at += LANES
        ref[...] = jnp.concatenate(parts, 1)


def cut_heads(blocks, widths):
    counts = [width // HEAD_SIZE for width in widths]
    rows = blocks[0].shape[0]
    keep = stays().astype(jnp.int32).reshape(1)
    return pl.pallas_call(
        functools.partial(cut_kernel, counts),
        in_specs=[pl.BlockSpec(memory_space=pltpu.SMEM)]
        + [pl.BlockSpec(memory_space=pltpu.VMEM)] * 3,
        out_shape=[jax.ShapeDtypeStruct((rows, width), f32) for width in widths],
        cost_estimate=light,
        name="cut",
    )(keep, *blocks)


swap_two = [(0, 1), (1, 0)]
cross_pairs = [(1, 2), (2, 1)]
slant_pairs = [(2 * c + zh, 2 * zh + (1 - c)) for c in range(2) for zh in range(2)]
slant_back = [(b, a) for a, b in slant_pairs]


def stays():
    return lax.axis_index("c") == lax.axis_index("zh")


def cross(a):
    return lax.ppermute(a, ("c", "zh"), cross_pairs)


def other_core(a):
    return lax.ppermute(a, "c", swap_two)


def from_neighbour(a, k, ring):
    return lax.ppermute(a, "zl", [(i, (i - k) % ring) for i in range(ring)])


def both_cores(a):
    return jnp.concatenate([a, other_core(a)], 0)


def spread_pair(w):
    return w, cross(w), lax.ppermute(w, ("c", "zh"), slant_pairs)


def arrange(own, crossed, slanted):
    first = lax.axis_index("zh") == 0
    straight = jnp.where(stays(), own, crossed)
    return jnp.concatenate(
        [jnp.where(first, straight, slanted), jnp.where(first, slanted, straight)], 0
    )


def gather_rows(w):
    return lax.all_gather(w, "d", axis=0, tiled=True)


def send_blocks(part):
    rows = part.shape[0] // 2
    first = lax.axis_index("zh") == 0
    upper, lower = part[:rows], part[rows:]
    straight = jnp.where(first, upper, lower)
    slanted = lax.ppermute(jnp.where(first, lower, upper), ("c", "zh"), slant_back)
    return straight, cross(straight), slanted


def add_blocks(blocks):
    straight, crossed, slanted = blocks
    return jnp.where(stays(), straight, crossed).astype(f32) + slanted.astype(f32)


def sum_rows(grad):
    return lax.psum_scatter(grad, "d", scatter_dimension=0, tiled=True)


def together(*items):
    return lax.optimization_barrier(items)


def mark_kernel(*refs):
    refs[-1][...] = jnp.zeros_like(refs[-1])


def mark(arrays, before, long):
    whole = pl.BlockSpec(before.shape, lambda: (0, 0))
    cost = pl.CostEstimate(flops=1 + long * 10**9, bytes_accessed=1, transcendentals=0)
    return pl.pallas_call(
        mark_kernel,
        in_specs=[pl.BlockSpec(memory_space=pl.ANY)] * len(arrays) + [whole],
        out_specs=whole,
        out_shape=jax.ShapeDtypeStruct(before.shape, before.dtype),
        cost_estimate=cost,
        name="mark",
    )(*arrays, before)


def dot(a, b):
    return jnp.dot(a, b, preferred_element_type=f32)


def dot_cols(a, b):
    return lax.dot_general(a, b, cols_both, preferred_element_type=f32)


def dot_rows(a, b):
    return lax.dot_general(a, b, rows_both, preferred_element_type=f32)


def sum_steps(first, second):
    out = first
    for item in second:
        out = out + item
    return out


def per_device(
    ring,
    tokens,
    positions,
    norm1_gain,
    w_query,
    key_weight,
    value_weight,
    w_out,
    norm2_gain,
    w_gate,
    w_up,
    w_down,
    cotangent,
):
    steps = range(ring)
    core = lax.axis_index("c")
    column = lax.axis_index("zl")
    place = jnp.stack([core, column, lax.axis_index("zh")]).astype(jnp.int32)
    rows = tokens.shape[0]
    length = 2 * ring * rows
    marks = [jnp.zeros((8, LANES), f32)]

    def order(first, then, long=0):
        marks[0], then = together(mark(first, marks[0], long), then)
        return then

    def swap_chips(own):
        return [from_neighbour(own, k, ring) for k in steps[1:]]

    def join_cores(partial, kind=bf16):
        theirs = other_core(partial(rows, bf16, None))
        return partial(0, kind, theirs)

    def join(mine, theirs):
        return row_pass(add_rows, "join", [(mine, 0), (theirs, 0)], [], [bf16])[0]

    def split_cores(partial):
        return [partial(0, bf16, None), other_core(partial(rows, bf16, None))]

    def send_chips(joined):
        return [
            lax.ppermute(p.astype(bf16), "zl", [(i, (i + k) % ring) for i in steps])
            for k, p in zip(steps[1:], joined)
        ]

    def pairs_of(kept, k):
        out = []
        for c in range(2):
            for zh in range(2):
                if (c == zh) == kept:
                    base = (2 * c + zh) * ring
                    out += [(base + i, base + (i - k) % ring) for i in steps]
        return out

    def cross_tokens(a):
        pairs = []
        for c, zh in ((0, 1), (1, 0)):
            pairs += [
                ((2 * c + zh) * ring + i, (2 * zh + c) * ring + ring - 1 - i) for i in steps
            ]
        return lax.ppermute(a, ("c", "zh", "zl"), pairs)

    def home_pairs(k):
        pairs = []
        for c in range(2):
            for zh in range(2):
                for i in steps:
                    at = (i + k) % ring
                    home = (2 * c + zh) * ring + at
                    if c != zh:
                        home = (2 * zh + c) * ring + ring - 1 - at
                    pairs.append(((2 * c + zh) * ring + i, home))
        return pairs

    def early_neighbours(original):
        return [
            lax.ppermute(original, ("c", "zh", "zl"), pairs_of(True, k)) for k in steps if k
        ]

    def late_neighbours(moved):
        return [lax.ppermute(moved, ("c", "zh", "zl"), pairs_of(False, k)) for k in steps[1:]]

    def choose(early, late):
        return [jnp.where(stays(), e, l) for e, l in zip(early, late)]

    qcols, kcols = w_query.shape[1], key_weight.shape[1]
    qw = qcols // HEAD_SIZE * LANES
    kw = kcols // HEAD_SIZE * LANES
    half = HEAD_SIZE // 2
    attn_shard = pad_heads(
        [w_query, key_weight, value_weight, w_out], jnp.stack([norm1_gain, norm2_gain], 1)
    )
    other_positions = other_core(positions)
    attn_pair = spread_pair(attn_shard)
    cot_early = early_neighbours(cotangent)
    attn_pair, cot_early, tokens, other_positions = together(
        attn_pair, cot_early, tokens, other_positions
    )
    places = jnp.where(stays(), positions, other_positions).reshape(2 * ring, rows)
    attn_rows = arrange(*attn_pair)
    attn_full = gather_rows(attn_rows)
    stream_raw = cross_tokens(tokens)
    tokens_early = early_neighbours(tokens)

    blocks = [global_block(l, place, ring) for l in range(2 * ring)]
    ordered = [lax.dynamic_index_in_dim(places, g, 0, keepdims=False) for g in blocks]
    start = jnp.concatenate(
        [g * rows + jnp.arange(rows, dtype=jnp.int32) - o for g, o in zip(blocks, ordered)]
    )[None, :]
    spots = jnp.concatenate(ordered).astype(f32)
    inverse = rope_base ** (-(2.0 / HEAD_SIZE) * jnp.arange(half, dtype=f32))
    angles = spots[:, None] * inverse[None, :]
    gap = jnp.zeros((length, LANES // 2 - half), f32)
    cos_half, sin_half = jnp.cos(angles), jnp.sin(angles)
    cos = jnp.concatenate([cos_half, gap, cos_half, gap], 1)
    sin = jnp.concatenate([-sin_half, gap, sin_half, gap], 1)

    ff_cols = jnp.concatenate([w_gate, w_up, w_down], 1)
    cos, sin, start, stream_raw, tokens_early, ff_cols = together(
        cos, sin, start, stream_raw, tokens_early, ff_cols
    )
    stream_own = jnp.where(stays(), tokens, stream_raw)
    tokens_late = late_neighbours(stream_raw)
    ff_pair = spread_pair(ff_cols)

    out_columns = ((qw + 2 * kw) // qw, qw)
    qkv_columns = (0, qw + 2 * kw)
    gain_first = attn_full[:, half].astype(f32)[None, :]
    gain_second = attn_full[:, half + 1].astype(f32)[None, :]

    projected = project(
        (stream_own, other_core(stream_own)), gain_first, attn_full, cos, sin, qw, kw, 0, ()
    )
    tokens_late, ff_pair, projected, cot_sent = together(
        tokens_late, ff_pair, projected, cotangent
    )
    others = [(x, other_core(x)) for x in choose(tokens_early, tokens_late)]
    ff_rows = arrange(*ff_pair)
    ff_full = gather_rows(ff_rows)
    cot_raw = cross_tokens(cot_sent)
    for k, pair in enumerate(others, 1):
        projected = project(
            pair, gain_first, attn_full, cos, sin, qw, kw, k, projected, (ff_rows,)
        )
    normed_first, q, k, v = projected

    def out_product(o):
        return lambda first, kind, add: product(
            [(o, first)], rows, attn_full, cols_both, kind, out_columns, add
        )

    def whole_rows(*arrays):
        return [(a, 0) for a in arrays]

    attended = [attend(i, place, q, k, v, start, ring) for i in steps[1:]]
    attended, cot_raw = together(attended, cot_raw)
    joined = [join_cores(out_product(o)) for o, _ in attended]
    sent = send_chips(joined)
    cot_late = late_neighbours(cot_raw)
    q, k, v = order(joined, (q, k, v), 8)
    attended.insert(0, attend(0, place, q, k, v, start, ring))
    out_own = split_cores(out_product(attended[0][0]))
    sent, out_own[0], cot_late = together(sent, out_own[0], cot_late)
    middle, normed_second = row_pass(
        norm_forward,
        "norm_forward",
        whole_rows(stream_own, *out_own, *sent),
        [gain_second],
        [bf16, bf16],
    )
    normed_second, cot_raw = together(normed_second, cot_raw)
    cot_own = jnp.where(stays(), cotangent, cot_raw)
    ff_others = swap_chips(normed_second)
    ff_in = [(normed_second, other_core(normed_second))]
    out_grads = [(cot_own, other_core(cot_own))]
    ff_in, out_grads = order([normed_second], (ff_in, out_grads), 8)
    hidden = [hidden_pass(ff_in[0], out_grads[0], ff_full)]
    hidden, ff_others = together(hidden, ff_others)

    second_own = [hidden[0][2], other_core(hidden[0][3])]
    mixed_own = [hidden[0][4], other_core(hidden[0][5])]
    mixed_own = row_pass(add_rows, "mixed", whole_rows(middle, *mixed_own), [], [bf16])[0]
    mixed_raw = cross_tokens(mixed_own)
    for a, dy in zip(ff_others, choose(cot_early, cot_late)):
        a, dy = (a, other_core(a)), (dy, other_core(dy))
        a, dy, second_own, mixed_own = together(a, dy, second_own, mixed_own)
        ff_in.append(a)
        out_grads.append(dy)
        hidden.append(hidden_pass(a, dy, ff_full))

    def pieces(pairs, hidden, i):
        return [(a, 0, h[i], j) for pair, h in zip(pairs, hidden) for j, a in enumerate(pair)]

    hidden, mixed_raw = together(hidden, mixed_raw)
    joined = [join(h[2], other_core(h[3])) for h in hidden[1:]]
    sent = send_chips(joined)
    mixed_halves = [(h[4], other_core(h[5])) for h in hidden[1:]]
    mixed_joined = [join(*pair) for pair in mixed_halves]
    ff_wgrad = wgrad([pieces(ff_in, hidden, 1), pieces(out_grads, hidden, 0)], rows, joined)
    sent, mixed_joined, ff_wgrad = together(sent, mixed_joined, ff_wgrad)
    ff_part = sum_rows(ff_wgrad)
    db = row_pass(
        norm_back,
        "norm_back",
        whole_rows(cot_own, middle, *second_own, *sent),
        [gain_second],
        [bf16],
    )[0]
    branch_others = swap_chips(db)
    branch = [(db, other_core(db))]

    def heads_grad(pair):
        return jnp.concatenate(
            [
                product([(b, 0)], rows, attn_full, plain, columns=out_columns, cost=cost)
                for b, cost in zip(pair, (heavy, light))
            ],
            0,
        )

    def queries_back(i, do, before):
        o, lse = attended[i]
        return attend_back(i, place, q, k, v, o, do, lse, start, cos, sin, ring, before)

    dq, *dkv = queries_back(0, heads_grad(branch[0]), ())
    dqs = [dq]
    branch_others, mixed_joined, dqs, dkv = together(branch_others, mixed_joined, dqs, dkv)
    mixed_others = [
        lax.ppermute(p, ("c", "zh", "zl"), home_pairs(k)) for k, p in zip(steps[1:], mixed_joined)
    ]
    branch += [(b, other_core(b)) for b in branch_others]
    for i in steps[1:]:
        dq, *dkv = queries_back(i, heads_grad(branch[i]), tuple(dkv))
        dqs.append(dq)
    mixed_others, dqs, dkv = together(mixed_others, dqs, dkv)
    def first_product(i, after=()):
        base = 2 * rows * i
        return lambda first, kind, add: product(
            [(dqs[i], first)] + [(d, base + first) for d in dkv],
            rows,
            attn_full,
            cols_both,
            kind,
            qkv_columns,
            add,
            after=after,
        )

    joined = [join_cores(first_product(i)) for i in steps[1:]]
    sent = send_chips(joined)
    ff_blocks = send_blocks(ff_part)
    first_own = split_cores(first_product(0, joined))
    attn_wgrad = wgrad(
        [[(normed_first, 2 * i + j, dqs[i], j) for i in steps for j in range(2)]]
        + [[(normed_first, i, d, i) for i in range(2 * ring)] for d in dkv]
        + [[(branch[i][j], 0, attended[i][0], j) for i in steps for j in range(2)]],
        rows,
        (*joined, ff_blocks[0]),
    )
    attn_part = sum_rows(attn_wgrad)
    sent, first_own[0], wgrad_there = together(sent, first_own[0], attn_wgrad)

    input_grad = row_pass(
        norm_back,
        "norm_back",
        whole_rows(db, stream_own, *first_own, *sent),
        [gain_first],
        [bf16],
        [wgrad_there],
    )[0]
    input_raw = cross_tokens(input_grad)
    attn_part, ff_blocks, mixed_others = order(
        [input_grad, *ff_blocks[1:]], (attn_part, ff_blocks, mixed_others), 400
    )
    attn_part, input_raw = together(attn_part, input_raw)
    attn_blocks = send_blocks(attn_part)
    attn_part = order([attn_part, attn_blocks[0]], attn_part, 8)
    mixed = jnp.where(stays(), mixed_own, mixed_raw)
    mixed = row_pass(add_rows, "mixed", whole_rows(mixed, *mixed_others), [], [bf16])[0]
    grad_ff = add_blocks(ff_blocks)
    units = w_gate.shape[1]
    grad_gate, grad_up, grad_down = (grad_ff[:, units * i : units * (i + 1)] for i in range(3))
    input_grad = jnp.where(stays(), input_grad, input_raw).astype(f32)

    def weighed(weights, part, width):
        product = weights[:, :width].astype(f32) * part[:, :width].astype(f32)
        return jnp.sum(product, 1).reshape(2, -1)

    gain_parts = jnp.stack(
        [weighed(attn_rows, attn_part, qw + 2 * kw), weighed(ff_rows, ff_part, 2 * units)]
    )
    gain_parts = jnp.where(core == 0, gain_parts, gain_parts[:, ::-1])
    gain_parts = gain_parts[:, 0] + other_core(gain_parts[:, 1]) + marks[0][0, 0]
    count = 2 * ring
    gain_grads = sum_steps(
        gain_parts,
        [
            lax.ppermute(gain_parts, ("zh", "zl"), [(i, (i + j) % count) for i in range(count)])
            for j in range(1, count)
        ],
    )
    gain_first_grad = gain_grads[0] / norm1_gain.astype(f32)
    gain_second_grad = gain_grads[1] / norm2_gain.astype(f32)
    mixed, input_grad, gain_first_grad, gain_second_grad, grad_gate, grad_up, grad_down, attn_blocks = (
        together(
            mixed,
            input_grad,
            gain_first_grad,
            gain_second_grad,
            grad_gate,
            grad_up,
            grad_down,
            attn_blocks,
        )
    )
    grad_query, grad_key, grad_value, grad_output = cut_heads(
        attn_blocks, [qcols, kcols, kcols, qcols]
    )
    return (
        mixed,
        input_grad,
        gain_first_grad,
        grad_query,
        grad_key,
        grad_value,
        grad_output,
        gain_second_grad,
        grad_gate,
        grad_up,
        grad_down,
    )


def solution(mesh):
    dp, tensor = mesh.devices.shape
    ring = tensor // 2
    regrouped = Mesh(mesh.devices.reshape(dp // 2, 2, 2, ring), ("d", "c", "zh", "zl"))
    data, parts = ("d", "c"), ("zh", "zl")
    tokens_spec = P(data + parts, None)
    weight_spec = P(data, parts)
    in_specs = (
        tokens_spec,
        P(data),
        P(data),
        weight_spec,
        weight_spec,
        weight_spec,
        weight_spec,
        P(data),
        weight_spec,
        weight_spec,
        weight_spec,
        tokens_spec,
    )
    out_specs = (
        tokens_spec,
        tokens_spec,
        P(data),
        weight_spec,
        weight_spec,
        weight_spec,
        weight_spec,
        P(data),
        weight_spec,
        weight_spec,
        weight_spec,
    )
    return jax.shard_map(
        functools.partial(per_device, ring),
        mesh=regrouped,
        in_specs=in_specs,
        out_specs=out_specs,
        check_vma=False,
    )
```

```python
import functools
import math

import jax
import jax.numpy as jnp
from jax import lax
from jax.experimental import pallas as pl
from jax.experimental.pallas import tpu as pltpu
from jax.sharding import Mesh
from jax.sharding import PartitionSpec as P

HEAD_SIZE = 96
SEQUENCE_LENGTH = 2048
LANES = 128

epsilon = 1e-05
rope_base = 100000.0
masked_score = -1e30
query_scale = math.log2(math.e) * HEAD_SIZE ** (-0.5)
rows_both = (((0,), (0,)), ((), ()))
cols_both = (((1,), (1,)), ((), ()))
plain = (((1,), (0,)), ((), ()))
f32 = jnp.float32
light = pl.CostEstimate(flops=1, bytes_accessed=1, transcendentals=0)
heavy = pl.CostEstimate(flops=8 * 10**9, bytes_accessed=1, transcendentals=0)
unread = pl.BlockSpec(memory_space=pl.ANY)
bf16 = jnp.bfloat16


def flipped(core, column, place, ring):
    return jnp.where(core == place[2], column, ring - 1 - column)


def local_block(g, place, ring):
    core = g // ring
    column = flipped(core, lax.rem(g, ring), place, ring)
    step = lax.rem(column - place[1] + ring, ring)
    return 2 * step + lax.rem(core + place[0], 2)


def global_block(l, place, ring):
    core = lax.rem(lax.rem(l, 2) + place[0], 2)
    column = lax.rem(l // 2 + place[1], ring)
    return core * ring + flipped(core, column, place, ring)


def in_hbm(*arrays):
    return [pltpu.with_memory_space_constraint(a, pltpu.HBM) for a in arrays]


def attend_kernel(ring, block, chip, place_ref, q_ref, k_ref, v_ref, start_ref, *refs):
    o_ref, lse_ref = refs[-2:]
    g = global_block(2 * chip + pl.program_id(1), place_ref, ring)
    share = q_ref.shape[1] // LANES
    start = start_ref[...]
    row = lax.broadcasted_iota(jnp.int32, (block, block), 0)
    col = lax.broadcasted_iota(jnp.int32, (block, block), 1)
    queries = [q_ref[:, h * LANES : (h + 1) * LANES] for h in range(share)]

    def step(kb, carry, diagonal):
        offset = pl.multiple_of(local_block(kb, place_ref, ring) * block, block)
        keys = k_ref[pl.ds(offset, block), :]
        values = v_ref[pl.ds(offset, block), :]
        shown = row >= start - kb * block
        if diagonal:
            shown = shown & (row <= col)
        out = []
        for h in range(share):
            largest, total, acc = carry[h]
            s = lax.dot_general(keys, queries[h], cols_both, preferred_element_type=f32)
            s = jnp.where(shown, s, masked_score)
            newest = jnp.maximum(largest, jnp.max(s, 0, keepdims=True))
            fade = jnp.exp2(largest - newest)
            p = jnp.exp2(s - newest)
            total = total * fade + jnp.sum(p, 0, keepdims=True)
            acc = acc * fade + lax.dot_general(
                values, p.astype(bf16), rows_both, preferred_element_type=f32
            )
            out.append((newest, total, acc))
        return tuple(out)

    carry = tuple(
        (
            jnp.full((1, block), masked_score, f32),
            jnp.zeros((1, block), f32),
            jnp.zeros((LANES, block), f32),
        )
        for _ in range(share)
    )
    carry = step(g, carry, True)
    carry = lax.fori_loop(0, g, lambda kb, c: step(kb, c, False), carry)
    for h in range(share):
        largest, total, acc = carry[h]
        o_ref[:, h * LANES : (h + 1) * LANES] = jnp.transpose(acc / total).astype(bf16)
        lse_ref[0, h : h + 1, :] = largest + jnp.log2(total)


def attend(chip, place, q, k, v, start, ring, first=()):
    length = q.shape[0]
    block = length // (2 * ring)
    kv = k.shape[1] // LANES
    share = q.shape[1] // k.shape[1]
    return pl.pallas_call(
        functools.partial(attend_kernel, ring, block, chip),
        grid_spec=pltpu.PrefetchScalarGridSpec(
            num_scalar_prefetch=1,
            grid=(kv, 2),
            in_specs=[
                pl.BlockSpec((block, share * LANES), lambda h, j, z: (2 * chip + j, h)),
                pl.BlockSpec((length, LANES), lambda h, j, z: (0, h)),
                pl.BlockSpec((length, LANES), lambda h, j, z: (0, h)),
                pl.BlockSpec((1, block), lambda h, j, z: (0, 2 * chip + j)),
            ]
            + [unread] * len(first),
            out_specs=[
                pl.BlockSpec((block, share * LANES), lambda h, j, z: (j, h)),
                pl.BlockSpec((1, share, block), lambda h, j, z: (h, 0, j)),
            ],
        ),
        out_shape=[
            jax.ShapeDtypeStruct((2 * block, q.shape[1]), bf16),
            jax.ShapeDtypeStruct((kv, share, 2 * block), f32),
        ],
        compiler_params=pltpu.CompilerParams(
            vmem_limit_bytes=40 * 2**20, dimension_semantics=("arbitrary", "arbitrary")
        ),
        cost_estimate=heavy if first else light,
        name="attend",
    )(place, q, k, v, start, *first)


def attend_back_kernel(
    ring,
    block,
    chip,
    final,
    place_ref,
    q_ref,
    k_ref,
    v_ref,
    o_ref,
    do_ref,
    lse_ref,
    start_ref,
    cosq_ref,
    sinq_ref,
    *refs,
):
    if final:
        cosk_ref, sink_ref = refs[:2]
    before = refs[2 * final : -5]
    dq_ref, dk_ref, dv_ref, dk_acc, dv_acc = refs[-5:]
    j = pl.program_id(1)
    g = global_block(2 * chip + j, place_ref, ring)
    share = q_ref.shape[1] // LANES

    @pl.when(j == 0)
    def _():
        if before:
            dk_acc[...] = before[0][...]
            dv_acc[...] = before[1][...]
        else:
            dk_acc[...] = jnp.zeros_like(dk_acc)
            dv_acc[...] = jnp.zeros_like(dv_acc)

    start = start_ref[...]
    row = lax.broadcasted_iota(jnp.int32, (block, block), 0)
    col = lax.broadcasted_iota(jnp.int32, (block, block), 1)
    heads = [slice(h * LANES, (h + 1) * LANES) for h in range(share)]
    queries = [q_ref[:, h] for h in heads]
    grads = [do_ref[:, h] for h in heads]
    lses = [lse_ref[0, h : h + 1, :] for h in range(share)]
    inner = [
        jnp.sum(
            jnp.transpose(do_ref[:, h].astype(f32) * o_ref[:, h].astype(f32)), 0, keepdims=True
        )
        for h in heads
    ]

    def step(kb, carry, diagonal):
        offset = pl.multiple_of(local_block(kb, place_ref, ring) * block, block)
        keys = k_ref[pl.ds(offset, block), :]
        values = v_ref[pl.ds(offset, block), :]
        shown = row >= start - kb * block
        if diagonal:
            shown = shown & (row <= col)
        out = []
        dk = jnp.zeros((block, LANES), f32)
        dv = jnp.zeros((block, LANES), f32)
        for h in range(share):
            s = lax.dot_general(keys, queries[h], cols_both, preferred_element_type=f32)
            p = jnp.where(shown, jnp.exp2(s - lses[h]), 0.0)
            dp = lax.dot_general(values, grads[h], cols_both, preferred_element_type=f32)
            ds = (p * (dp - inner[h])).astype(bf16)
            dv += jnp.dot(p.astype(bf16), grads[h], preferred_element_type=f32)
            dk += jnp.dot(ds, queries[h], preferred_element_type=f32)
            out.append(carry[h] + lax.dot_general(keys, ds, rows_both, preferred_element_type=f32))
        dk_acc[pl.ds(offset, block), :] += dk
        dv_acc[pl.ds(offset, block), :] += dv
        return tuple(out)

    carry = step(g, tuple(jnp.zeros((LANES, block), f32) for _ in range(share)), True)
    carry = lax.fori_loop(0, g, lambda kb, c: step(kb, c, False), carry)
    for h in range(share):
        u = jnp.transpose(carry[h]) * HEAD_SIZE ** (-0.5)
        turned = u * cosq_ref[...] - pltpu.roll(u, LANES // 2, 1) * sinq_ref[...]
        dq_ref[:, heads[h]] = turned.astype(bf16)

    @pl.when(j == 1)
    def _():
        def finish(i, _):
            r = pl.ds(pl.multiple_of(i * block, block), block)
            u = dk_acc[r, :]
            if final:
                u = u * math.log(2.0)
                u = u * cosk_ref[r, :] - pltpu.roll(u, LANES // 2, 1) * sink_ref[r, :]
            dk_ref[r, :] = u.astype(dk_ref.dtype)
            dv_ref[r, :] = dv_acc[r, :].astype(dv_ref.dtype)
            return 0

        lax.fori_loop(0, 2 * ring, finish, 0)


def attend_back(chip, place, q, k, v, o, do, lse, start, cos, sin, ring, before):
    length = q.shape[0]
    block = length // (2 * ring)
    kv = k.shape[1] // LANES
    share = q.shape[1] // k.shape[1]
    final = chip == ring - 1
    kind = bf16 if final else f32
    qspec = pl.BlockSpec((block, share * LANES), lambda h, j, z: (2 * chip + j, h))
    own = pl.BlockSpec((block, share * LANES), lambda h, j, z: (j, h))
    kspec = pl.BlockSpec((length, LANES), lambda h, j, z: (0, h))
    table = pl.BlockSpec((block, LANES), lambda h, j, z: (2 * chip + j, 0))
    whole = pl.BlockSpec((length, LANES), lambda h, j, z: (0, 0))
    return pl.pallas_call(
        functools.partial(attend_back_kernel, ring, block, chip, final),
        grid_spec=pltpu.PrefetchScalarGridSpec(
            num_scalar_prefetch=1,
            grid=(kv, 2),
            in_specs=[
                qspec,
                kspec,
                kspec,
                own,
                own,
                pl.BlockSpec((1, share, block), lambda h, j, z: (h, 0, j)),
                pl.BlockSpec((1, block), lambda h, j, z: (0, 2 * chip + j)),
                table,
                table,
            ]
            + [whole, whole] * final
            + [kspec] * len(before),
            out_specs=[own, kspec, kspec],
            scratch_shapes=[pltpu.VMEM((length, LANES), f32), pltpu.VMEM((length, LANES), f32)],
        ),
        out_shape=[
            jax.ShapeDtypeStruct((2 * block, q.shape[1]), bf16),
            jax.ShapeDtypeStruct(k.shape, kind),
            jax.ShapeDtypeStruct(k.shape, kind),
        ],
        compiler_params=pltpu.CompilerParams(
            vmem_limit_bytes=40 * 2**20, dimension_semantics=("arbitrary", "arbitrary")
        ),
        cost_estimate=light,
        name="attend_back",
    )(place, q, k, v, o, do, lse, start, cos, sin, *[cos, sin] * final, *before)


def pieces_spec(block, width, count):
    return [
        pl.BlockSpec((block, width), lambda i: (jnp.minimum(i, count - 1), 0)),
        pl.BlockSpec((block, width), lambda i: (jnp.maximum(i - count, 0), 0)),
    ]


def picked(count, first_ref, second_ref):
    return jnp.where(pl.program_id(0) < count, first_ref[...], second_ref[...])


def project_kernel(
    widths, count, x_ref, y_ref, gain_ref, w_ref, cos_ref, sin_ref, *refs
):
    a_ref, q_ref, k_ref, v_ref = refs[-4:]
    x = picked(count, x_ref, y_ref).astype(f32)
    root = lax.rsqrt(jnp.mean(x * x, -1, keepdims=True) + epsilon)
    a = (x * root * gain_ref[...]).astype(bf16)
    a_ref[...] = a
    cos = cos_ref[...]
    sin = sin_ref[...]
    whole = jnp.dot(a, w_ref[...], preferred_element_type=f32)
    qw, kw = widths
    for h in range((qw + kw) // LANES):
        u = whole[:, h * LANES : (h + 1) * LANES]
        turned = u * cos + pltpu.roll(u, LANES // 2, 1) * sin
        if h < qw // LANES:
            q_ref[:, h * LANES : (h + 1) * LANES] = (turned * query_scale).astype(bf16)
        else:
            j = h - qw // LANES
            k_ref[:, j * LANES : (j + 1) * LANES] = turned.astype(bf16)
    v_ref[...] = whole[:, qw + kw :].astype(bf16)


def project(pair, gain, w, cos, sin, qw, kw, step, before, first=()):
    rows, width = pair[0].shape
    length = cos.shape[0]
    block = min(256, rows)
    count = rows // block
    base = step * 2 * count
    widths = (width, qw, kw, kw)

    def row(n):
        return pl.BlockSpec((block, n), lambda i: (base + i, 0))

    def whole(shape):
        return pl.BlockSpec(shape, lambda i: (0, 0))

    return pl.pallas_call(
        functools.partial(project_kernel, (qw, kw), count),
        grid=(2 * count,),
        in_specs=pieces_spec(block, width, count)
        + [whole(gain.shape), whole((width, qw + 2 * kw)), row(LANES), row(LANES)]
        + [unread] * (len(before) + len(first)),
        out_specs=[row(n) for n in widths],
        out_shape=[jax.ShapeDtypeStruct((length, n), bf16) for n in widths],
        input_output_aliases={6 + i: i for i in range(len(before))},
        compiler_params=pltpu.CompilerParams(
            vmem_limit_bytes=40 * 2**20, dimension_semantics=("arbitrary",)
        ),
        cost_estimate=heavy if first else light,
        name="project",
    )(*in_hbm(*pair), gain, *in_hbm(w), cos, sin, *in_hbm(*before), *first)


def hidden_kernel(
    chunk, count, a_ref, b_ref, dy_ref, dz_ref, w_ref, hid_ref, dgu_ref, *refs
):
    a = picked(count, a_ref, b_ref)
    dy = picked(count, dy_ref, dz_ref)
    units = hid_ref.shape[1]
    for j in range(units // chunk):
        at = slice(j * chunk, (j + 1) * chunk)
        up = slice(units + j * chunk, units + (j + 1) * chunk)
        down = slice(2 * units + j * chunk, 2 * units + (j + 1) * chunk)
        g = jnp.dot(a, w_ref[:, at], preferred_element_type=f32)
        u = jnp.dot(a, w_ref[:, up], preferred_element_type=f32)
        dh = jnp.dot(dy, w_ref[:, down], preferred_element_type=f32)
        sig = jax.nn.sigmoid(g)
        silu = g * sig
        hid_ref[:, at] = (silu * u).astype(bf16)
        dgu_ref[:, at] = (dh * u * (sig + silu * (1.0 - sig))).astype(bf16)
        dgu_ref[:, up] = (dh * silu).astype(bf16)
    da = lax.dot_general(
        dgu_ref[...], w_ref[:, : 2 * units], cols_both, preferred_element_type=f32
    ).astype(bf16)
    mixed = lax.dot_general(
        hid_ref[...], w_ref[:, 2 * units :], cols_both, preferred_element_type=f32
    ).astype(bf16)
    mine = pl.program_id(0) < count

    @pl.when(mine)
    def _():
        refs[0][...] = da
        refs[2][...] = mixed

    @pl.when(jnp.logical_not(mine))
    def _():
        refs[1][...] = da
        refs[3][...] = mixed


def hidden_pass(a, dy, w):
    rows, width = a[0].shape
    units = w.shape[1] // 3
    block = min(256, rows)
    count = rows // block
    widths = [units, 2 * units]

    def row(n):
        return pl.BlockSpec((block, n), lambda i: (i, 0))

    return pl.pallas_call(
        functools.partial(hidden_kernel, min(256, units), count),
        grid=(2 * count,),
        in_specs=pieces_spec(block, width, count)
        + pieces_spec(block, width, count)
        + [pl.BlockSpec(w.shape, lambda i: (0, 0), pipeline_mode=pl.Buffered(1))],
        out_specs=[row(n) for n in widths] + 2 * pieces_spec(block, width, count),
        out_shape=[jax.ShapeDtypeStruct((2 * rows, n), bf16) for n in widths]
        + [jax.ShapeDtypeStruct((rows, width), bf16)] * 4,
        compiler_params=pltpu.CompilerParams(
            vmem_limit_bytes=40 * 2**20, dimension_semantics=("arbitrary",)
        ),
        cost_estimate=heavy,
        name="hidden",
    )(*a, *dy, w)


def product_kernel(dims, parts, unused, *refs):
    x = refs[0][...]
    if parts > 1:
        x = jnp.concatenate([ref[...] for ref in refs[:parts]], 1)
    p = lax.dot_general(x, refs[parts][...], dims, preferred_element_type=f32)
    out_ref = refs[-1]
    for ref in refs[parts + 1 + unused : -1]:
        p = p + ref[...].astype(f32)
    out_ref[...] = p.astype(out_ref.dtype)


def product(parts, rows, w, dims, kind=bf16, columns=None, add=None, cost=light, after=()):
    block = min(256, rows)
    columns = columns or (0, w.shape[1])
    wide = columns[1]
    out = w.shape[0] if dims == cols_both else wide
    row = pl.BlockSpec((block, out), lambda i: (i, 0))
    extra = [] if add is None else [add]
    return pl.pallas_call(
        functools.partial(product_kernel, dims, len(parts), len(after)),
        grid=(rows // block,),
        in_specs=[
            pl.BlockSpec((block, x.shape[1]), lambda i, first=first: (first // block + i, 0))
            for x, first in parts
        ]
        + [pl.BlockSpec((w.shape[0], wide), lambda i: (0, columns[0]))]
        + [unread] * len(after)
        + [row] * len(extra),
        out_specs=row,
        out_shape=jax.ShapeDtypeStruct((rows, out), kind),
        compiler_params=pltpu.CompilerParams(
            vmem_limit_bytes=40 * 2**20, dimension_semantics=("arbitrary",)
        ),
        cost_estimate=cost,
        name="product",
    )(*[x for x, _ in parts], *in_hbm(w), *after, *extra)


def without_gaps(w):
    half = HEAD_SIZE // 2
    parts = [w[:, at : at + half] for at in range(0, w.shape[1], LANES // 2)]
    return jnp.concatenate(parts, 1)


def wgrad_kernel(counts, cut, *refs):
    out_ref = refs[-1]
    j = pl.program_id(0)
    first = 0
    for pieces, parts, blocks in counts:
        lefts, refs = refs[:pieces], refs[pieces:]
        rights, refs = refs[: pieces * parts], refs[pieces * parts :]

        @pl.when((j >= first) & (j < first + blocks))
        def _():
            total = None
            for i, a in enumerate(lefts):
                b = [ref[...] for ref in rights[parts * i : parts * (i + 1)]]
                b = b[0] if parts == 1 else jnp.concatenate(b, 1)
                p = lax.dot_general(a[...], b, rows_both, preferred_element_type=f32)
                total = p if total is None else total + p
            total = total.astype(bf16)
            out_ref[...] = without_gaps(total) if cut else total

        first += blocks


def wgrad(groups, rows, block, first=(), cut=False):
    width = groups[0][0][0].shape[1]
    counts, specs, args = [], [], []
    column = 0
    for group in groups:
        parts = len(group[0][2])
        blocks = sum(b.shape[1] for b in group[0][2]) // block
        counts.append((len(group), parts, blocks))
        for a, at, _, _ in group:
            specs.append(
                pl.BlockSpec(
                    (rows, width), lambda j, at=at: (at, 0), pipeline_mode=pl.Buffered(1)
                )
            )
            args.append(a)
        for _, _, sides, at in group:

            def spot(j, at=at, column=column, blocks=blocks):
                return (at, jnp.clip(j - column, 0, blocks - 1))

            for b in sides:
                specs.append(pl.BlockSpec((rows, b.shape[1] if parts > 1 else block), spot))
                args.append(b)
        column += blocks
    wide = block * 3 // 4 if cut else block
    return pl.pallas_call(
        functools.partial(wgrad_kernel, counts, cut),
        grid=(column,),
        in_specs=specs + [unread] * len(first),
        out_specs=pl.BlockSpec((width, wide), lambda j: (0, j)),
        out_shape=pltpu.HBM((width, column * wide), bf16),
        compiler_params=pltpu.CompilerParams(
            vmem_limit_bytes=40 * 2**20, dimension_semantics=("arbitrary",)
        ),
        cost_estimate=heavy if first else light,
        name="wgrad",
    )(*in_hbm(*args), *first)


def row_pass(body, name, inputs, whole, kinds, after=()):
    width = inputs[0][0].shape[1]
    rows = min(a.shape[0] - first for a, first in inputs)
    block = min(256, rows)

    def kernel(*refs):
        count = len(inputs) + len(whole)
        values = [ref[...].astype(f32) for ref in refs[:count]]
        for ref, value in zip(refs[count + len(after) :], body(*values)):
            ref[...] = value.astype(ref.dtype)

    return pl.pallas_call(
        kernel,
        grid=(rows // block,),
        in_specs=[
            pl.BlockSpec((block, width), lambda i, first=first: (first // block + i, 0))
            for _, first in inputs
        ]
        + [pl.BlockSpec(a.shape, lambda i: (0, 0)) for a in whole]
        + [unread] * len(after),
        out_specs=[pl.BlockSpec((block, width), lambda i: (i, 0)) for _ in kinds],
        out_shape=[jax.ShapeDtypeStruct((rows, width), kind) for kind in kinds],
        compiler_params=pltpu.CompilerParams(dimension_semantics=("arbitrary",)),
        cost_estimate=light,
        name=name,
    )(*[a for a, _ in inputs], *whole, *after)


def inverse_root(x):
    return lax.rsqrt(jnp.mean(x * x, -1, keepdims=True) + epsilon)


def add_rows(*items):
    return (sum_steps(items[0], items[1:]),)


def norm_forward(stream, *rest):
    *terms, gain = rest
    middle = sum_steps(stream, terms)
    return middle, middle * inverse_root(middle) * gain


def norm_back(residual, values, *rest):
    *terms, gain = rest
    root = inverse_root(values)
    scaled = sum_steps(terms[0], terms[1:]) * gain
    mean = jnp.mean(scaled * values, -1, keepdims=True)
    return (residual + root * scaled - values * root**3 * mean,)


def pad_kernel(counts, *refs):
    out_ref = refs[-1]
    gains = refs[-2][...]
    half = HEAD_SIZE // 2
    rows = out_ref.shape[0]
    at = 0
    for ref, heads in zip(refs[:-2], counts):
        w = ref[...]
        for h in range(heads):
            gap = jnp.zeros((rows, LANES // 2 - half), bf16)
            first = w[:, h * HEAD_SIZE : h * HEAD_SIZE + half]
            second = w[:, h * HEAD_SIZE + half : (h + 1) * HEAD_SIZE]
            free = gap if at else jnp.concatenate([gains, gap[:, 2:]], 1)
            out_ref[:, at : at + LANES] = jnp.concatenate([first, free, second, gap], 1)
            at += LANES


def pad_heads(weights, gains):
    counts = [w.shape[1] // HEAD_SIZE for w in weights]
    return pl.pallas_call(
        functools.partial(pad_kernel, counts),
        out_shape=jax.ShapeDtypeStruct((weights[0].shape[0], sum(counts) * LANES), bf16),
        cost_estimate=light,
        name="pad",
    )(*weights, gains)


def cut_kernel(widths, padded, keep_ref, own_ref, crossed_ref, slanted_ref, *out_refs):
    kept = keep_ref[0] == 1
    at = 0
    for ref, width in zip(out_refs, widths):
        wide = width // HEAD_SIZE * LANES if padded else width
        lanes = slice(at, at + wide)
        w = jnp.where(kept, own_ref[:, lanes], crossed_ref[:, lanes]).astype(f32)
        w = w + slanted_ref[:, lanes].astype(f32)
        ref[...] = without_gaps(w) if padded else w
        at += wide


def cut_heads(blocks, widths):
    rows, columns = blocks[0].shape
    keep = stays().astype(jnp.int32).reshape(1)
    return pl.pallas_call(
        functools.partial(cut_kernel, widths, columns != sum(widths)),
        in_specs=[pl.BlockSpec(memory_space=pltpu.SMEM)]
        + [pl.BlockSpec(memory_space=pltpu.VMEM)] * 3,
        out_shape=[jax.ShapeDtypeStruct((rows, width), f32) for width in widths],
        cost_estimate=light,
        name="cut",
    )(keep, *blocks)


def cut_rows_kernel(in_ref, out_ref):
    out_ref[...] = without_gaps(in_ref[...])


def cut_rows(w):
    return pl.pallas_call(
        cut_rows_kernel,
        out_shape=jax.ShapeDtypeStruct((w.shape[0], w.shape[1] * 3 // 4), w.dtype),
        cost_estimate=light,
        name="cut_rows",
    )(w)


swap_two = [(0, 1), (1, 0)]
cross_pairs = [(1, 2), (2, 1)]
slant_pairs = [(2 * c + zh, 2 * zh + (1 - c)) for c in range(2) for zh in range(2)]
slant_back = [(b, a) for a, b in slant_pairs]


def stays():
    return lax.axis_index("c") == lax.axis_index("zh")


def cross(a):
    return lax.ppermute(a, ("c", "zh"), cross_pairs)


def other_core(a):
    return lax.ppermute(a, "c", swap_two)


def from_neighbour(a, k, ring):
    return lax.ppermute(a, "zl", [(i, (i - k) % ring) for i in range(ring)])


def both_cores(a):
    return jnp.concatenate([a, other_core(a)], 0)


def spread_pair(w):
    return w, cross(w), lax.ppermute(w, ("c", "zh"), slant_pairs)


def arrange(own, crossed, slanted):
    first = lax.axis_index("zh") == 0
    straight = jnp.where(stays(), own, crossed)
    return jnp.concatenate(
        [jnp.where(first, straight, slanted), jnp.where(first, slanted, straight)], 0
    )


def gather_rows(w):
    return lax.all_gather(w, "d", axis=0, tiled=True)


def send_blocks(part):
    rows = part.shape[0] // 2
    first = lax.axis_index("zh") == 0
    upper, lower = part[:rows], part[rows:]
    straight = jnp.where(first, upper, lower)
    slanted = lax.ppermute(jnp.where(first, lower, upper), ("c", "zh"), slant_back)
    return straight, cross(straight), slanted


def add_blocks(blocks):
    straight, crossed, slanted = blocks
    return jnp.where(stays(), straight, crossed).astype(f32) + slanted.astype(f32)


def sum_rows(grad):
    return lax.psum_scatter(grad, "d", scatter_dimension=0, tiled=True)


def together(*items):
    return lax.optimization_barrier(items)


def mark_kernel(*refs):
    refs[-1][...] = jnp.zeros_like(refs[-1])


def mark(arrays, before, long):
    whole = pl.BlockSpec(before.shape, lambda: (0, 0))
    cost = pl.CostEstimate(flops=1 + long * 10**9, bytes_accessed=1, transcendentals=0)
    return pl.pallas_call(
        mark_kernel,
        in_specs=[pl.BlockSpec(memory_space=pl.ANY)] * len(arrays) + [whole],
        out_specs=whole,
        out_shape=jax.ShapeDtypeStruct(before.shape, before.dtype),
        cost_estimate=cost,
        name="mark",
    )(*arrays, before)


def dot(a, b):
    return jnp.dot(a, b, preferred_element_type=f32)


def dot_cols(a, b):
    return lax.dot_general(a, b, cols_both, preferred_element_type=f32)


def dot_rows(a, b):
    return lax.dot_general(a, b, rows_both, preferred_element_type=f32)


def sum_steps(first, second):
    out = first
    for item in second:
        out = out + item
    return out


def per_device(
    ring,
    tokens,
    positions,
    norm1_gain,
    w_query,
    key_weight,
    value_weight,
    w_out,
    norm2_gain,
    w_gate,
    w_up,
    w_down,
    cotangent,
):
    steps = range(ring)
    core = lax.axis_index("c")
    column = lax.axis_index("zl")
    place = jnp.stack([core, column, lax.axis_index("zh")]).astype(jnp.int32)
    rows = tokens.shape[0]
    length = 2 * ring * rows
    marks = [jnp.zeros((8, LANES), f32)]

    def order(first, then, long=0):
        marks[0], then = together(mark(first, marks[0], long), then)
        return then

    def swap_chips(own):
        return [from_neighbour(own, k, ring) for k in steps[1:]]

    def join_cores(partial, kind=bf16):
        theirs = other_core(partial(rows, bf16, None))
        return partial(0, kind, theirs)

    def join(mine, theirs):
        return row_pass(add_rows, "join", [(mine, 0), (theirs, 0)], [], [bf16])[0]

    def split_cores(partial):
        return [partial(0, bf16, None), other_core(partial(rows, bf16, None))]

    def send_chips(joined):
        return [
            lax.ppermute(p.astype(bf16), "zl", [(i, (i + k) % ring) for i in steps])
            for k, p in zip(steps[1:], joined)
        ]

    def pairs_of(kept, k):
        out = []
        for c in range(2):
            for zh in range(2):
                if (c == zh) == kept:
                    base = (2 * c + zh) * ring
                    out += [(base + i, base + (i - k) % ring) for i in steps]
        return out

    def cross_tokens(a):
        pairs = []
        for c, zh in ((0, 1), (1, 0)):
            pairs += [
                ((2 * c + zh) * ring + i, (2 * zh + c) * ring + ring - 1 - i) for i in steps
            ]
        return lax.ppermute(a, ("c", "zh", "zl"), pairs)

    def home_pairs(k):
        pairs = []
        for c in range(2):
            for zh in range(2):
                for i in steps:
                    at = (i + k) % ring
                    home = (2 * c + zh) * ring + at
                    if c != zh:
                        home = (2 * zh + c) * ring + ring - 1 - at
                    pairs.append(((2 * c + zh) * ring + i, home))
        return pairs

    def early_neighbours(original):
        return [
            lax.ppermute(original, ("c", "zh", "zl"), pairs_of(True, k)) for k in steps if k
        ]

    def late_neighbours(moved):
        return [lax.ppermute(moved, ("c", "zh", "zl"), pairs_of(False, k)) for k in steps[1:]]

    def choose(early, late):
        return [jnp.where(stays(), e, l) for e, l in zip(early, late)]

    qcols, kcols = w_query.shape[1], key_weight.shape[1]
    qw = qcols // HEAD_SIZE * LANES
    kw = kcols // HEAD_SIZE * LANES
    half = HEAD_SIZE // 2
    attn_shard = pad_heads(
        [w_query, key_weight, value_weight, w_out], jnp.stack([norm1_gain, norm2_gain], 1)
    )
    other_positions = other_core(positions)
    attn_pair = spread_pair(attn_shard)
    cot_early = early_neighbours(cotangent)
    attn_pair, cot_early, tokens, other_positions = together(
        attn_pair, cot_early, tokens, other_positions
    )
    places = jnp.where(stays(), positions, other_positions).reshape(2 * ring, rows)
    attn_rows = arrange(*attn_pair)
    attn_full = gather_rows(attn_rows)
    cut = qw * 3 // 4 % LANES == 0
    attn_kept = cut_rows(attn_rows) if cut else attn_rows
    stream_raw = cross_tokens(tokens)
    tokens_early = early_neighbours(tokens)

    blocks = [global_block(l, place, ring) for l in range(2 * ring)]
    ordered = [lax.dynamic_index_in_dim(places, g, 0, keepdims=False) for g in blocks]
    start = jnp.concatenate(
        [g * rows + jnp.arange(rows, dtype=jnp.int32) - o for g, o in zip(blocks, ordered)]
    )[None, :]
    spots = jnp.concatenate(ordered).astype(f32)
    inverse = rope_base ** (-(2.0 / HEAD_SIZE) * jnp.arange(half, dtype=f32))
    angles = spots[:, None] * inverse[None, :]
    gap = jnp.zeros((length, LANES // 2 - half), f32)
    cos_half, sin_half = jnp.cos(angles), jnp.sin(angles)
    cos = jnp.concatenate([cos_half, gap, cos_half, gap], 1)
    sin = jnp.concatenate([-sin_half, gap, sin_half, gap], 1)

    ff_cols = jnp.concatenate([w_gate, w_up, w_down], 1)
    cos, sin, start, stream_raw, tokens_early, ff_cols, attn_kept = together(
        cos, sin, start, stream_raw, tokens_early, ff_cols, attn_kept
    )
    stream_own = jnp.where(stays(), tokens, stream_raw)
    tokens_late = late_neighbours(stream_raw)
    ff_pair = spread_pair(ff_cols)

    out_columns = ((qw + 2 * kw) // qw, qw)
    qkv_columns = (0, qw + 2 * kw)
    gain_first = attn_full[:, half].astype(f32)[None, :]
    gain_second = attn_full[:, half + 1].astype(f32)[None, :]

    projected = project(
        (stream_own, other_core(stream_own)), gain_first, attn_full, cos, sin, qw, kw, 0, ()
    )
    tokens_late, ff_pair, projected, cot_sent = together(
        tokens_late, ff_pair, projected, cotangent
    )
    others = [(x, other_core(x)) for x in choose(tokens_early, tokens_late)]
    ff_rows = arrange(*ff_pair)
    ff_full = gather_rows(ff_rows)
    cot_raw = cross_tokens(cot_sent)
    for k, pair in enumerate(others, 1):
        projected = project(
            pair, gain_first, attn_full, cos, sin, qw, kw, k, projected, (ff_rows,)
        )
    normed_first, q, k, v = projected

    def out_product(o):
        return lambda first, kind, add: product(
            [(o, first)], rows, attn_full, cols_both, kind, out_columns, add
        )

    def whole_rows(*arrays):
        return [(a, 0) for a in arrays]

    attended = [attend(i, place, q, k, v, start, ring) for i in steps[1:]]
    attended, cot_raw = together(attended, cot_raw)
    joined = [join_cores(out_product(o)) for o, _ in attended]
    sent = send_chips(joined)
    cot_late = late_neighbours(cot_raw)
    q, k, v = order(joined, (q, k, v), 8)
    attended.insert(0, attend(0, place, q, k, v, start, ring))
    out_own = split_cores(out_product(attended[0][0]))
    sent, out_own[0], cot_late = together(sent, out_own[0], cot_late)
    middle, normed_second = row_pass(
        norm_forward,
        "norm_forward",
        whole_rows(stream_own, *out_own, *sent),
        [gain_second],
        [bf16, bf16],
    )
    normed_second, cot_raw = together(normed_second, cot_raw)
    cot_own = jnp.where(stays(), cotangent, cot_raw)
    ff_others = swap_chips(normed_second)
    ff_in = [(normed_second, other_core(normed_second))]
    out_grads = [(cot_own, other_core(cot_own))]
    ff_in, out_grads = order([normed_second], (ff_in, out_grads), 8)
    hidden = [hidden_pass(ff_in[0], out_grads[0], ff_full)]
    hidden, ff_others = together(hidden, ff_others)

    second_own = [hidden[0][2], other_core(hidden[0][3])]
    mixed_own = [hidden[0][4], other_core(hidden[0][5])]
    mixed_own = row_pass(add_rows, "mixed", whole_rows(middle, *mixed_own), [], [bf16])[0]
    mixed_raw = cross_tokens(mixed_own)
    for a, dy in zip(ff_others, choose(cot_early, cot_late)):
        a, dy = (a, other_core(a)), (dy, other_core(dy))
        a, dy, second_own, mixed_own = together(a, dy, second_own, mixed_own)
        ff_in.append(a)
        out_grads.append(dy)
        hidden.append(hidden_pass(a, dy, ff_full))

    def pieces(pairs, hidden, i):
        return [(a, 0, (h[i],), j) for pair, h in zip(pairs, hidden) for j, a in enumerate(pair)]

    hidden, mixed_raw = together(hidden, mixed_raw)
    joined = [join(h[2], other_core(h[3])) for h in hidden[1:]]
    sent = send_chips(joined)
    mixed_halves = [(h[4], other_core(h[5])) for h in hidden[1:]]
    mixed_joined = [join(*pair) for pair in mixed_halves]
    ff_wgrad = wgrad(
        [pieces(ff_in, hidden, 1), pieces(out_grads, hidden, 0)],
        rows,
        min(512, w_down.shape[1]),
        joined,
    )
    sent, mixed_joined, ff_wgrad = together(sent, mixed_joined, ff_wgrad)
    ff_part = sum_rows(ff_wgrad)
    db = row_pass(
        norm_back,
        "norm_back",
        whole_rows(cot_own, middle, *second_own, *sent),
        [gain_second],
        [bf16],
    )[0]
    branch_others = swap_chips(db)
    branch = [(db, other_core(db))]

    def heads_grad(pair):
        return jnp.concatenate(
            [
                product([(b, 0)], rows, attn_full, plain, columns=out_columns, cost=cost)
                for b, cost in zip(pair, (heavy, light))
            ],
            0,
        )

    def queries_back(i, do, before):
        o, lse = attended[i]
        return attend_back(i, place, q, k, v, o, do, lse, start, cos, sin, ring, before)

    dq, *dkv = queries_back(0, heads_grad(branch[0]), ())
    dqs = [dq]
    branch_others, mixed_joined, dqs, dkv = together(branch_others, mixed_joined, dqs, dkv)
    mixed_others = [
        lax.ppermute(p, ("c", "zh", "zl"), home_pairs(k)) for k, p in zip(steps[1:], mixed_joined)
    ]
    branch += [(b, other_core(b)) for b in branch_others]
    for i in steps[1:]:
        dq, *dkv = queries_back(i, heads_grad(branch[i]), tuple(dkv))
        dqs.append(dq)
    mixed_others, dqs, dkv = together(mixed_others, dqs, dkv)
    def first_product(i, after=()):
        base = 2 * rows * i
        return lambda first, kind, add: product(
            [(dqs[i], first)] + [(d, base + first) for d in dkv],
            rows,
            attn_full,
            cols_both,
            kind,
            qkv_columns,
            add,
            after=after,
        )

    joined = [join_cores(first_product(i)) for i in steps[1:]]
    sent = send_chips(joined)
    ff_blocks = send_blocks(ff_part)
    first_own = split_cores(first_product(0, joined))
    attn_wgrad = wgrad(
        [
            [(normed_first, 2 * i + j, (dqs[i],), j) for i in steps for j in range(2)],
            [(normed_first, i, tuple(dkv), i) for i in range(2 * ring)],
            [(branch[i][j], 0, (attended[i][0],), j) for i in steps for j in range(2)],
        ],
        rows,
        qw,
        (*joined, ff_blocks[0]),
        cut,
    )
    attn_part = sum_rows(attn_wgrad)
    sent, first_own[0], wgrad_there = together(sent, first_own[0], attn_wgrad)

    input_grad = row_pass(
        norm_back,
        "norm_back",
        whole_rows(db, stream_own, *first_own, *sent),
        [gain_first],
        [bf16],
        [wgrad_there],
    )[0]
    input_raw = cross_tokens(input_grad)
    attn_part, ff_blocks, mixed_others = order(
        [input_grad, *ff_blocks[1:]], (attn_part, ff_blocks, mixed_others), 400
    )
    attn_part, input_raw = together(attn_part, input_raw)
    attn_blocks = send_blocks(attn_part)
    attn_part = order([attn_part, attn_blocks[0]], attn_part, 8)
    mixed = jnp.where(stays(), mixed_own, mixed_raw)
    mixed = row_pass(add_rows, "mixed", whole_rows(mixed, *mixed_others), [], [bf16])[0]
    grad_ff = add_blocks(ff_blocks)
    units = w_gate.shape[1]
    grad_gate, grad_up, grad_down = (grad_ff[:, units * i : units * (i + 1)] for i in range(3))
    input_grad = jnp.where(stays(), input_grad, input_raw).astype(f32)

    def weighed(weights, part, width):
        product = weights[:, :width].astype(f32) * part[:, :width].astype(f32)
        return jnp.sum(product, 1).reshape(2, -1)

    gain_parts = jnp.stack(
        [weighed(attn_kept, attn_part, qcols + 2 * kcols if cut else qw + 2 * kw), weighed(ff_rows, ff_part, 2 * units)]
    )
    gain_parts = jnp.where(core == 0, gain_parts, gain_parts[:, ::-1])
    gain_parts = gain_parts[:, 0] + other_core(gain_parts[:, 1]) + marks[0][0, 0]
    count = 2 * ring
    gain_grads = sum_steps(
        gain_parts,
        [
            lax.ppermute(gain_parts, ("zh", "zl"), [(i, (i + j) % count) for i in range(count)])
            for j in range(1, count)
        ],
    )
    gain_first_grad = gain_grads[0] / norm1_gain.astype(f32)
    gain_second_grad = gain_grads[1] / norm2_gain.astype(f32)
    mixed, input_grad, gain_first_grad, gain_second_grad, grad_gate, grad_up, grad_down, attn_blocks = (
        together(
            mixed,
            input_grad,
            gain_first_grad,
            gain_second_grad,
            grad_gate,
            grad_up,
            grad_down,
            attn_blocks,
        )
    )
    grad_query, grad_key, grad_value, grad_output = cut_heads(
        attn_blocks, [qcols, kcols, kcols, qcols]
    )
    return (
        mixed,
        input_grad,
        gain_first_grad,
        grad_query,
        grad_key,
        grad_value,
        grad_output,
        gain_second_grad,
        grad_gate,
        grad_up,
        grad_down,
    )


def solution(mesh):
    dp, tensor = mesh.devices.shape
    ring = tensor // 2
    regrouped = Mesh(mesh.devices.reshape(dp // 2, 2, 2, ring), ("d", "c", "zh", "zl"))
    data, parts = ("d", "c"), ("zh", "zl")
    tokens_spec = P(data + parts, None)
    weight_spec = P(data, parts)
    in_specs = (
        tokens_spec,
        P(data),
        P(data),
        weight_spec,
        weight_spec,
        weight_spec,
        weight_spec,
        P(data),
        weight_spec,
        weight_spec,
        weight_spec,
        tokens_spec,
    )
    out_specs = (
        tokens_spec,
        tokens_spec,
        P(data),
        weight_spec,
        weight_spec,
        weight_spec,
        weight_spec,
        P(data),
        weight_spec,
        weight_spec,
        weight_spec,
    )
    return jax.shard_map(
        functools.partial(per_device, ring),
        mesh=regrouped,
        in_specs=in_specs,
        out_specs=out_specs,
        check_vma=False,
    )
```

```python
import functools
import math

import jax
import jax.numpy as jnp
from jax import lax
from jax.experimental import pallas as pl
from jax.experimental.pallas import tpu as pltpu
from jax.sharding import Mesh
from jax.sharding import PartitionSpec as P

HEAD_SIZE = 96
SEQUENCE_LENGTH = 2048
LANES = 128

epsilon = 1e-05
rope_base = 100000.0
masked_score = -1e30
query_scale = math.log2(math.e) * HEAD_SIZE ** (-0.5)
rows_both = (((0,), (0,)), ((), ()))
cols_both = (((1,), (1,)), ((), ()))
plain = (((1,), (0,)), ((), ()))
f32 = jnp.float32
light = pl.CostEstimate(flops=1, bytes_accessed=1, transcendentals=0)
heavy = pl.CostEstimate(flops=8 * 10**9, bytes_accessed=1, transcendentals=0)
unread = pl.BlockSpec(memory_space=pl.ANY)
bf16 = jnp.bfloat16


def flipped(core, column, place, ring):
    return jnp.where(core == place[2], column, ring - 1 - column)


def local_block(g, place, ring):
    core = g // ring
    column = flipped(core, lax.rem(g, ring), place, ring)
    step = lax.rem(column - place[1] + ring, ring)
    return 2 * step + lax.rem(core + place[0], 2)


def global_block(l, place, ring):
    core = lax.rem(lax.rem(l, 2) + place[0], 2)
    column = lax.rem(l // 2 + place[1], ring)
    return core * ring + flipped(core, column, place, ring)


def in_hbm(*arrays):
    return [pltpu.with_memory_space_constraint(a, pltpu.HBM) for a in arrays]


def attend_kernel(ring, block, chip, place_ref, q_ref, k_ref, v_ref, start_ref, *refs):
    o_ref, lse_ref = refs[-2:]
    g = global_block(2 * chip + pl.program_id(1), place_ref, ring)
    share = q_ref.shape[1] // LANES
    start = start_ref[...]
    row = lax.broadcasted_iota(jnp.int32, (block, block), 0)
    col = lax.broadcasted_iota(jnp.int32, (block, block), 1)
    queries = [q_ref[:, h * LANES : (h + 1) * LANES] for h in range(share)]

    def step(kb, carry, diagonal):
        offset = pl.multiple_of(local_block(kb, place_ref, ring) * block, block)
        keys = k_ref[pl.ds(offset, block), :]
        values = v_ref[pl.ds(offset, block), :]
        shown = row >= start - kb * block
        if diagonal:
            shown = shown & (row <= col)
        out = []
        for h in range(share):
            largest, total, acc = carry[h]
            s = lax.dot_general(keys, queries[h], cols_both, preferred_element_type=f32)
            s = jnp.where(shown, s, masked_score)
            newest = jnp.maximum(largest, jnp.max(s, 0, keepdims=True))
            fade = jnp.exp2(largest - newest)
            p = jnp.exp2(s - newest)
            total = total * fade + jnp.sum(p, 0, keepdims=True)
            acc = acc * fade + lax.dot_general(
                values, p.astype(bf16), rows_both, preferred_element_type=f32
            )
            out.append((newest, total, acc))
        return tuple(out)

    carry = tuple(
        (
            jnp.full((1, block), masked_score, f32),
            jnp.zeros((1, block), f32),
            jnp.zeros((LANES, block), f32),
        )
        for _ in range(share)
    )
    carry = step(g, carry, True)
    carry = lax.fori_loop(0, g, lambda kb, c: step(kb, c, False), carry)
    for h in range(share):
        largest, total, acc = carry[h]
        o_ref[:, h * LANES : (h + 1) * LANES] = jnp.transpose(acc / total).astype(bf16)
        lse_ref[0, h : h + 1, :] = largest + jnp.log2(total)


def attend(chip, place, q, k, v, start, ring, first=()):
    length = q.shape[0]
    block = length // (2 * ring)
    kv = k.shape[1] // LANES
    share = q.shape[1] // k.shape[1]
    return pl.pallas_call(
        functools.partial(attend_kernel, ring, block, chip),
        grid_spec=pltpu.PrefetchScalarGridSpec(
            num_scalar_prefetch=1,
            grid=(kv, 2),
            in_specs=[
                pl.BlockSpec((block, share * LANES), lambda h, j, z: (2 * chip + j, h)),
                pl.BlockSpec((length, LANES), lambda h, j, z: (0, h)),
                pl.BlockSpec((length, LANES), lambda h, j, z: (0, h)),
                pl.BlockSpec((1, block), lambda h, j, z: (0, 2 * chip + j)),
            ]
            + [unread] * len(first),
            out_specs=[
                pl.BlockSpec((block, share * LANES), lambda h, j, z: (j, h)),
                pl.BlockSpec((1, share, block), lambda h, j, z: (h, 0, j)),
            ],
        ),
        out_shape=[
            jax.ShapeDtypeStruct((2 * block, q.shape[1]), bf16),
            jax.ShapeDtypeStruct((kv, share, 2 * block), f32),
        ],
        compiler_params=pltpu.CompilerParams(
            vmem_limit_bytes=40 * 2**20, dimension_semantics=("arbitrary", "arbitrary")
        ),
        cost_estimate=heavy if first else light,
        name="attend",
    )(place, q, k, v, start, *first)


def attend_back_kernel(
    ring,
    block,
    chip,
    final,
    place_ref,
    q_ref,
    k_ref,
    v_ref,
    o_ref,
    do_ref,
    lse_ref,
    start_ref,
    cosq_ref,
    sinq_ref,
    *refs,
):
    if final:
        cosk_ref, sink_ref = refs[:2]
    before = refs[2 * final : -5]
    dq_ref, dk_ref, dv_ref, dk_acc, dv_acc = refs[-5:]
    j = pl.program_id(1)
    g = global_block(2 * chip + j, place_ref, ring)
    share = q_ref.shape[1] // LANES

    @pl.when(j == 0)
    def _():
        if before:
            dk_acc[...] = before[0][...]
            dv_acc[...] = before[1][...]
        else:
            dk_acc[...] = jnp.zeros_like(dk_acc)
            dv_acc[...] = jnp.zeros_like(dv_acc)

    start = start_ref[...]
    row = lax.broadcasted_iota(jnp.int32, (block, block), 0)
    col = lax.broadcasted_iota(jnp.int32, (block, block), 1)
    heads = [slice(h * LANES, (h + 1) * LANES) for h in range(share)]
    queries = [q_ref[:, h] for h in heads]
    grads = [do_ref[:, h] for h in heads]
    lses = [lse_ref[0, h : h + 1, :] for h in range(share)]
    inner = [
        jnp.sum(
            jnp.transpose(do_ref[:, h].astype(f32) * o_ref[:, h].astype(f32)), 0, keepdims=True
        )
        for h in heads
    ]

    def step(kb, carry):
        offset = pl.multiple_of(local_block(kb, place_ref, ring) * block, block)
        keys = k_ref[pl.ds(offset, block), :]
        values = v_ref[pl.ds(offset, block), :]
        shown = row >= start - kb * block
        out = []
        dk = jnp.zeros((block, LANES), f32)
        dv = jnp.zeros((block, LANES), f32)
        for h in range(share):
            s = lax.dot_general(keys, queries[h], cols_both, preferred_element_type=f32)
            p = jnp.where(shown, jnp.exp2(s - lses[h]), 0.0)
            dp = lax.dot_general(values, grads[h], cols_both, preferred_element_type=f32)
            ds = (p * (dp - inner[h])).astype(bf16)
            dv += jnp.dot(p.astype(bf16), grads[h], preferred_element_type=f32)
            dk += jnp.dot(ds, queries[h], preferred_element_type=f32)
            out.append(carry[h] + lax.dot_general(keys, ds, rows_both, preferred_element_type=f32))
        dk_acc[pl.ds(offset, block), :] += dk
        dv_acc[pl.ds(offset, block), :] += dv
        return tuple(out)

    half = block // 2
    offset = pl.multiple_of(local_block(g, place_ref, ring) * block, block)
    found = [[] for _ in range(share)]
    for part in range(2):
        seen, lanes = (part + 1) * half, slice(part * half, (part + 1) * half)
        keys = k_ref[pl.ds(offset, seen), :]
        values = v_ref[pl.ds(offset, seen), :]
        shown = (row[:seen, :half] >= start[:, lanes] - g * block) & (
            row[:seen, :half] <= col[:seen, lanes]
        )
        dk = jnp.zeros((seen, LANES), f32)
        dv = jnp.zeros((seen, LANES), f32)
        for h in range(share):
            q, do = queries[h][lanes], grads[h][lanes]
            s = lax.dot_general(keys, q, cols_both, preferred_element_type=f32)
            p = jnp.where(shown, jnp.exp2(s - lses[h][:, lanes]), 0.0)
            dp = lax.dot_general(values, do, cols_both, preferred_element_type=f32)
            ds = (p * (dp - inner[h][:, lanes])).astype(bf16)
            dv += jnp.dot(p.astype(bf16), do, preferred_element_type=f32)
            dk += jnp.dot(ds, q, preferred_element_type=f32)
            found[h].append(lax.dot_general(keys, ds, rows_both, preferred_element_type=f32))
        dk_acc[pl.ds(offset, seen), :] += dk
        dv_acc[pl.ds(offset, seen), :] += dv
    carry = tuple(jnp.concatenate(found[h], 1) for h in range(share))
    carry = lax.fori_loop(0, g, step, carry)
    for h in range(share):
        u = jnp.transpose(carry[h]) * HEAD_SIZE ** (-0.5)
        turned = u * cosq_ref[...] - pltpu.roll(u, LANES // 2, 1) * sinq_ref[...]
        dq_ref[:, heads[h]] = turned.astype(bf16)

    @pl.when(j == 1)
    def _():
        def finish(i, _):
            r = pl.ds(pl.multiple_of(i * block, block), block)
            u = dk_acc[r, :]
            if final:
                u = u * math.log(2.0)
                u = u * cosk_ref[r, :] - pltpu.roll(u, LANES // 2, 1) * sink_ref[r, :]
            dk_ref[r, :] = u.astype(dk_ref.dtype)
            dv_ref[r, :] = dv_acc[r, :].astype(dv_ref.dtype)
            return 0

        lax.fori_loop(0, 2 * ring, finish, 0)


def attend_back(chip, place, q, k, v, o, do, lse, start, cos, sin, ring, before):
    length = q.shape[0]
    block = length // (2 * ring)
    kv = k.shape[1] // LANES
    share = q.shape[1] // k.shape[1]
    final = chip == ring - 1
    kind = bf16 if final else f32
    qspec = pl.BlockSpec((block, share * LANES), lambda h, j, z: (2 * chip + j, h))
    own = pl.BlockSpec((block, share * LANES), lambda h, j, z: (j, h))
    kspec = pl.BlockSpec((length, LANES), lambda h, j, z: (0, h))
    table = pl.BlockSpec((block, LANES), lambda h, j, z: (2 * chip + j, 0))
    whole = pl.BlockSpec((length, LANES), lambda h, j, z: (0, 0))
    return pl.pallas_call(
        functools.partial(attend_back_kernel, ring, block, chip, final),
        grid_spec=pltpu.PrefetchScalarGridSpec(
            num_scalar_prefetch=1,
            grid=(kv, 2),
            in_specs=[
                qspec,
                kspec,
                kspec,
                own,
                own,
                pl.BlockSpec((1, share, block), lambda h, j, z: (h, 0, j)),
                pl.BlockSpec((1, block), lambda h, j, z: (0, 2 * chip + j)),
                table,
                table,
            ]
            + [whole, whole] * final
            + [kspec] * len(before),
            out_specs=[own, kspec, kspec],
            scratch_shapes=[pltpu.VMEM((length, LANES), f32), pltpu.VMEM((length, LANES), f32)],
        ),
        out_shape=[
            jax.ShapeDtypeStruct((2 * block, q.shape[1]), bf16),
            jax.ShapeDtypeStruct(k.shape, kind),
            jax.ShapeDtypeStruct(k.shape, kind),
        ],
        compiler_params=pltpu.CompilerParams(
            vmem_limit_bytes=40 * 2**20, dimension_semantics=("arbitrary", "arbitrary")
        ),
        cost_estimate=light,
        name="attend_back",
    )(place, q, k, v, o, do, lse, start, cos, sin, *[cos, sin] * final, *before)


def pieces_spec(block, width, count):
    return [
        pl.BlockSpec((block, width), lambda i: (jnp.minimum(i, count - 1), 0)),
        pl.BlockSpec((block, width), lambda i: (jnp.maximum(i - count, 0), 0)),
    ]


def picked(count, first_ref, second_ref):
    return jnp.where(pl.program_id(0) < count, first_ref[...], second_ref[...])


def project_kernel(
    widths, count, x_ref, y_ref, gain_ref, w_ref, cos_ref, sin_ref, *refs
):
    a_ref, q_ref, k_ref, v_ref = refs[-4:]
    x = picked(count, x_ref, y_ref).astype(f32)
    root = lax.rsqrt(jnp.mean(x * x, -1, keepdims=True) + epsilon)
    a = (x * root * gain_ref[...]).astype(bf16)
    a_ref[...] = a
    cos = cos_ref[...]
    sin = sin_ref[...]
    whole = jnp.dot(a, w_ref[...], preferred_element_type=f32)
    qw, kw = widths
    for h in range((qw + kw) // LANES):
        u = whole[:, h * LANES : (h + 1) * LANES]
        turned = u * cos + pltpu.roll(u, LANES // 2, 1) * sin
        if h < qw // LANES:
            q_ref[:, h * LANES : (h + 1) * LANES] = (turned * query_scale).astype(bf16)
        else:
            j = h - qw // LANES
            k_ref[:, j * LANES : (j + 1) * LANES] = turned.astype(bf16)
    v_ref[...] = whole[:, qw + kw :].astype(bf16)


def project(pair, gain, w, cos, sin, qw, kw, step, before, first=()):
    rows, width = pair[0].shape
    length = cos.shape[0]
    block = min(256, rows)
    count = rows // block
    base = step * 2 * count
    widths = (width, qw, kw, kw)

    def row(n):
        return pl.BlockSpec((block, n), lambda i: (base + i, 0))

    def whole(shape):
        return pl.BlockSpec(shape, lambda i: (0, 0))

    return pl.pallas_call(
        functools.partial(project_kernel, (qw, kw), count),
        grid=(2 * count,),
        in_specs=pieces_spec(block, width, count)
        + [whole(gain.shape), whole((width, qw + 2 * kw)), row(LANES), row(LANES)]
        + [unread] * (len(before) + len(first)),
        out_specs=[row(n) for n in widths],
        out_shape=[jax.ShapeDtypeStruct((length, n), bf16) for n in widths],
        input_output_aliases={6 + i: i for i in range(len(before))},
        compiler_params=pltpu.CompilerParams(
            vmem_limit_bytes=40 * 2**20, dimension_semantics=("arbitrary",)
        ),
        cost_estimate=heavy if first else light,
        name="project",
    )(*in_hbm(*pair), gain, *in_hbm(w), cos, sin, *in_hbm(*before), *first)


def hidden_kernel(
    chunk, count, a_ref, b_ref, dy_ref, dz_ref, w_ref, hid_ref, dgu_ref, *refs
):
    a = picked(count, a_ref, b_ref)
    dy = picked(count, dy_ref, dz_ref)
    units = hid_ref.shape[1]
    for j in range(units // chunk):
        at = slice(j * chunk, (j + 1) * chunk)
        up = slice(units + j * chunk, units + (j + 1) * chunk)
        down = slice(2 * units + j * chunk, 2 * units + (j + 1) * chunk)
        g = jnp.dot(a, w_ref[:, at], preferred_element_type=f32)
        u = jnp.dot(a, w_ref[:, up], preferred_element_type=f32)
        dh = jnp.dot(dy, w_ref[:, down], preferred_element_type=f32)
        sig = jax.nn.sigmoid(g)
        silu = g * sig
        hid_ref[:, at] = (silu * u).astype(bf16)
        dgu_ref[:, at] = (dh * u * (sig + silu * (1.0 - sig))).astype(bf16)
        dgu_ref[:, up] = (dh * silu).astype(bf16)
    da = lax.dot_general(
        dgu_ref[...], w_ref[:, : 2 * units], cols_both, preferred_element_type=f32
    ).astype(bf16)
    mixed = lax.dot_general(
        hid_ref[...], w_ref[:, 2 * units :], cols_both, preferred_element_type=f32
    ).astype(bf16)
    mine = pl.program_id(0) < count

    @pl.when(mine)
    def _():
        refs[0][...] = da
        refs[2][...] = mixed

    @pl.when(jnp.logical_not(mine))
    def _():
        refs[1][...] = da
        refs[3][...] = mixed


def hidden_pass(a, dy, w):
    rows, width = a[0].shape
    units = w.shape[1] // 3
    block = min(256, rows)
    count = rows // block
    widths = [units, 2 * units]

    def row(n):
        return pl.BlockSpec((block, n), lambda i: (i, 0))

    return pl.pallas_call(
        functools.partial(hidden_kernel, min(256, units), count),
        grid=(2 * count,),
        in_specs=pieces_spec(block, width, count)
        + pieces_spec(block, width, count)
        + [pl.BlockSpec(w.shape, lambda i: (0, 0), pipeline_mode=pl.Buffered(1))],
        out_specs=[row(n) for n in widths] + 2 * pieces_spec(block, width, count),
        out_shape=[jax.ShapeDtypeStruct((2 * rows, n), bf16) for n in widths]
        + [jax.ShapeDtypeStruct((rows, width), bf16)] * 4,
        compiler_params=pltpu.CompilerParams(
            vmem_limit_bytes=40 * 2**20, dimension_semantics=("arbitrary",)
        ),
        cost_estimate=heavy,
        name="hidden",
    )(*a, *dy, w)


def product_kernel(dims, parts, unused, *refs):
    x = refs[0][...]
    if parts > 1:
        x = jnp.concatenate([ref[...] for ref in refs[:parts]], 1)
    p = lax.dot_general(x, refs[parts][...], dims, preferred_element_type=f32)
    out_ref = refs[-1]
    for ref in refs[parts + 1 + unused : -1]:
        p = p + ref[...].astype(f32)
    out_ref[...] = p.astype(out_ref.dtype)


def product(parts, rows, w, dims, kind=bf16, columns=None, add=None, cost=light, after=()):
    block = min(256, rows)
    columns = columns or (0, w.shape[1])
    wide = columns[1]
    out = w.shape[0] if dims == cols_both else wide
    row = pl.BlockSpec((block, out), lambda i: (i, 0))
    extra = [] if add is None else [add]
    return pl.pallas_call(
        functools.partial(product_kernel, dims, len(parts), len(after)),
        grid=(rows // block,),
        in_specs=[
            pl.BlockSpec((block, x.shape[1]), lambda i, first=first: (first // block + i, 0))
            for x, first in parts
        ]
        + [pl.BlockSpec((w.shape[0], wide), lambda i: (0, columns[0]))]
        + [unread] * len(after)
        + [row] * len(extra),
        out_specs=row,
        out_shape=jax.ShapeDtypeStruct((rows, out), kind),
        compiler_params=pltpu.CompilerParams(
            vmem_limit_bytes=40 * 2**20, dimension_semantics=("arbitrary",)
        ),
        cost_estimate=cost,
        name="product",
    )(*[x for x, _ in parts], *in_hbm(w), *after, *extra)


def without_gaps(w):
    half = HEAD_SIZE // 2
    parts = [w[:, at : at + half] for at in range(0, w.shape[1], LANES // 2)]
    return jnp.concatenate(parts, 1)


def wgrad_kernel(counts, cut, *refs):
    out_ref = refs[-1]
    j = pl.program_id(0)
    first = 0
    for pieces, parts, blocks in counts:
        lefts, refs = refs[:pieces], refs[pieces:]
        rights, refs = refs[: pieces * parts], refs[pieces * parts :]

        @pl.when((j >= first) & (j < first + blocks))
        def _():
            total = None
            for i, a in enumerate(lefts):
                b = [ref[...] for ref in rights[parts * i : parts * (i + 1)]]
                b = b[0] if parts == 1 else jnp.concatenate(b, 1)
                p = lax.dot_general(a[...], b, rows_both, preferred_element_type=f32)
                total = p if total is None else total + p
            total = total.astype(bf16)
            out_ref[...] = without_gaps(total) if cut else total

        first += blocks


def wgrad(groups, rows, block, first=(), cut=False):
    width = groups[0][0][0].shape[1]
    counts, specs, args = [], [], []
    column = 0
    for group in groups:
        parts = len(group[0][2])
        blocks = sum(b.shape[1] for b in group[0][2]) // block
        counts.append((len(group), parts, blocks))
        for a, at, _, _ in group:
            specs.append(
                pl.BlockSpec(
                    (rows, width), lambda j, at=at: (at, 0), pipeline_mode=pl.Buffered(1)
                )
            )
            args.append(a)
        for _, _, sides, at in group:

            def spot(j, at=at, column=column, blocks=blocks):
                return (at, jnp.clip(j - column, 0, blocks - 1))

            for b in sides:
                specs.append(pl.BlockSpec((rows, b.shape[1] if parts > 1 else block), spot))
                args.append(b)
        column += blocks
    wide = block * 3 // 4 if cut else block
    return pl.pallas_call(
        functools.partial(wgrad_kernel, counts, cut),
        grid=(column,),
        in_specs=specs + [unread] * len(first),
        out_specs=pl.BlockSpec((width, wide), lambda j: (0, j)),
        out_shape=pltpu.HBM((width, column * wide), bf16),
        compiler_params=pltpu.CompilerParams(
            vmem_limit_bytes=40 * 2**20, dimension_semantics=("arbitrary",)
        ),
        cost_estimate=heavy if first else light,
        name="wgrad",
    )(*in_hbm(*args), *first)


def row_pass(body, name, inputs, whole, kinds, after=()):
    width = inputs[0][0].shape[1]
    rows = min(a.shape[0] - first for a, first in inputs)
    block = min(256, rows)

    def kernel(*refs):
        count = len(inputs) + len(whole)
        values = [ref[...].astype(f32) for ref in refs[:count]]
        for ref, value in zip(refs[count + len(after) :], body(*values)):
            ref[...] = value.astype(ref.dtype)

    return pl.pallas_call(
        kernel,
        grid=(rows // block,),
        in_specs=[
            pl.BlockSpec((block, width), lambda i, first=first: (first // block + i, 0))
            for _, first in inputs
        ]
        + [pl.BlockSpec(a.shape, lambda i: (0, 0)) for a in whole]
        + [unread] * len(after),
        out_specs=[pl.BlockSpec((block, width), lambda i: (i, 0)) for _ in kinds],
        out_shape=[jax.ShapeDtypeStruct((rows, width), kind) for kind in kinds],
        compiler_params=pltpu.CompilerParams(dimension_semantics=("arbitrary",)),
        cost_estimate=light,
        name=name,
    )(*[a for a, _ in inputs], *whole, *after)


def inverse_root(x):
    return lax.rsqrt(jnp.mean(x * x, -1, keepdims=True) + epsilon)


def add_rows(*items):
    return (sum_steps(items[0], items[1:]),)


def norm_forward(stream, *rest):
    *terms, gain = rest
    middle = sum_steps(stream, terms)
    return middle, middle * inverse_root(middle) * gain


def norm_back(residual, values, *rest):
    *terms, gain = rest
    root = inverse_root(values)
    scaled = sum_steps(terms[0], terms[1:]) * gain
    mean = jnp.mean(scaled * values, -1, keepdims=True)
    return (residual + root * scaled - values * root**3 * mean,)


def pad_kernel(counts, *refs):
    out_ref = refs[-1]
    gains = refs[-2][...]
    half = HEAD_SIZE // 2
    rows = out_ref.shape[0]
    at = 0
    for ref, heads in zip(refs[:-2], counts):
        w = ref[...]
        for h in range(heads):
            gap = jnp.zeros((rows, LANES // 2 - half), bf16)
            first = w[:, h * HEAD_SIZE : h * HEAD_SIZE + half]
            second = w[:, h * HEAD_SIZE + half : (h + 1) * HEAD_SIZE]
            free = gap if at else jnp.concatenate([gains, gap[:, 2:]], 1)
            out_ref[:, at : at + LANES] = jnp.concatenate([first, free, second, gap], 1)
            at += LANES


def pad_heads(weights, gains):
    counts = [w.shape[1] // HEAD_SIZE for w in weights]
    return pl.pallas_call(
        functools.partial(pad_kernel, counts),
        out_shape=jax.ShapeDtypeStruct((weights[0].shape[0], sum(counts) * LANES), bf16),
        cost_estimate=light,
        name="pad",
    )(*weights, gains)


def cut_kernel(widths, padded, keep_ref, own_ref, crossed_ref, slanted_ref, *out_refs):
    kept = keep_ref[0] == 1
    at = 0
    for ref, width in zip(out_refs, widths):
        wide = width // HEAD_SIZE * LANES if padded else width
        lanes = slice(at, at + wide)
        w = jnp.where(kept, own_ref[:, lanes], crossed_ref[:, lanes]).astype(f32)
        w = w + slanted_ref[:, lanes].astype(f32)
        ref[...] = without_gaps(w) if padded else w
        at += wide


def cut_heads(blocks, widths):
    rows, columns = blocks[0].shape
    keep = stays().astype(jnp.int32).reshape(1)
    return pl.pallas_call(
        functools.partial(cut_kernel, widths, columns != sum(widths)),
        in_specs=[pl.BlockSpec(memory_space=pltpu.SMEM)]
        + [pl.BlockSpec(memory_space=pltpu.VMEM)] * 3,
        out_shape=[jax.ShapeDtypeStruct((rows, width), f32) for width in widths],
        cost_estimate=light,
        name="cut",
    )(keep, *blocks)


def cut_rows_kernel(in_ref, out_ref):
    out_ref[...] = without_gaps(in_ref[...])


def cut_rows(w):
    return pl.pallas_call(
        cut_rows_kernel,
        out_shape=jax.ShapeDtypeStruct((w.shape[0], w.shape[1] * 3 // 4), w.dtype),
        cost_estimate=light,
        name="cut_rows",
    )(w)


swap_two = [(0, 1), (1, 0)]
cross_pairs = [(1, 2), (2, 1)]
slant_pairs = [(2 * c + zh, 2 * zh + (1 - c)) for c in range(2) for zh in range(2)]
slant_back = [(b, a) for a, b in slant_pairs]


def stays():
    return lax.axis_index("c") == lax.axis_index("zh")


def cross(a):
    return lax.ppermute(a, ("c", "zh"), cross_pairs)


def other_core(a):
    return lax.ppermute(a, "c", swap_two)


def from_neighbour(a, k, ring):
    return lax.ppermute(a, "zl", [(i, (i - k) % ring) for i in range(ring)])


def both_cores(a):
    return jnp.concatenate([a, other_core(a)], 0)


def spread_pair(w):
    return w, cross(w), lax.ppermute(w, ("c", "zh"), slant_pairs)


def arrange(own, crossed, slanted):
    first = lax.axis_index("zh") == 0
    straight = jnp.where(stays(), own, crossed)
    return jnp.concatenate(
        [jnp.where(first, straight, slanted), jnp.where(first, slanted, straight)], 0
    )


def gather_rows(w):
    return lax.all_gather(w, "d", axis=0, tiled=True)


def send_blocks(part):
    rows = part.shape[0] // 2
    first = lax.axis_index("zh") == 0
    upper, lower = part[:rows], part[rows:]
    straight = jnp.where(first, upper, lower)
    slanted = lax.ppermute(jnp.where(first, lower, upper), ("c", "zh"), slant_back)
    return straight, cross(straight), slanted


def add_blocks(blocks):
    straight, crossed, slanted = blocks
    return jnp.where(stays(), straight, crossed).astype(f32) + slanted.astype(f32)


def sum_rows(grad):
    return lax.psum_scatter(grad, "d", scatter_dimension=0, tiled=True)


def together(*items):
    return lax.optimization_barrier(items)


def mark_kernel(*refs):
    refs[-1][...] = jnp.zeros_like(refs[-1])


def mark(arrays, before, long):
    whole = pl.BlockSpec(before.shape, lambda: (0, 0))
    cost = pl.CostEstimate(flops=1 + long * 10**9, bytes_accessed=1, transcendentals=0)
    return pl.pallas_call(
        mark_kernel,
        in_specs=[pl.BlockSpec(memory_space=pl.ANY)] * len(arrays) + [whole],
        out_specs=whole,
        out_shape=jax.ShapeDtypeStruct(before.shape, before.dtype),
        cost_estimate=cost,
        name="mark",
    )(*arrays, before)


def dot(a, b):
    return jnp.dot(a, b, preferred_element_type=f32)


def dot_cols(a, b):
    return lax.dot_general(a, b, cols_both, preferred_element_type=f32)


def dot_rows(a, b):
    return lax.dot_general(a, b, rows_both, preferred_element_type=f32)


def sum_steps(first, second):
    out = first
    for item in second:
        out = out + item
    return out


def per_device(
    ring,
    tokens,
    positions,
    norm1_gain,
    w_query,
    key_weight,
    value_weight,
    w_out,
    norm2_gain,
    w_gate,
    w_up,
    w_down,
    cotangent,
):
    steps = range(ring)
    core = lax.axis_index("c")
    column = lax.axis_index("zl")
    place = jnp.stack([core, column, lax.axis_index("zh")]).astype(jnp.int32)
    rows = tokens.shape[0]
    length = 2 * ring * rows
    marks = [jnp.zeros((8, LANES), f32)]

    def order(first, then, long=0):
        marks[0], then = together(mark(first, marks[0], long), then)
        return then

    def swap_chips(own):
        return [from_neighbour(own, k, ring) for k in steps[1:]]

    def join_cores(partial, kind=bf16):
        theirs = other_core(partial(rows, bf16, None))
        return partial(0, kind, theirs)

    def join(mine, theirs):
        return row_pass(add_rows, "join", [(mine, 0), (theirs, 0)], [], [bf16])[0]

    def split_cores(partial):
        return [partial(0, bf16, None), other_core(partial(rows, bf16, None))]

    def send_chips(joined):
        return [
            lax.ppermute(p.astype(bf16), "zl", [(i, (i + k) % ring) for i in steps])
            for k, p in zip(steps[1:], joined)
        ]

    def pairs_of(kept, k):
        out = []
        for c in range(2):
            for zh in range(2):
                if (c == zh) == kept:
                    base = (2 * c + zh) * ring
                    out += [(base + i, base + (i - k) % ring) for i in steps]
        return out

    def cross_tokens(a):
        pairs = []
        for c, zh in ((0, 1), (1, 0)):
            pairs += [
                ((2 * c + zh) * ring + i, (2 * zh + c) * ring + ring - 1 - i) for i in steps
            ]
        return lax.ppermute(a, ("c", "zh", "zl"), pairs)

    def home_pairs(k):
        pairs = []
        for c in range(2):
            for zh in range(2):
                for i in steps:
                    at = (i + k) % ring
                    home = (2 * c + zh) * ring + at
                    if c != zh:
                        home = (2 * zh + c) * ring + ring - 1 - at
                    pairs.append(((2 * c + zh) * ring + i, home))
        return pairs

    def early_neighbours(original):
        return [
            lax.ppermute(original, ("c", "zh", "zl"), pairs_of(True, k)) for k in steps if k
        ]

    def first_moves(original):
        pairs = [(a, b) for a, b in home_pairs(0) if a != b] + pairs_of(True, 1)
        moved = lax.ppermute(original, ("c", "zh", "zl"), pairs)
        rest = [
            lax.ppermute(original, ("c", "zh", "zl"), pairs_of(True, k)) for k in steps[2:]
        ]
        return moved, [moved] + rest

    def late_neighbours(moved):
        return [lax.ppermute(moved, ("c", "zh", "zl"), pairs_of(False, k)) for k in steps[1:]]

    def choose(early, late):
        return [jnp.where(stays(), e, l) for e, l in zip(early, late)]

    qcols, kcols = w_query.shape[1], key_weight.shape[1]
    qw = qcols // HEAD_SIZE * LANES
    kw = kcols // HEAD_SIZE * LANES
    half = HEAD_SIZE // 2
    attn_shard = pad_heads(
        [w_query, key_weight, value_weight, w_out], jnp.stack([norm1_gain, norm2_gain], 1)
    )
    other_positions = other_core(positions)
    attn_pair = spread_pair(attn_shard)
    cot_early = early_neighbours(cotangent)
    attn_pair, cot_early, tokens, other_positions = together(
        attn_pair, cot_early, tokens, other_positions
    )
    places = jnp.where(stays(), positions, other_positions).reshape(2 * ring, rows)
    attn_rows = arrange(*attn_pair)
    attn_full = gather_rows(attn_rows)
    cut = qw * 3 // 4 % LANES == 0
    stream_raw, tokens_early = first_moves(tokens)

    blocks = [global_block(l, place, ring) for l in range(2 * ring)]
    ordered = [lax.dynamic_index_in_dim(places, g, 0, keepdims=False) for g in blocks]
    start = jnp.concatenate(
        [g * rows + jnp.arange(rows, dtype=jnp.int32) - o for g, o in zip(blocks, ordered)]
    )[None, :]
    spots = jnp.concatenate(ordered).astype(f32)
    inverse = rope_base ** (-(2.0 / HEAD_SIZE) * jnp.arange(half, dtype=f32))
    angles = spots[:, None] * inverse[None, :]
    gap = jnp.zeros((length, LANES // 2 - half), f32)
    cos_half, sin_half = jnp.cos(angles), jnp.sin(angles)
    cos = jnp.concatenate([cos_half, gap, cos_half, gap], 1)
    sin = jnp.concatenate([-sin_half, gap, sin_half, gap], 1)

    ff_cols = jnp.concatenate([w_gate, w_up, w_down], 1)
    cos, sin, start, stream_raw, tokens_early, ff_cols, attn_rows = together(
        cos, sin, start, stream_raw, tokens_early, ff_cols, attn_rows
    )
    attn_kept = cut_rows(attn_rows) if cut else attn_rows
    stream_own = jnp.where(stays(), tokens, stream_raw)
    tokens_late = late_neighbours(stream_raw)
    ff_pair = spread_pair(ff_cols)

    out_columns = ((qw + 2 * kw) // qw, qw)
    qkv_columns = (0, qw + 2 * kw)
    gain_first = attn_full[:, half].astype(f32)[None, :]
    gain_second = attn_full[:, half + 1].astype(f32)[None, :]

    projected = project(
        (stream_own, other_core(stream_own)), gain_first, attn_full, cos, sin, qw, kw, 0, ()
    )
    tokens_late, ff_pair, projected, cot_sent, attn_kept = together(
        tokens_late, ff_pair, projected, cotangent, attn_kept
    )
    others = [(x, other_core(x)) for x in choose(tokens_early, tokens_late)]
    ff_rows = arrange(*ff_pair)
    ff_full = gather_rows(ff_rows)
    cot_raw = cross_tokens(cot_sent)
    for k, pair in enumerate(others, 1):
        projected = project(
            pair, gain_first, attn_full, cos, sin, qw, kw, k, projected, (ff_rows,)
        )
    normed_first, q, k, v = projected

    def out_product(o):
        return lambda first, kind, add: product(
            [(o, first)], rows, attn_full, cols_both, kind, out_columns, add
        )

    def whole_rows(*arrays):
        return [(a, 0) for a in arrays]

    attended = [attend(i, place, q, k, v, start, ring) for i in steps[1:]]
    attended, cot_raw = together(attended, cot_raw)
    joined = [join_cores(out_product(o)) for o, _ in attended]
    sent = send_chips(joined)
    cot_late = late_neighbours(cot_raw)
    q, k, v = order(joined, (q, k, v), 8)
    attended.insert(0, attend(0, place, q, k, v, start, ring))
    out_own = split_cores(out_product(attended[0][0]))
    sent, out_own[0], cot_late = together(sent, out_own[0], cot_late)
    middle, normed_second = row_pass(
        norm_forward,
        "norm_forward",
        whole_rows(stream_own, *out_own, *sent),
        [gain_second],
        [bf16, bf16],
    )
    normed_second, cot_raw = together(normed_second, cot_raw)
    cot_own = jnp.where(stays(), cotangent, cot_raw)
    ff_others = swap_chips(normed_second)
    ff_in = [(normed_second, other_core(normed_second))]
    out_grads = [(cot_own, other_core(cot_own))]
    ff_in, out_grads = order([normed_second], (ff_in, out_grads), 8)
    hidden = [hidden_pass(ff_in[0], out_grads[0], ff_full)]
    hidden, ff_others = together(hidden, ff_others)

    second_own = [hidden[0][2], other_core(hidden[0][3])]
    mixed_own = [hidden[0][4], other_core(hidden[0][5])]
    mixed_own = row_pass(add_rows, "mixed", whole_rows(middle, *mixed_own), [], [bf16])[0]
    mixed_raw = cross_tokens(mixed_own)
    for a, dy in zip(ff_others, choose(cot_early, cot_late)):
        a, dy = (a, other_core(a)), (dy, other_core(dy))
        a, dy, second_own, mixed_own = together(a, dy, second_own, mixed_own)
        ff_in.append(a)
        out_grads.append(dy)
        hidden.append(hidden_pass(a, dy, ff_full))

    def pieces(pairs, hidden, i):
        return [(a, 0, (h[i],), j) for pair, h in zip(pairs, hidden) for j, a in enumerate(pair)]

    hidden, mixed_raw = together(hidden, mixed_raw)
    joined = [join(h[2], other_core(h[3])) for h in hidden[1:]]
    sent = send_chips(joined)
    mixed_halves = [(h[4], other_core(h[5])) for h in hidden[1:]]
    mixed_joined = [join(*pair) for pair in mixed_halves]
    ff_wgrad = wgrad(
        [pieces(ff_in, hidden, 1), pieces(out_grads, hidden, 0)],
        rows,
        min(512, w_down.shape[1]),
        joined,
    )
    sent, mixed_joined, ff_wgrad = together(sent, mixed_joined, ff_wgrad)
    ff_part = sum_rows(ff_wgrad)
    db = row_pass(
        norm_back,
        "norm_back",
        whole_rows(cot_own, middle, *second_own, *sent),
        [gain_second],
        [bf16],
    )[0]
    branch_others = swap_chips(db)
    branch = [(db, other_core(db))]

    def heads_grad(pair):
        return jnp.concatenate(
            [
                product([(b, 0)], rows, attn_full, plain, columns=out_columns, cost=cost)
                for b, cost in zip(pair, (heavy, light))
            ],
            0,
        )

    def queries_back(i, do, before):
        o, lse = attended[i]
        return attend_back(i, place, q, k, v, o, do, lse, start, cos, sin, ring, before)

    dq, *dkv = queries_back(0, heads_grad(branch[0]), ())
    dqs = [dq]
    branch_others, mixed_joined, dqs, dkv = together(branch_others, mixed_joined, dqs, dkv)
    mixed_others = [
        lax.ppermute(p, ("c", "zh", "zl"), home_pairs(k)) for k, p in zip(steps[1:], mixed_joined)
    ]
    branch += [(b, other_core(b)) for b in branch_others]
    for i in steps[1:]:
        dq, *dkv = queries_back(i, heads_grad(branch[i]), tuple(dkv))
        dqs.append(dq)
    mixed_others, dqs, dkv = together(mixed_others, dqs, dkv)
    def first_product(i, after=()):
        base = 2 * rows * i
        return lambda first, kind, add: product(
            [(dqs[i], first)] + [(d, base + first) for d in dkv],
            rows,
            attn_full,
            cols_both,
            kind,
            qkv_columns,
            add,
            after=after,
        )

    joined = [join_cores(first_product(i)) for i in steps[1:]]
    sent = send_chips(joined)
    ff_blocks = send_blocks(ff_part)
    first_own = split_cores(first_product(0, joined))
    attn_wgrad = wgrad(
        [
            [(normed_first, 2 * i + j, (dqs[i],), j) for i in steps for j in range(2)],
            [(normed_first, i, tuple(dkv), i) for i in range(2 * ring)],
            [(branch[i][j], 0, (attended[i][0],), j) for i in steps for j in range(2)],
        ],
        rows,
        qw,
        (*joined, ff_blocks[0]),
        cut,
    )
    attn_part = sum_rows(attn_wgrad)
    sent, first_own[0], wgrad_there = together(sent, first_own[0], attn_wgrad)

    input_grad = row_pass(
        norm_back,
        "norm_back",
        whole_rows(db, stream_own, *first_own, *sent),
        [gain_first],
        [bf16],
        [wgrad_there],
    )[0]
    input_raw = cross_tokens(input_grad)
    attn_part, ff_blocks, mixed_others = order(
        [input_grad, *ff_blocks[1:]], (attn_part, ff_blocks, mixed_others), 400
    )
    attn_part, input_raw = together(attn_part, input_raw)
    attn_blocks = send_blocks(attn_part)
    attn_part = order([attn_part, attn_blocks[0]], attn_part, 8)
    mixed = jnp.where(stays(), mixed_own, mixed_raw)
    mixed = row_pass(add_rows, "mixed", whole_rows(mixed, *mixed_others), [], [bf16])[0]
    grad_ff = add_blocks(ff_blocks)
    units = w_gate.shape[1]
    grad_gate, grad_up, grad_down = (grad_ff[:, units * i : units * (i + 1)] for i in range(3))
    input_grad = jnp.where(stays(), input_grad, input_raw).astype(f32)

    def weighed(weights, part, width):
        product = weights[:, :width].astype(f32) * part[:, :width].astype(f32)
        return jnp.sum(product, 1).reshape(2, -1)

    gain_parts = jnp.stack(
        [weighed(attn_kept, attn_part, qcols + 2 * kcols if cut else qw + 2 * kw), weighed(ff_rows, ff_part, 2 * units)]
    )
    gain_parts = jnp.where(core == 0, gain_parts, gain_parts[:, ::-1])
    gain_parts = gain_parts[:, 0] + other_core(gain_parts[:, 1]) + marks[0][0, 0]
    count = 2 * ring
    gain_grads = sum_steps(
        gain_parts,
        [
            lax.ppermute(gain_parts, ("zh", "zl"), [(i, (i + j) % count) for i in range(count)])
            for j in range(1, count)
        ],
    )
    gain_first_grad = gain_grads[0] / norm1_gain.astype(f32)
    gain_second_grad = gain_grads[1] / norm2_gain.astype(f32)
    mixed, input_grad, gain_first_grad, gain_second_grad, grad_gate, grad_up, grad_down, attn_blocks = (
        together(
            mixed,
            input_grad,
            gain_first_grad,
            gain_second_grad,
            grad_gate,
            grad_up,
            grad_down,
            attn_blocks,
        )
    )
    grad_query, grad_key, grad_value, grad_output = cut_heads(
        attn_blocks, [qcols, kcols, kcols, qcols]
    )
    return (
        mixed,
        input_grad,
        gain_first_grad,
        grad_query,
        grad_key,
        grad_value,
        grad_output,
        gain_second_grad,
        grad_gate,
        grad_up,
        grad_down,
    )


def solution(mesh):
    dp, tensor = mesh.devices.shape
    ring = tensor // 2
    regrouped = Mesh(mesh.devices.reshape(dp // 2, 2, 2, ring), ("d", "c", "zh", "zl"))
    data, parts = ("d", "c"), ("zh", "zl")
    tokens_spec = P(data + parts, None)
    weight_spec = P(data, parts)
    in_specs = (
        tokens_spec,
        P(data),
        P(data),
        weight_spec,
        weight_spec,
        weight_spec,
        weight_spec,
        P(data),
        weight_spec,
        weight_spec,
        weight_spec,
        tokens_spec,
    )
    out_specs = (
        tokens_spec,
        tokens_spec,
        P(data),
        weight_spec,
        weight_spec,
        weight_spec,
        weight_spec,
        P(data),
        weight_spec,
        weight_spec,
        weight_spec,
    )
    return jax.shard_map(
        functools.partial(per_device, ring),
        mesh=regrouped,
        in_specs=in_specs,
        out_specs=out_specs,
        check_vma=False,
    )
```

```python
import functools
import math

import jax
import jax.numpy as jnp
from jax import lax
from jax.experimental import pallas as pl
from jax.experimental.pallas import tpu as pltpu
from jax.sharding import Mesh
from jax.sharding import PartitionSpec as P

HEAD_SIZE = 96
SEQUENCE_LENGTH = 2048
LANES = 128

epsilon = 1e-05
rope_base = 100000.0
masked_score = -1e30
query_scale = math.log2(math.e) * HEAD_SIZE ** (-0.5)
rows_both = (((0,), (0,)), ((), ()))
cols_both = (((1,), (1,)), ((), ()))
plain = (((1,), (0,)), ((), ()))
f32 = jnp.float32
light = pl.CostEstimate(flops=1, bytes_accessed=1, transcendentals=0)
heavy = pl.CostEstimate(flops=8 * 10**9, bytes_accessed=1, transcendentals=0)
unread = pl.BlockSpec(memory_space=pl.ANY)
bf16 = jnp.bfloat16


def flipped(core, column, place, ring):
    return jnp.where(core == place[2], column, ring - 1 - column)


def local_block(g, place, ring):
    core = g // ring
    column = flipped(core, lax.rem(g, ring), place, ring)
    step = lax.rem(column - place[1] + ring, ring)
    return 2 * step + lax.rem(core + place[0], 2)


def global_block(l, place, ring):
    core = lax.rem(lax.rem(l, 2) + place[0], 2)
    column = lax.rem(l // 2 + place[1], ring)
    return core * ring + flipped(core, column, place, ring)


def in_hbm(*arrays):
    return [pltpu.with_memory_space_constraint(a, pltpu.HBM) for a in arrays]


def attend_kernel(ring, block, chip, place_ref, q_ref, k_ref, v_ref, start_ref, *refs):
    o_ref, lse_ref = refs[-2:]
    g = global_block(2 * chip + pl.program_id(1), place_ref, ring)
    share = q_ref.shape[1] // LANES
    start = start_ref[...]
    row = lax.broadcasted_iota(jnp.int32, (block, block), 0)
    col = lax.broadcasted_iota(jnp.int32, (block, block), 1)
    queries = [q_ref[:, h * LANES : (h + 1) * LANES] for h in range(share)]

    def step(kb, carry, diagonal):
        offset = pl.multiple_of(local_block(kb, place_ref, ring) * block, block)
        keys = k_ref[pl.ds(offset, block), :]
        values = v_ref[pl.ds(offset, block), :]
        shown = row >= start - kb * block
        if diagonal:
            shown = shown & (row <= col)
        out = []
        for h in range(share):
            largest, total, acc = carry[h]
            s = lax.dot_general(keys, queries[h], cols_both, preferred_element_type=f32)
            s = jnp.where(shown, s, masked_score)
            newest = jnp.maximum(largest, jnp.max(s, 0, keepdims=True))
            fade = jnp.exp2(largest - newest)
            p = jnp.exp2(s - newest)
            total = total * fade + jnp.sum(p, 0, keepdims=True)
            acc = acc * fade + lax.dot_general(
                values, p.astype(bf16), rows_both, preferred_element_type=f32
            )
            out.append((newest, total, acc))
        return tuple(out)

    carry = tuple(
        (
            jnp.full((1, block), masked_score, f32),
            jnp.zeros((1, block), f32),
            jnp.zeros((LANES, block), f32),
        )
        for _ in range(share)
    )
    carry = step(g, carry, True)
    carry = lax.fori_loop(0, g, lambda kb, c: step(kb, c, False), carry)
    for h in range(share):
        largest, total, acc = carry[h]
        o_ref[:, h * LANES : (h + 1) * LANES] = jnp.transpose(acc / total).astype(bf16)
        lse_ref[0, h : h + 1, :] = largest + jnp.log2(total)


def attend(chip, place, q, k, v, start, ring, first=()):
    length = q.shape[0]
    block = length // (2 * ring)
    kv = k.shape[1] // LANES
    share = q.shape[1] // k.shape[1]
    return pl.pallas_call(
        functools.partial(attend_kernel, ring, block, chip),
        grid_spec=pltpu.PrefetchScalarGridSpec(
            num_scalar_prefetch=1,
            grid=(kv, 2),
            in_specs=[
                pl.BlockSpec((block, share * LANES), lambda h, j, z: (2 * chip + j, h)),
                pl.BlockSpec((length, LANES), lambda h, j, z: (0, h)),
                pl.BlockSpec((length, LANES), lambda h, j, z: (0, h)),
                pl.BlockSpec((1, block), lambda h, j, z: (0, 2 * chip + j)),
            ]
            + [unread] * len(first),
            out_specs=[
                pl.BlockSpec((block, share * LANES), lambda h, j, z: (j, h)),
                pl.BlockSpec((1, share, block), lambda h, j, z: (h, 0, j)),
            ],
        ),
        out_shape=[
            jax.ShapeDtypeStruct((2 * block, q.shape[1]), bf16),
            jax.ShapeDtypeStruct((kv, share, 2 * block), f32),
        ],
        compiler_params=pltpu.CompilerParams(
            vmem_limit_bytes=40 * 2**20, dimension_semantics=("arbitrary", "arbitrary")
        ),
        cost_estimate=heavy if first else light,
        name="attend",
    )(place, q, k, v, start, *first)


def attend_back_kernel(
    ring,
    block,
    chip,
    final,
    place_ref,
    q_ref,
    k_ref,
    v_ref,
    o_ref,
    do_ref,
    lse_ref,
    start_ref,
    cosq_ref,
    sinq_ref,
    *refs,
):
    if final:
        cosk_ref, sink_ref = refs[:2]
    before = refs[2 * final : -5]
    dq_ref, dk_ref, dv_ref, dk_acc, dv_acc = refs[-5:]
    j = pl.program_id(1)
    g = global_block(2 * chip + j, place_ref, ring)
    share = q_ref.shape[1] // LANES

    @pl.when(j == 0)
    def _():
        if before:
            dk_acc[...] = before[0][...]
            dv_acc[...] = before[1][...]
        else:
            dk_acc[...] = jnp.zeros_like(dk_acc)
            dv_acc[...] = jnp.zeros_like(dv_acc)

    start = start_ref[...]
    row = lax.broadcasted_iota(jnp.int32, (block, block), 0)
    col = lax.broadcasted_iota(jnp.int32, (block, block), 1)
    heads = [slice(h * LANES, (h + 1) * LANES) for h in range(share)]
    queries = [q_ref[:, h] for h in heads]
    grads = [do_ref[:, h] for h in heads]
    lses = [lse_ref[0, h : h + 1, :] for h in range(share)]
    inner = [
        jnp.sum(
            jnp.transpose(do_ref[:, h].astype(f32) * o_ref[:, h].astype(f32)), 0, keepdims=True
        )
        for h in heads
    ]

    def step(kb, carry):
        offset = pl.multiple_of(local_block(kb, place_ref, ring) * block, block)
        keys = k_ref[pl.ds(offset, block), :]
        values = v_ref[pl.ds(offset, block), :]
        shown = row >= start - kb * block
        out = []
        dk = jnp.zeros((block, LANES), f32)
        dv = jnp.zeros((block, LANES), f32)
        for h in range(share):
            s = lax.dot_general(keys, queries[h], cols_both, preferred_element_type=f32)
            p = jnp.where(shown, jnp.exp2(s - lses[h]), 0.0)
            dp = lax.dot_general(values, grads[h], cols_both, preferred_element_type=f32)
            ds = (p * (dp - inner[h])).astype(bf16)
            dv += jnp.dot(p.astype(bf16), grads[h], preferred_element_type=f32)
            dk += jnp.dot(ds, queries[h], preferred_element_type=f32)
            out.append(carry[h] + lax.dot_general(keys, ds, rows_both, preferred_element_type=f32))
        dk_acc[pl.ds(offset, block), :] += dk
        dv_acc[pl.ds(offset, block), :] += dv
        return tuple(out)

    half = block // 2
    offset = pl.multiple_of(local_block(g, place_ref, ring) * block, block)
    found = [[] for _ in range(share)]
    for part in range(2):
        seen, lanes = (part + 1) * half, slice(part * half, (part + 1) * half)
        keys = k_ref[pl.ds(offset, seen), :]
        values = v_ref[pl.ds(offset, seen), :]
        shown = (row[:seen, :half] >= start[:, lanes] - g * block) & (
            row[:seen, :half] <= col[:seen, lanes]
        )
        dk = jnp.zeros((seen, LANES), f32)
        dv = jnp.zeros((seen, LANES), f32)
        for h in range(share):
            q, do = queries[h][lanes], grads[h][lanes]
            s = lax.dot_general(keys, q, cols_both, preferred_element_type=f32)
            p = jnp.where(shown, jnp.exp2(s - lses[h][:, lanes]), 0.0)
            dp = lax.dot_general(values, do, cols_both, preferred_element_type=f32)
            ds = (p * (dp - inner[h][:, lanes])).astype(bf16)
            dv += jnp.dot(p.astype(bf16), do, preferred_element_type=f32)
            dk += jnp.dot(ds, q, preferred_element_type=f32)
            found[h].append(lax.dot_general(keys, ds, rows_both, preferred_element_type=f32))
        dk_acc[pl.ds(offset, seen), :] += dk
        dv_acc[pl.ds(offset, seen), :] += dv
    carry = tuple(jnp.concatenate(found[h], 1) for h in range(share))
    carry = lax.fori_loop(0, g, step, carry)
    for h in range(share):
        u = jnp.transpose(carry[h]) * HEAD_SIZE ** (-0.5)
        turned = u * cosq_ref[...] - pltpu.roll(u, LANES // 2, 1) * sinq_ref[...]
        dq_ref[:, heads[h]] = turned.astype(bf16)

    @pl.when(j == 1)
    def _():
        def finish(i, _):
            r = pl.ds(pl.multiple_of(i * block, block), block)
            u = dk_acc[r, :]
            if final:
                u = u * math.log(2.0)
                u = u * cosk_ref[r, :] - pltpu.roll(u, LANES // 2, 1) * sink_ref[r, :]
            dk_ref[r, :] = u.astype(dk_ref.dtype)
            dv_ref[r, :] = dv_acc[r, :].astype(dv_ref.dtype)
            return 0

        lax.fori_loop(0, 2 * ring, finish, 0)


def attend_back(chip, place, q, k, v, o, do, lse, start, cos, sin, ring, before):
    length = q.shape[0]
    block = length // (2 * ring)
    kv = k.shape[1] // LANES
    share = q.shape[1] // k.shape[1]
    final = chip == ring - 1
    kind = bf16 if final else f32
    qspec = pl.BlockSpec((block, share * LANES), lambda h, j, z: (2 * chip + j, h))
    own = pl.BlockSpec((block, share * LANES), lambda h, j, z: (j, h))
    kspec = pl.BlockSpec((length, LANES), lambda h, j, z: (0, h))
    table = pl.BlockSpec((block, LANES), lambda h, j, z: (2 * chip + j, 0))
    whole = pl.BlockSpec((length, LANES), lambda h, j, z: (0, 0))
    return pl.pallas_call(
        functools.partial(attend_back_kernel, ring, block, chip, final),
        grid_spec=pltpu.PrefetchScalarGridSpec(
            num_scalar_prefetch=1,
            grid=(kv, 2),
            in_specs=[
                qspec,
                kspec,
                kspec,
                own,
                own,
                pl.BlockSpec((1, share, block), lambda h, j, z: (h, 0, j)),
                pl.BlockSpec((1, block), lambda h, j, z: (0, 2 * chip + j)),
                table,
                table,
            ]
            + [whole, whole] * final
            + [kspec] * len(before),
            out_specs=[own, kspec, kspec],
            scratch_shapes=[pltpu.VMEM((length, LANES), f32), pltpu.VMEM((length, LANES), f32)],
        ),
        out_shape=[
            jax.ShapeDtypeStruct((2 * block, q.shape[1]), bf16),
            jax.ShapeDtypeStruct(k.shape, kind),
            jax.ShapeDtypeStruct(k.shape, kind),
        ],
        compiler_params=pltpu.CompilerParams(
            vmem_limit_bytes=40 * 2**20, dimension_semantics=("arbitrary", "arbitrary")
        ),
        cost_estimate=light,
        name="attend_back",
    )(place, q, k, v, o, do, lse, start, cos, sin, *[cos, sin] * final, *before)


def pieces_spec(block, width, count):
    return [
        pl.BlockSpec((block, width), lambda i: (jnp.minimum(i, count - 1), 0)),
        pl.BlockSpec((block, width), lambda i: (jnp.maximum(i - count, 0), 0)),
    ]


def picked(count, first_ref, second_ref):
    return jnp.where(pl.program_id(0) < count, first_ref[...], second_ref[...])


def project_kernel(
    widths, count, x_ref, y_ref, gain_ref, w_ref, cos_ref, sin_ref, *refs
):
    a_ref, q_ref, k_ref, v_ref = refs[-4:]
    x = picked(count, x_ref, y_ref).astype(f32)
    root = lax.rsqrt(jnp.mean(x * x, -1, keepdims=True) + epsilon)
    a = (x * root * gain_ref[...]).astype(bf16)
    a_ref[...] = a
    cos = cos_ref[...]
    sin = sin_ref[...]
    whole = jnp.dot(a, w_ref[...], preferred_element_type=f32)
    qw, kw = widths
    for h in range((qw + kw) // LANES):
        u = whole[:, h * LANES : (h + 1) * LANES]
        turned = u * cos + pltpu.roll(u, LANES // 2, 1) * sin
        if h < qw // LANES:
            q_ref[:, h * LANES : (h + 1) * LANES] = (turned * query_scale).astype(bf16)
        else:
            j = h - qw // LANES
            k_ref[:, j * LANES : (j + 1) * LANES] = turned.astype(bf16)
    v_ref[...] = whole[:, qw + kw :].astype(bf16)


def project(pair, gain, w, cos, sin, qw, kw, step, before, first=()):
    rows, width = pair[0].shape
    length = cos.shape[0]
    block = min(256, rows)
    count = rows // block
    base = step * 2 * count
    widths = (width, qw, kw, kw)

    def row(n):
        return pl.BlockSpec((block, n), lambda i: (base + i, 0))

    def whole(shape):
        return pl.BlockSpec(shape, lambda i: (0, 0))

    return pl.pallas_call(
        functools.partial(project_kernel, (qw, kw), count),
        grid=(2 * count,),
        in_specs=pieces_spec(block, width, count)
        + [whole(gain.shape), whole((width, qw + 2 * kw)), row(LANES), row(LANES)]
        + [unread] * (len(before) + len(first)),
        out_specs=[row(n) for n in widths],
        out_shape=[jax.ShapeDtypeStruct((length, n), bf16) for n in widths],
        input_output_aliases={6 + i: i for i in range(len(before))},
        compiler_params=pltpu.CompilerParams(
            vmem_limit_bytes=40 * 2**20, dimension_semantics=("arbitrary",)
        ),
        cost_estimate=heavy if first else light,
        name="project",
    )(*in_hbm(*pair), gain, *in_hbm(w), cos, sin, *in_hbm(*before), *first)


def hidden_kernel(
    chunk, count, a_ref, b_ref, dy_ref, dz_ref, w_ref, hid_ref, dgu_ref, *refs
):
    a = picked(count, a_ref, b_ref)
    dy = picked(count, dy_ref, dz_ref)
    units = hid_ref.shape[1]
    for j in range(units // chunk):
        at = slice(j * chunk, (j + 1) * chunk)
        up = slice(units + j * chunk, units + (j + 1) * chunk)
        down = slice(2 * units + j * chunk, 2 * units + (j + 1) * chunk)
        g = jnp.dot(a, w_ref[:, at], preferred_element_type=f32)
        u = jnp.dot(a, w_ref[:, up], preferred_element_type=f32)
        dh = jnp.dot(dy, w_ref[:, down], preferred_element_type=f32)
        sig = jax.nn.sigmoid(g)
        silu = g * sig
        hid_ref[:, at] = (silu * u).astype(bf16)
        dgu_ref[:, at] = (dh * u * (sig + silu * (1.0 - sig))).astype(bf16)
        dgu_ref[:, up] = (dh * silu).astype(bf16)
    da = lax.dot_general(
        dgu_ref[...], w_ref[:, : 2 * units], cols_both, preferred_element_type=f32
    ).astype(bf16)
    mixed = lax.dot_general(
        hid_ref[...], w_ref[:, 2 * units :], cols_both, preferred_element_type=f32
    ).astype(bf16)
    mine = pl.program_id(0) < count

    @pl.when(mine)
    def _():
        refs[0][...] = da
        refs[2][...] = mixed

    @pl.when(jnp.logical_not(mine))
    def _():
        refs[1][...] = da
        refs[3][...] = mixed


def hidden_pass(a, dy, w):
    rows, width = a[0].shape
    units = w.shape[1] // 3
    block = min(256, rows)
    count = rows // block
    widths = [units, 2 * units]

    def row(n):
        return pl.BlockSpec((block, n), lambda i: (i, 0))

    return pl.pallas_call(
        functools.partial(hidden_kernel, min(256, units), count),
        grid=(2 * count,),
        in_specs=pieces_spec(block, width, count)
        + pieces_spec(block, width, count)
        + [pl.BlockSpec(w.shape, lambda i: (0, 0), pipeline_mode=pl.Buffered(1))],
        out_specs=[row(n) for n in widths] + 2 * pieces_spec(block, width, count),
        out_shape=[jax.ShapeDtypeStruct((2 * rows, n), bf16) for n in widths]
        + [jax.ShapeDtypeStruct((rows, width), bf16)] * 4,
        compiler_params=pltpu.CompilerParams(
            vmem_limit_bytes=40 * 2**20, dimension_semantics=("arbitrary",)
        ),
        cost_estimate=heavy,
        name="hidden",
    )(*a, *dy, w)


def product_kernel(dims, parts, unused, *refs):
    x = refs[0][...]
    if parts > 1:
        x = jnp.concatenate([ref[...] for ref in refs[:parts]], 1)
    p = lax.dot_general(x, refs[parts][...], dims, preferred_element_type=f32)
    out_ref = refs[-1]
    for ref in refs[parts + 1 + unused : -1]:
        p = p + ref[...].astype(f32)
    out_ref[...] = p.astype(out_ref.dtype)


def product(parts, rows, w, dims, kind=bf16, columns=None, add=None, cost=light, after=()):
    block = min(256, rows)
    columns = columns or (0, w.shape[1])
    wide = columns[1]
    out = w.shape[0] if dims == cols_both else wide
    row = pl.BlockSpec((block, out), lambda i: (i, 0))
    extra = [] if add is None else [add]
    return pl.pallas_call(
        functools.partial(product_kernel, dims, len(parts), len(after)),
        grid=(rows // block,),
        in_specs=[
            pl.BlockSpec((block, x.shape[1]), lambda i, first=first: (first // block + i, 0))
            for x, first in parts
        ]
        + [pl.BlockSpec((w.shape[0], wide), lambda i: (0, columns[0]))]
        + [unread] * len(after)
        + [row] * len(extra),
        out_specs=row,
        out_shape=jax.ShapeDtypeStruct((rows, out), kind),
        compiler_params=pltpu.CompilerParams(
            vmem_limit_bytes=40 * 2**20, dimension_semantics=("arbitrary",)
        ),
        cost_estimate=cost,
        name="product",
    )(*[x for x, _ in parts], *in_hbm(w), *after, *extra)


def without_gaps(w):
    half = HEAD_SIZE // 2
    parts = [w[:, at : at + half] for at in range(0, w.shape[1], LANES // 2)]
    return jnp.concatenate(parts, 1)


def wgrad_kernel(counts, cut, *refs):
    out_ref = refs[-1]
    j = pl.program_id(0)
    first = 0
    for pieces, parts, blocks in counts:
        lefts, refs = refs[:pieces], refs[pieces:]
        rights, refs = refs[: pieces * parts], refs[pieces * parts :]

        @pl.when((j >= first) & (j < first + blocks))
        def _():
            total = None
            for i, a in enumerate(lefts):
                b = [ref[...] for ref in rights[parts * i : parts * (i + 1)]]
                b = b[0] if parts == 1 else jnp.concatenate(b, 1)
                p = lax.dot_general(a[...], b, rows_both, preferred_element_type=f32)
                total = p if total is None else total + p
            total = total.astype(bf16)
            out_ref[...] = without_gaps(total) if cut else total

        first += blocks


def wgrad(groups, rows, block, first=(), cut=False):
    width = groups[0][0][0].shape[1]
    counts, specs, args = [], [], []
    column = 0
    for group in groups:
        parts = len(group[0][2])
        blocks = sum(b.shape[1] for b in group[0][2]) // block
        counts.append((len(group), parts, blocks))
        for a, at, _, _ in group:
            specs.append(
                pl.BlockSpec(
                    (rows, width), lambda j, at=at: (at, 0), pipeline_mode=pl.Buffered(1)
                )
            )
            args.append(a)
        for _, _, sides, at in group:

            def spot(j, at=at, column=column, blocks=blocks):
                return (at, jnp.clip(j - column, 0, blocks - 1))

            for b in sides:
                specs.append(pl.BlockSpec((rows, b.shape[1] if parts > 1 else block), spot))
                args.append(b)
        column += blocks
    wide = block * 3 // 4 if cut else block
    return pl.pallas_call(
        functools.partial(wgrad_kernel, counts, cut),
        grid=(column,),
        in_specs=specs + [unread] * len(first),
        out_specs=pl.BlockSpec((width, wide), lambda j: (0, j)),
        out_shape=pltpu.HBM((width, column * wide), bf16),
        compiler_params=pltpu.CompilerParams(
            vmem_limit_bytes=40 * 2**20, dimension_semantics=("arbitrary",)
        ),
        cost_estimate=heavy if first else light,
        name="wgrad",
    )(*in_hbm(*args), *first)


def row_pass(body, name, inputs, whole, kinds, after=()):
    width = inputs[0][0].shape[1]
    rows = min(a.shape[0] - first for a, first in inputs)
    block = min(512, rows) if body is add_rows else min(256, rows)

    def kernel(*refs):
        count = len(inputs) + len(whole)
        values = [ref[...].astype(f32) for ref in refs[:count]]
        for ref, value in zip(refs[count + len(after) :], body(*values)):
            ref[...] = value.astype(ref.dtype)

    return pl.pallas_call(
        kernel,
        grid=(rows // block,),
        in_specs=[
            pl.BlockSpec((block, width), lambda i, first=first: (first // block + i, 0))
            for _, first in inputs
        ]
        + [pl.BlockSpec(a.shape, lambda i: (0, 0)) for a in whole]
        + [unread] * len(after),
        out_specs=[pl.BlockSpec((block, width), lambda i: (i, 0)) for _ in kinds],
        out_shape=[jax.ShapeDtypeStruct((rows, width), kind) for kind in kinds],
        compiler_params=pltpu.CompilerParams(
            vmem_limit_bytes=40 * 2**20, dimension_semantics=("arbitrary",)
        ),
        cost_estimate=light,
        name=name,
    )(*[a for a, _ in inputs], *whole, *after)


def inverse_root(x):
    return lax.rsqrt(jnp.mean(x * x, -1, keepdims=True) + epsilon)


def add_rows(*items):
    return (sum_steps(items[0], items[1:]),)


def norm_forward(stream, *rest):
    *terms, gain = rest
    middle = sum_steps(stream, terms)
    return middle, middle * inverse_root(middle) * gain


def norm_back(residual, values, *rest):
    *terms, gain = rest
    root = inverse_root(values)
    scaled = sum_steps(terms[0], terms[1:]) * gain
    mean = jnp.mean(scaled * values, -1, keepdims=True)
    return (residual + root * scaled - values * root**3 * mean,)


def pad_kernel(counts, *refs):
    out_ref = refs[-1]
    gains = refs[-2][...]
    half = HEAD_SIZE // 2
    rows = out_ref.shape[0]
    at = 0
    for ref, heads in zip(refs[:-2], counts):
        w = ref[...]
        for h in range(heads):
            gap = jnp.zeros((rows, LANES // 2 - half), bf16)
            first = w[:, h * HEAD_SIZE : h * HEAD_SIZE + half]
            second = w[:, h * HEAD_SIZE + half : (h + 1) * HEAD_SIZE]
            free = gap if at else jnp.concatenate([gains, gap[:, 2:]], 1)
            out_ref[:, at : at + LANES] = jnp.concatenate([first, free, second, gap], 1)
            at += LANES


def pad_heads(weights, gains):
    counts = [w.shape[1] // HEAD_SIZE for w in weights]
    return pl.pallas_call(
        functools.partial(pad_kernel, counts),
        out_shape=jax.ShapeDtypeStruct((weights[0].shape[0], sum(counts) * LANES), bf16),
        cost_estimate=light,
        name="pad",
    )(*weights, gains)


def cut_kernel(widths, padded, keep_ref, own_ref, crossed_ref, slanted_ref, *out_refs):
    kept = keep_ref[0] == 1
    at = 0
    for ref, width in zip(out_refs, widths):
        wide = width // HEAD_SIZE * LANES if padded else width
        lanes = slice(at, at + wide)
        w = jnp.where(kept, own_ref[:, lanes], crossed_ref[:, lanes]).astype(f32)
        w = w + slanted_ref[:, lanes].astype(f32)
        ref[...] = without_gaps(w) if padded else w
        at += wide


def cut_heads(blocks, widths):
    rows, columns = blocks[0].shape
    keep = stays().astype(jnp.int32).reshape(1)
    return pl.pallas_call(
        functools.partial(cut_kernel, widths, columns != sum(widths)),
        in_specs=[pl.BlockSpec(memory_space=pltpu.SMEM)]
        + [pl.BlockSpec(memory_space=pltpu.VMEM)] * 3,
        out_shape=[jax.ShapeDtypeStruct((rows, width), f32) for width in widths],
        cost_estimate=light,
        name="cut",
    )(keep, *blocks)


def cut_rows_kernel(in_ref, out_ref):
    out_ref[...] = without_gaps(in_ref[...])


def cut_rows(w):
    return pl.pallas_call(
        cut_rows_kernel,
        out_shape=jax.ShapeDtypeStruct((w.shape[0], w.shape[1] * 3 // 4), w.dtype),
        cost_estimate=light,
        name="cut_rows",
    )(w)


swap_two = [(0, 1), (1, 0)]
cross_pairs = [(1, 2), (2, 1)]
slant_pairs = [(2 * c + zh, 2 * zh + (1 - c)) for c in range(2) for zh in range(2)]
slant_back = [(b, a) for a, b in slant_pairs]


def stays():
    return lax.axis_index("c") == lax.axis_index("zh")


def cross(a):
    return lax.ppermute(a, ("c", "zh"), cross_pairs)


def other_core(a):
    return lax.ppermute(a, "c", swap_two)


def from_neighbour(a, k, ring):
    return lax.ppermute(a, "zl", [(i, (i - k) % ring) for i in range(ring)])


def both_cores(a):
    return jnp.concatenate([a, other_core(a)], 0)


def spread_pair(w):
    return w, cross(w), lax.ppermute(w, ("c", "zh"), slant_pairs)


def arrange(own, crossed, slanted):
    first = lax.axis_index("zh") == 0
    straight = jnp.where(stays(), own, crossed)
    return jnp.concatenate(
        [jnp.where(first, straight, slanted), jnp.where(first, slanted, straight)], 0
    )


def gather_rows(w):
    return lax.all_gather(w, "d", axis=0, tiled=True)


def send_blocks(part):
    rows = part.shape[0] // 2
    first = lax.axis_index("zh") == 0
    upper, lower = part[:rows], part[rows:]
    straight = jnp.where(first, upper, lower)
    slanted = lax.ppermute(jnp.where(first, lower, upper), ("c", "zh"), slant_back)
    return straight, cross(straight), slanted


def add_blocks(blocks):
    straight, crossed, slanted = blocks
    return jnp.where(stays(), straight, crossed).astype(f32) + slanted.astype(f32)


def sum_rows(grad):
    return lax.psum_scatter(grad, "d", scatter_dimension=0, tiled=True)


def together(*items):
    return lax.optimization_barrier(items)


def mark_kernel(*refs):
    refs[-1][...] = jnp.zeros_like(refs[-1])


def mark(arrays, before, long):
    whole = pl.BlockSpec(before.shape, lambda: (0, 0))
    cost = pl.CostEstimate(flops=1 + long * 10**9, bytes_accessed=1, transcendentals=0)
    return pl.pallas_call(
        mark_kernel,
        in_specs=[pl.BlockSpec(memory_space=pl.ANY)] * len(arrays) + [whole],
        out_specs=whole,
        out_shape=jax.ShapeDtypeStruct(before.shape, before.dtype),
        cost_estimate=cost,
        name="mark",
    )(*arrays, before)


def dot(a, b):
    return jnp.dot(a, b, preferred_element_type=f32)


def dot_cols(a, b):
    return lax.dot_general(a, b, cols_both, preferred_element_type=f32)


def dot_rows(a, b):
    return lax.dot_general(a, b, rows_both, preferred_element_type=f32)


def sum_steps(first, second):
    out = first
    for item in second:
        out = out + item
    return out


def per_device(
    ring,
    tokens,
    positions,
    norm1_gain,
    w_query,
    key_weight,
    value_weight,
    w_out,
    norm2_gain,
    w_gate,
    w_up,
    w_down,
    cotangent,
):
    steps = range(ring)
    core = lax.axis_index("c")
    column = lax.axis_index("zl")
    place = jnp.stack([core, column, lax.axis_index("zh")]).astype(jnp.int32)
    rows = tokens.shape[0]
    length = 2 * ring * rows
    marks = [jnp.zeros((8, LANES), f32)]

    def order(first, then, long=0):
        marks[0], then = together(mark(first, marks[0], long), then)
        return then

    def swap_chips(own):
        return [from_neighbour(own, k, ring) for k in steps[1:]]

    def join_cores(partial, kind=bf16):
        theirs = other_core(partial(rows, bf16, None))
        return partial(0, kind, theirs)

    def join(mine, theirs):
        return row_pass(add_rows, "join", [(mine, 0), (theirs, 0)], [], [bf16])[0]

    def split_cores(partial):
        return [partial(0, bf16, None), other_core(partial(rows, bf16, None))]

    def send_chips(joined):
        return [
            lax.ppermute(p.astype(bf16), "zl", [(i, (i + k) % ring) for i in steps])
            for k, p in zip(steps[1:], joined)
        ]

    def pairs_of(kept, k):
        out = []
        for c in range(2):
            for zh in range(2):
                if (c == zh) == kept:
                    base = (2 * c + zh) * ring
                    out += [(base + i, base + (i - k) % ring) for i in steps]
        return out

    def cross_tokens(a):
        pairs = []
        for c, zh in ((0, 1), (1, 0)):
            pairs += [
                ((2 * c + zh) * ring + i, (2 * zh + c) * ring + ring - 1 - i) for i in steps
            ]
        return lax.ppermute(a, ("c", "zh", "zl"), pairs)

    def home_pairs(k):
        pairs = []
        for c in range(2):
            for zh in range(2):
                for i in steps:
                    at = (i + k) % ring
                    home = (2 * c + zh) * ring + at
                    if c != zh:
                        home = (2 * zh + c) * ring + ring - 1 - at
                    pairs.append(((2 * c + zh) * ring + i, home))
        return pairs

    def early_neighbours(original):
        return [
            lax.ppermute(original, ("c", "zh", "zl"), pairs_of(True, k)) for k in steps if k
        ]

    def first_moves(original):
        pairs = [(a, b) for a, b in home_pairs(0) if a != b] + pairs_of(True, 1)
        moved = lax.ppermute(original, ("c", "zh", "zl"), pairs)
        rest = [
            lax.ppermute(original, ("c", "zh", "zl"), pairs_of(True, k)) for k in steps[2:]
        ]
        return moved, [moved] + rest

    def late_neighbours(moved):
        return [lax.ppermute(moved, ("c", "zh", "zl"), pairs_of(False, k)) for k in steps[1:]]

    def choose(early, late):
        return [jnp.where(stays(), e, l) for e, l in zip(early, late)]

    qcols, kcols = w_query.shape[1], key_weight.shape[1]
    qw = qcols // HEAD_SIZE * LANES
    kw = kcols // HEAD_SIZE * LANES
    half = HEAD_SIZE // 2
    attn_shard = pad_heads(
        [w_query, key_weight, value_weight, w_out], jnp.stack([norm1_gain, norm2_gain], 1)
    )
    other_positions = other_core(positions)
    attn_pair = spread_pair(attn_shard)
    cot_early = early_neighbours(cotangent)
    attn_pair, cot_early, tokens, other_positions = together(
        attn_pair, cot_early, tokens, other_positions
    )
    places = jnp.where(stays(), positions, other_positions).reshape(2 * ring, rows)
    attn_rows = arrange(*attn_pair)
    attn_full = gather_rows(attn_rows)
    cut = qw * 3 // 4 % LANES == 0
    stream_raw, tokens_early = first_moves(tokens)

    blocks = [global_block(l, place, ring) for l in range(2 * ring)]
    ordered = [lax.dynamic_index_in_dim(places, g, 0, keepdims=False) for g in blocks]
    start = jnp.concatenate(
        [g * rows + jnp.arange(rows, dtype=jnp.int32) - o for g, o in zip(blocks, ordered)]
    )[None, :]
    spots = jnp.concatenate(ordered).astype(f32)
    inverse = rope_base ** (-(2.0 / HEAD_SIZE) * jnp.arange(half, dtype=f32))
    angles = spots[:, None] * inverse[None, :]
    gap = jnp.zeros((length, LANES // 2 - half), f32)
    cos_half, sin_half = jnp.cos(angles), jnp.sin(angles)
    cos = jnp.concatenate([cos_half, gap, cos_half, gap], 1)
    sin = jnp.concatenate([-sin_half, gap, sin_half, gap], 1)

    ff_cols = jnp.concatenate([w_gate, w_up, w_down], 1)
    cos, sin, start, stream_raw, tokens_early, ff_cols, attn_rows = together(
        cos, sin, start, stream_raw, tokens_early, ff_cols, attn_rows
    )
    attn_kept = cut_rows(attn_rows) if cut else attn_rows
    stream_own = jnp.where(stays(), tokens, stream_raw)
    tokens_late = late_neighbours(stream_raw)
    ff_pair = spread_pair(ff_cols)

    out_columns = ((qw + 2 * kw) // qw, qw)
    qkv_columns = (0, qw + 2 * kw)
    gain_first = attn_full[:, half].astype(f32)[None, :]
    gain_second = attn_full[:, half + 1].astype(f32)[None, :]

    projected = project(
        (stream_own, other_core(stream_own)), gain_first, attn_full, cos, sin, qw, kw, 0, ()
    )
    tokens_late, ff_pair, projected, cot_sent, attn_kept = together(
        tokens_late, ff_pair, projected, cotangent, attn_kept
    )
    others = [(x, other_core(x)) for x in choose(tokens_early, tokens_late)]
    ff_rows = arrange(*ff_pair)
    ff_full = gather_rows(ff_rows)
    cot_raw = cross_tokens(cot_sent)
    for k, pair in enumerate(others, 1):
        projected = project(
            pair, gain_first, attn_full, cos, sin, qw, kw, k, projected, (ff_rows,)
        )
    normed_first, q, k, v = projected

    def out_product(o):
        return lambda first, kind, add: product(
            [(o, first)], rows, attn_full, cols_both, kind, out_columns, add
        )

    def whole_rows(*arrays):
        return [(a, 0) for a in arrays]

    attended = [attend(i, place, q, k, v, start, ring) for i in steps[1:]]
    attended, cot_raw = together(attended, cot_raw)
    joined = [join_cores(out_product(o)) for o, _ in attended]
    sent = send_chips(joined)
    cot_late = late_neighbours(cot_raw)
    q, k, v = order(joined, (q, k, v), 8)
    attended.insert(0, attend(0, place, q, k, v, start, ring))
    out_own = split_cores(out_product(attended[0][0]))
    sent, out_own[0], cot_late = together(sent, out_own[0], cot_late)
    middle, normed_second = row_pass(
        norm_forward,
        "norm_forward",
        whole_rows(stream_own, *out_own, *sent),
        [gain_second],
        [bf16, bf16],
    )
    normed_second, cot_raw = together(normed_second, cot_raw)
    cot_own = jnp.where(stays(), cotangent, cot_raw)
    ff_others = swap_chips(normed_second)
    ff_in = [(normed_second, other_core(normed_second))]
    out_grads = [(cot_own, other_core(cot_own))]
    ff_in, out_grads = order([normed_second], (ff_in, out_grads), 8)
    hidden = [hidden_pass(ff_in[0], out_grads[0], ff_full)]
    hidden, ff_others = together(hidden, ff_others)

    second_own = [hidden[0][2], other_core(hidden[0][3])]
    mixed_own = [hidden[0][4], other_core(hidden[0][5])]
    mixed_own = row_pass(add_rows, "mixed", whole_rows(middle, *mixed_own), [], [bf16])[0]
    mixed_raw = cross_tokens(mixed_own)
    for a, dy in zip(ff_others, choose(cot_early, cot_late)):
        a, dy = (a, other_core(a)), (dy, other_core(dy))
        a, dy, second_own, mixed_own = together(a, dy, second_own, mixed_own)
        ff_in.append(a)
        out_grads.append(dy)
        hidden.append(hidden_pass(a, dy, ff_full))

    def pieces(pairs, hidden, i):
        return [(a, 0, (h[i],), j) for pair, h in zip(pairs, hidden) for j, a in enumerate(pair)]

    hidden, mixed_raw = together(hidden, mixed_raw)
    joined = [join(h[2], other_core(h[3])) for h in hidden[1:]]
    sent = send_chips(joined)
    mixed_halves = [(h[4], other_core(h[5])) for h in hidden[1:]]
    mixed_joined = [join(*pair) for pair in mixed_halves]
    ff_wgrad = wgrad(
        [pieces(ff_in, hidden, 1), pieces(out_grads, hidden, 0)],
        rows,
        min(512, w_down.shape[1]),
        joined,
    )
    sent, mixed_joined, ff_wgrad = together(sent, mixed_joined, ff_wgrad)
    ff_part = sum_rows(ff_wgrad)
    db = row_pass(
        norm_back,
        "norm_back",
        whole_rows(cot_own, middle, *second_own, *sent),
        [gain_second],
        [bf16],
    )[0]
    branch_others = swap_chips(db)
    branch = [(db, other_core(db))]

    def heads_grad(pair):
        return jnp.concatenate(
            [
                product([(b, 0)], rows, attn_full, plain, columns=out_columns, cost=cost)
                for b, cost in zip(pair, (heavy, light))
            ],
            0,
        )

    def queries_back(i, do, before):
        o, lse = attended[i]
        return attend_back(i, place, q, k, v, o, do, lse, start, cos, sin, ring, before)

    dq, *dkv = queries_back(0, heads_grad(branch[0]), ())
    dqs = [dq]
    branch_others, mixed_joined, dqs, dkv = together(branch_others, mixed_joined, dqs, dkv)
    mixed_others = [
        lax.ppermute(p, ("c", "zh", "zl"), home_pairs(k)) for k, p in zip(steps[1:], mixed_joined)
    ]
    branch += [(b, other_core(b)) for b in branch_others]
    for i in steps[1:]:
        dq, *dkv = queries_back(i, heads_grad(branch[i]), tuple(dkv))
        dqs.append(dq)
    mixed_others, dqs, dkv = together(mixed_others, dqs, dkv)
    def first_product(i, after=()):
        base = 2 * rows * i
        return lambda first, kind, add: product(
            [(dqs[i], first)] + [(d, base + first) for d in dkv],
            rows,
            attn_full,
            cols_both,
            kind,
            qkv_columns,
            add,
            after=after,
        )

    joined = [join_cores(first_product(i)) for i in steps[1:]]
    sent = send_chips(joined)
    ff_blocks = send_blocks(ff_part)
    first_own = split_cores(first_product(0, joined))
    attn_wgrad = wgrad(
        [
            [(normed_first, 2 * i + j, (dqs[i],), j) for i in steps for j in range(2)],
            [(normed_first, i, tuple(dkv), i) for i in range(2 * ring)],
            [(branch[i][j], 0, (attended[i][0],), j) for i in steps for j in range(2)],
        ],
        rows,
        qw,
        (*joined, ff_blocks[0]),
        cut,
    )
    attn_part = sum_rows(attn_wgrad)
    sent, first_own[0], wgrad_there = together(sent, first_own[0], attn_wgrad)

    input_grad = row_pass(
        norm_back,
        "norm_back",
        whole_rows(db, stream_own, *first_own, *sent),
        [gain_first],
        [bf16],
        [wgrad_there],
    )[0]
    input_raw = cross_tokens(input_grad)
    attn_part, ff_blocks, mixed_others = order(
        [input_grad, *ff_blocks[1:]], (attn_part, ff_blocks, mixed_others), 400
    )
    attn_part, input_raw = together(attn_part, input_raw)
    attn_blocks = send_blocks(attn_part)
    attn_part = order([attn_part, attn_blocks[0]], attn_part, 8)
    mixed = jnp.where(stays(), mixed_own, mixed_raw)
    mixed = row_pass(add_rows, "mixed", whole_rows(mixed, *mixed_others), [], [bf16])[0]
    grad_ff = add_blocks(ff_blocks)
    units = w_gate.shape[1]
    grad_gate, grad_up, grad_down = (grad_ff[:, units * i : units * (i + 1)] for i in range(3))
    input_grad = jnp.where(stays(), input_grad, input_raw).astype(f32)

    def weighed(weights, part, width):
        product = weights[:, :width].astype(f32) * part[:, :width].astype(f32)
        return jnp.sum(product, 1).reshape(2, -1)

    gain_parts = jnp.stack(
        [weighed(attn_kept, attn_part, qcols + 2 * kcols if cut else qw + 2 * kw), weighed(ff_rows, ff_part, 2 * units)]
    )
    gain_parts = jnp.where(core == 0, gain_parts, gain_parts[:, ::-1])
    gain_parts = gain_parts[:, 0] + other_core(gain_parts[:, 1]) + marks[0][0, 0]
    count = 2 * ring
    gain_grads = sum_steps(
        gain_parts,
        [
            lax.ppermute(gain_parts, ("zh", "zl"), [(i, (i + j) % count) for i in range(count)])
            for j in range(1, count)
        ],
    )
    gain_first_grad = gain_grads[0] / norm1_gain.astype(f32)
    gain_second_grad = gain_grads[1] / norm2_gain.astype(f32)
    mixed, input_grad, gain_first_grad, gain_second_grad, grad_gate, grad_up, grad_down, attn_blocks = (
        together(
            mixed,
            input_grad,
            gain_first_grad,
            gain_second_grad,
            grad_gate,
            grad_up,
            grad_down,
            attn_blocks,
        )
    )
    grad_query, grad_key, grad_value, grad_output = cut_heads(
        attn_blocks, [qcols, kcols, kcols, qcols]
    )
    return (
        mixed,
        input_grad,
        gain_first_grad,
        grad_query,
        grad_key,
        grad_value,
        grad_output,
        gain_second_grad,
        grad_gate,
        grad_up,
        grad_down,
    )


def solution(mesh):
    dp, tensor = mesh.devices.shape
    ring = tensor // 2
    regrouped = Mesh(mesh.devices.reshape(dp // 2, 2, 2, ring), ("d", "c", "zh", "zl"))
    data, parts = ("d", "c"), ("zh", "zl")
    tokens_spec = P(data + parts, None)
    weight_spec = P(data, parts)
    in_specs = (
        tokens_spec,
        P(data),
        P(data),
        weight_spec,
        weight_spec,
        weight_spec,
        weight_spec,
        P(data),
        weight_spec,
        weight_spec,
        weight_spec,
        tokens_spec,
    )
    out_specs = (
        tokens_spec,
        tokens_spec,
        P(data),
        weight_spec,
        weight_spec,
        weight_spec,
        weight_spec,
        P(data),
        weight_spec,
        weight_spec,
        weight_spec,
    )
    return jax.shard_map(
        functools.partial(per_device, ring),
        mesh=regrouped,
        in_specs=in_specs,
        out_specs=out_specs,
        check_vma=False,
    )
```
